32 devices in a mesh: seq: 2 (over y), dp: 16 (over z, x, core).
Axes of the slice: x: 2, y: 2, z: 4, core: 2. Of those that a mesh axis runs over, the one named last changes fastest.
Arguments:
- tokens: bfloat16 [16, 2048, 512], P('dp', 'seq'), may hold values from -6 to 6
- word_ids: int32 [16, 2048], P('dp'), may hold values from 0 to 408, as said below
- cotangent: bfloat16 [16, 2048, 512], P('dp', 'seq'), may hold values from -6 to 6
- conv_kernels: bfloat16 [9, 512], replicated, may hold values from -2 to 2
- conv_proj: bfloat16 [512, 512], replicated, may hold values from -0.25 to 0.25
- gain_attn: bfloat16 [512], replicated, may hold values from 0.5 to 1.5
- w_qkv: bfloat16 [512, 1536], replicated, may hold values from -0.25 to 0.25
- rel_bias: bfloat16 [32, 8], replicated, may hold values from -4 to 4
- out_proj: bfloat16 [512, 512], replicated, may hold values from -2 to 2
- gain_ffn: bfloat16 [512], replicated, may hold values from 0.5 to 1.5
- w_gate_up: bfloat16 [512, 4096], replicated, may hold values from -0.25 to 0.25
- w_down: bfloat16 [2048, 512], replicated, may hold values from -0.125 to 0.125
Outputs:
- result: bfloat16 [16, 2048, 512], P('dp', 'seq')
- grad_tokens: float32 [16, 2048, 512], P('dp', 'seq')
- grad_conv_kernels: float32 [9, 512], replicated
- grad_conv_proj: float32 [512, 512], replicated
- grad_gain_attn: float32 [512], replicated
- grad_w_qkv: float32 [512, 1536], replicated
- grad_rel_bias: float32 [32, 8], replicated
- grad_out_proj: float32 [512, 512], replicated
- grad_gain_ffn: float32 [512], replicated
- grad_w_gate_up: float32 [512, 4096], replicated
- grad_w_down: float32 [2048, 512], replicated
The draws below stay inside these ranges and needn't reach their ends.
Inputs may be any that keep to these rules, and one draw needn't show every extreme that they name: `word_ids`: in each sequence the ids start at 0 and rise by 0 or 1 from one byte to the next; each sequence holds exactly one fifth of 2048 words, rounded down.
All inputs are finite; a program needn't handle non-finite values.
Results may differ from the reference program's by a relative error of at most 0.015.
Values may be sent and summed in bfloat16 or wider, within the bound.
No kernel may reach another device: no remote copies, remote signals or barrier semaphores. Data moves between devices by JAX's collectives and lax.ppermute only.
A program may use at most 384 MiB of HBM per device.

```python
import jax
import jax.numpy as jnp
from jax import lax

D = 512
HEADS = 8
FF = 2048
NB = 32
LEN = 2048
SEQS = 16


def draw_word_ids(key, part):
    key = jax.random.fold_in(key, 11)
    row_keys = jax.random.split(key, SEQS)
    orders = jax.vmap(lambda row_key: jax.random.permutation(row_key, LEN - 1) + 1)(row_keys)
    chosen = orders[:, :LEN // 5 - 1]
    starts = jnp.zeros((SEQS, LEN), jnp.int32)
    starts = starts.at[jnp.arange(SEQS)[:, None], chosen].set(1)
    starts = starts.at[:, 0].set(1)
    return jnp.cumsum(starts, axis=1).astype(jnp.int32) - 1


def steps_of(key, shape, pieces, low, high):
    level = 1.0
    for position, parts in pieces:
        heights = jax.random.uniform(jax.random.fold_in(jax.random.fold_in(key, 6), position), (parts,), jnp.float32, low / len(pieces), high / len(pieces))
        level = level * jnp.repeat(jnp.exp(heights), shape[position] // parts).reshape((-1,) + (1,) * (len(shape) - 1 - position))
    return level


def scatter_about(stream_key, dims, width, bound, cuts=(), held_as=jnp.bfloat16):
    entries = jax.random.normal(stream_key, dims, jnp.float32) * width
    if len(cuts) > 0:
        entries = steps_of(stream_key, dims, cuts, -0.22, 0.18) * entries
    return jnp.clip(entries, min=-bound, max=bound).astype(held_as)


def setup_inputs(seed: int = 0) -> dict:
    key_list = jax.random.split(jax.random.key(seed), 13)
    tokens = scatter_about(key_list[0], (SEQS, LEN, D), 1.0, 6.0, ((0, 16), (1, 2)))
    word_ids = draw_word_ids(jax.random.fold_in(key_list[12], 71), 0)
    cotangent = scatter_about(key_list[2], (SEQS, LEN, D), 1.0, 6.0, ((0, 16), (1, 2)))
    conv_kernels = scatter_about(key_list[3], (9, D), 0.35, 2.0)
    conv_proj = scatter_about(key_list[4], (D, D), D ** -0.5, 0.25)
    gain_attn = jnp.clip(1.0 + 0.1 * jax.random.normal(key_list[5], (D,), jnp.float32), 0.5, 1.5).astype(jnp.bfloat16)
    w_qkv = scatter_about(key_list[6], (D, 3 * D), D ** -0.5, 0.25)
    rel_bias = scatter_about(key_list[7], (NB, HEADS), 1.0, 4.0)
    out_proj = scatter_about(key_list[8], (D, D), (D // 64) ** -0.5, 2.0)
    gain_ffn = jnp.clip(1.0 + 0.1 * jax.random.normal(key_list[9], (D,), jnp.float32), 0.5, 1.5).astype(jnp.bfloat16)
    w_gate_up = scatter_about(key_list[10], (D, 2 * FF), D ** -0.5, 0.25)
    w_down = scatter_about(key_list[11], (FF, D), FF ** -0.5, 0.125)
    return dict(tokens=tokens, word_ids=word_ids, cotangent=cotangent, conv_kernels=conv_kernels, conv_proj=conv_proj, gain_attn=gain_attn, w_qkv=w_qkv, rel_bias=rel_bias, out_proj=out_proj, gain_ffn=gain_ffn, w_gate_up=w_gate_up, w_down=w_down)


@jax.custom_vjp
def low(v):
    return lax.optimization_barrier(v.astype(jnp.bfloat16)).astype(jnp.float32)

@jax.custom_vjp
def low_back(v):
    return v

def low_keep(v):
    return (low(v), None)

def low_pass(kept, grad):
    return (grad,)

def back_keep(v):
    return (v, None)

def back_low(kept, grad):
    return (low(grad),)
low.defvjp(low_keep, low_pass)
low_back.defvjp(back_keep, back_low)
bucket_edges = (1, 2, 3, 4, 5, 6, 7, 8, 11, 16, 22, 32, 45, 64, 91)

def bucketize(offsets):
    magnitude = jnp.abs(offsets)
    bucketed = jnp.where(offsets > 0, 16, 0).astype(jnp.int32)
    for boundary in bucket_edges:
        bucketed = bucketed + (magnitude >= boundary).astype(jnp.int32)
    return bucketed

def matmul(left, right):
    return jnp.dot(left, right, precision=lax.Precision.HIGHEST, preferred_element_type=jnp.float32)

def effective_taps(kernels):
    return jnp.stack([kernels[0] + kernels[2] + kernels[5], kernels[1] + kernels[3] + kernels[6], kernels[4] + kernels[7], kernels[8]])

def rms_norm(values_in, gain_vec):
    return values_in * lax.rsqrt(lax.optimization_barrier(jnp.mean(values_in * values_in, axis=-1, keepdims=True)) + 1e-06) * gain_vec

def conv_mix(inputs, word_ids, kernels):
    taps = effective_taps(kernels)
    row_count = inputs.shape[0]
    padded = jnp.pad(inputs, ((3, 0), (0, 0)))
    padded_ids = jnp.concatenate([jnp.full((3,), -1, jnp.int32), word_ids])
    summed = jnp.zeros_like(inputs)
    for step_back in range(4):
        same_word = (padded_ids[3 - step_back:3 - step_back + row_count] == word_ids).astype(inputs.dtype)
        summed = summed + taps[step_back] * padded[3 - step_back:3 - step_back + row_count] * same_word[:, None]
    return summed

def layer(params, inputs, word_ids, buckets):
    kernels, conv_proj, gain_attn, w_qkv, rel_bias, out_proj, gain_ffn, w_gate_up, w_down = params
    row_count, model_width = inputs.shape
    head_count = rel_bias.shape[1]
    head_dim = model_width // head_count
    hidden_units = w_down.shape[0]
    mixed = conv_mix(inputs, word_ids, kernels)
    branch = inputs + low_back(matmul(low(mixed), conv_proj))
    projected = low(low_back(matmul(low(rms_norm(branch, gain_attn)), w_qkv)))
    split_up = projected.reshape(row_count, 3, head_count, head_dim).transpose(1, 2, 0, 3)

    def attend(head_args):
        query_h, key_h, value_h, column = head_args
        scores = low_back(matmul(query_h, key_h.T) * 0.125 + column[buckets])
        weights = jax.nn.softmax(scores, axis=-1)
        return matmul(low(weights), value_h)
    head_out = lax.map(jax.checkpoint(attend), (split_up[0], split_up[1], split_up[2], rel_bias.T))
    merged = head_out.transpose(1, 0, 2).reshape(row_count, model_width)
    after_attn = branch + low_back(matmul(low(low_back(merged)), out_proj))
    gate_up = low_back(matmul(low(rms_norm(after_attn, gain_ffn)), w_gate_up))
    hidden = low(jax.nn.gelu(gate_up[:, :hidden_units], approximate=True) * gate_up[:, hidden_units:])
    return after_attn + matmul(hidden, w_down)

def reference(tokens, word_ids, cotangent, conv_kernels, conv_proj, gain_attn, w_qkv, rel_bias, out_proj, gain_ffn, w_gate_up, w_down):
    params = tuple((weight.astype(jnp.float32) for weight in (conv_kernels, conv_proj, gain_attn, w_qkv, rel_bias, out_proj, gain_ffn, w_gate_up, w_down)))

    def one_sequence(running, scan_item):
        seq_tokens, seq_ids, seq_grad = scan_item
        buckets = bucketize(seq_ids[None, :] - seq_ids[:, None])

        def forward(weights_in, inputs):
            return layer(weights_in, inputs, seq_ids, buckets)
        outputs, pull_back = jax.vjp(forward, params, seq_tokens.astype(jnp.float32))
        weight_grads, input_grad = pull_back(seq_grad.astype(jnp.float32))
        running = jax.tree.map(jnp.add, running, weight_grads)
        return (running, (outputs.astype(jnp.bfloat16), input_grad))
    initial = jax.tree.map(jnp.zeros_like, params)
    sums, (results, input_grads) = lax.scan(one_sequence, initial, (tokens, word_ids, cotangent))
    return (results, input_grads, sums[0], sums[1], sums[2], sums[3], sums[4], sums[5], sums[6], sums[7], sums[8])
```

```python
import functools

import jax
import jax.numpy as jnp
from jax import lax
from jax.experimental import pallas as pl
from jax.experimental.pallas import tpu as pltpu
from jax.sharding import PartitionSpec as P

LOW = jnp.bfloat16
F32 = jnp.float32
EDGES = (1, 2, 3, 4, 5, 6, 7, 8, 11, 16, 22, 32, 45, 64, 91)
KEY_WORDS = 128
QUERY_WORDS = 256
FOLD = 512
VMEM_BYTES = 60 * 2**20


def bucketize(offsets):
    magnitude = jnp.abs(offsets)
    bucketed = jnp.where(offsets > 0, 16, 0).astype(jnp.int32)
    for edge in EDGES:
        bucketed = bucketed + (magnitude >= edge).astype(jnp.int32)
    return bucketed


def dot(a, b):
    return jnp.dot(a, b, preferred_element_type=F32)


def dot_nt(a, b):
    return lax.dot_general(a, b, (((1,), (1,)), ((), ())), preferred_element_type=F32)


def iota(shape, dim):
    return lax.broadcasted_iota(jnp.int32, shape, dim)


def onehot(mask):
    return mask.astype(F32).astype(LOW)


def params(**kw):
    return pltpu.CompilerParams(vmem_limit_bytes=VMEM_BYTES, **kw)


def full(shape):
    return pl.BlockSpec(shape, lambda *_: (0,) * len(shape))


def project_kernel(own, rows, off_ref, x_ref, halo_ref, mask_ref, taps_ref, conv_ref, gain_ref, w_ref, *rest):
    step = pl.program_id(0)
    tile = rest[0].shape[0]
    ext = rest[-1]
    width = x_ref.shape[1]

    @pl.when(step == 0)
    def _():
        ext[0:8, :] = halo_ref[...].astype(F32)
        ext[8:, :] = x_ref[...].astype(F32)

    start = pl.multiple_of(step * tile, tile)
    chunk = ext[pl.ds(start, tile + 8), :]
    lane = pl.multiple_of(off_ref[0] + step * tile, tile)
    same = mask_ref[:, pl.ds(lane, tile)].T
    inputs = chunk[8:, :]
    mixed = taps_ref[0:1, :] * inputs
    for back in range(1, 4):
        mixed = mixed + taps_ref[back : back + 1, :] * chunk[8 - back : 8 - back + tile, :] * same[:, back : back + 1]
    mixed_low = mixed.astype(LOW)
    branch = inputs + dot(mixed_low, conv_ref[...])
    factor = lax.rsqrt(jnp.mean(branch * branch, axis=-1, keepdims=True) + 1e-06)
    normed = (branch * factor * gain_ref[...]).astype(LOW)
    if own:
        branch_ref, mixed_ref, n_ref, q_ref, qt_ref, k_ref, kt_ref, v_ref, vt_ref = rest[:-1]
        qkv = dot(normed, w_ref[...]).astype(LOW)
        query = qkv[:, :width] * jnp.asarray(0.125, LOW)
        q_ref[...] = query
        qt_ref[...] = query.T
        branch_ref[...] = branch
        mixed_ref[...] = mixed_low
        key, value = qkv[:, width : 2 * width], qkv[:, 2 * width :]
    else:
        n_ref, k_ref, kt_ref, v_ref, vt_ref = rest[:-1]
        kv = dot(normed, w_ref[:, width:]).astype(LOW)
        key, value = kv[:, :width], kv[:, width:]
    n_ref[...] = normed
    k_ref[...] = key
    kt_ref[...] = key.T
    v_ref[...] = value
    vt_ref[...] = value.T


def project(own, off, x, halo, masks, taps, conv_proj, gain, w_qkv):
    rows, width = x.shape
    tile = min(256, rows)
    nat = pl.BlockSpec((tile, width), lambda i, *_: (i, 0))
    tra = pl.BlockSpec((width, tile), lambda i, *_: (0, i))
    nat_low = jax.ShapeDtypeStruct((rows, width), LOW)
    tra_low = jax.ShapeDtypeStruct((width, rows), LOW)
    nat_f32 = jax.ShapeDtypeStruct((rows, width), F32)
    if own:
        outs = [(nat_f32, nat), (nat_low, nat), (nat_low, nat), (nat_low, nat), (tra_low, tra)]
    else:
        outs = [(nat_low, nat)]
    outs = outs + [(nat_low, nat), (tra_low, tra), (nat_low, nat), (tra_low, tra)]
    operands = (x, halo, masks, taps, conv_proj, gain, w_qkv)
    return pl.pallas_call(
        functools.partial(project_kernel, own, rows),
        out_shape=[s for s, _ in outs],
        grid_spec=pltpu.PrefetchScalarGridSpec(
            num_scalar_prefetch=1,
            grid=(rows // tile,),
            in_specs=[full(o.shape) for o in operands],
            out_specs=[b for _, b in outs],
            scratch_shapes=[pltpu.VMEM((rows + 8, width), F32)],
        ),
        compiler_params=params(),
        name="project_own" if own else "project_other",
    )(off, *operands)


def word_spans(ids, q_off, k_off, rows_q, rows_k, unit):
    q_first = ids[0, q_off]
    q_wins = (ids[0, q_off + rows_q - 1] - q_first) // QUERY_WORDS + 1
    firsts, wins = [], []
    for at in range(0, rows_k, unit):
        first = ids[0, k_off + at]
        firsts.append(first)
        wins.append((ids[0, k_off + at + unit - 1] - first) // KEY_WORDS + 1)
    fits = q_wins == 1
    for count in wins:
        fits = jnp.logical_and(fits, count == 1)
    return q_first, q_wins, firsts, wins, fits


def unit_of(rows_k):
    return min(512, rows_k)


def stat_rows(rows_k):
    return -(-(2 * (rows_k // unit_of(rows_k)) + 4) // 8) * 8


def attend_kernel(rows_q, rows_k, ids, offs, ids_ref, tab_ref, k_ref, vt_ref, qt_ref, p_ref, o_ref, stat_ref, eqt, ek, bidx, raw):
    pair = pl.program_id(0)
    unit = unit_of(rows_k)
    units = rows_k // unit
    q_off, k_off = offs[0], offs[1]
    q_first, q_wins, firsts, wins, fits = word_spans(ids, q_off, k_off, rows_q, rows_k, unit)
    q_ids = ids_ref[:, pl.ds(pl.multiple_of(q_off, 128), rows_q)]

    def unit_ids(at):
        return ids_ref[:, pl.ds(pl.multiple_of(k_off + at * unit, 128), unit)]

    def query_words(win):
        return onehot(iota((QUERY_WORDS, rows_q), 0) + (q_first + win * QUERY_WORDS) == q_ids)

    def key_words(at, win):
        return onehot(iota((KEY_WORDS, unit), 0) + (firsts[at] + win * KEY_WORDS) == unit_ids(at)).T

    def buckets(at, win, q_win):
        shift = firsts[at] + win * KEY_WORDS - q_first - q_win * QUERY_WORDS
        shape = (KEY_WORDS, QUERY_WORDS)
        return bucketize(shift + iota(shape, 0) - iota(shape, 1))

    def window_bias(head, index):
        row = jnp.broadcast_to(tab_ref[pl.ds(head, 1), :], (KEY_WORDS, 128))
        parts = [
            jnp.take_along_axis(row, index[:, c : c + 128], axis=1) for c in range(0, QUERY_WORDS, 128)
        ]
        return jnp.concatenate(parts, axis=1).astype(LOW)

    @pl.when(pair == 0)
    def _():
        eqt[...] = query_words(0)
        for at in range(units):
            ek[at * unit : (at + 1) * unit, :] = key_words(at, 0)
            bidx[at] = buckets(at, 0, 0)

    def queries(side):
        zero = jnp.zeros((64, rows_q), LOW)
        mine = qt_ref[64 * side : 64 * side + 64, :]
        return [mine, zero] if side == 0 else [zero, mine]

    def fast_scores(side, at):
        rows = slice(at * unit, (at + 1) * unit)
        bias = window_bias(2 * pair + side, bidx[at])
        spread = dot(bias, eqt[...]).astype(LOW)
        right = jnp.concatenate(queries(side) + [spread], axis=0)
        left = jnp.concatenate([k_ref[rows, :], ek[rows, :]], axis=1)
        return dot(left, right)

    def slow_scores(side, at):
        rows = slice(at * unit, (at + 1) * unit)
        raw[...] = dot(k_ref[rows, :], jnp.concatenate(queries(side), axis=0))

        def over_keys(win, carry):
            def over_queries(q_win, inner):
                bias = window_bias(2 * pair + side, buckets(at, win, q_win))
                spread = dot(bias, query_words(q_win)).astype(LOW)
                raw[...] += dot(key_words(at, win), spread)
                return inner

            return lax.fori_loop(0, q_wins, over_queries, carry)

        lax.fori_loop(0, wins[at], over_keys, 0)
        return raw[...]

    def run(scores):
        ones = jnp.ones((16, unit), LOW)
        for side in range(2):
            total = peak = None
            for at in range(units):
                rows = slice(at * unit, (at + 1) * unit)
                score = scores(side, at)
                top = jnp.max(score, axis=0, keepdims=True)
                expo = jnp.exp(score - top).astype(LOW)
                p_ref[side, rows, :] = expo
                left = jnp.concatenate([vt_ref[64 * side : 64 * side + 64, rows], ones], axis=0)
                part = dot(left, expo)
                stat_ref[0, side * units + at : side * units + at + 1, :] = top
                if total is None:
                    total, peak = part, top
                else:
                    higher = jnp.maximum(peak, top)
                    total = total * jnp.exp(peak - higher) + part * jnp.exp(top - higher)
                    peak = higher
            o_ref[64 * side : 64 * side + 64, :] = total[:64, :]
            stat_ref[0, 2 * units + side : 2 * units + side + 1, :] = peak
            stat_ref[0, 2 * units + 2 + side : 2 * units + 3 + side, :] = total[64:65, :]

    @pl.when(fits)
    def _():
        run(fast_scores)

    @pl.when(jnp.logical_not(fits))
    def _():
        run(slow_scores)


def attend(ids, offs, tab, key, value_t, query_t):
    rows_k, width = key.shape
    rows_q = query_t.shape[1]
    length = ids.shape[1]
    unit = unit_of(rows_k)
    units = rows_k // unit
    stats = stat_rows(rows_k)
    pairs = width // 128
    return pl.pallas_call(
        functools.partial(attend_kernel, rows_q, rows_k),
        out_shape=[
            jax.ShapeDtypeStruct((2 * pairs, rows_k, rows_q), LOW),
            jax.ShapeDtypeStruct((width, rows_q), F32),
            jax.ShapeDtypeStruct((pairs, stats, rows_q), F32),
        ],
        grid_spec=pltpu.PrefetchScalarGridSpec(
            num_scalar_prefetch=2,
            grid=(pairs,),
            in_specs=[
                full((1, length)),
                full(tab.shape),
                pl.BlockSpec((rows_k, 128), lambda p, *_: (0, p)),
                pl.BlockSpec((128, rows_k), lambda p, *_: (p, 0)),
                pl.BlockSpec((128, rows_q), lambda p, *_: (p, 0)),
            ],
            out_specs=[
                pl.BlockSpec((2, rows_k, rows_q), lambda p, *_: (p, 0, 0)),
                pl.BlockSpec((128, rows_q), lambda p, *_: (p, 0)),
                pl.BlockSpec((1, stats, rows_q), lambda p, *_: (p, 0, 0)),
            ],
            scratch_shapes=[
                pltpu.VMEM((QUERY_WORDS, rows_q), LOW),
                pltpu.VMEM((rows_k, KEY_WORDS), LOW),
                pltpu.VMEM((units, KEY_WORDS, QUERY_WORDS), jnp.int32),
                pltpu.VMEM((unit, rows_q), F32),
            ],
        ),
        compiler_params=params(),
        name="attend",
    )(ids, offs, ids, tab, key, value_t, query_t)


def attend_back_kernel(rows_q, rows_k, ids, offs, ids_ref, p_ref, kt_ref, v_ref, q_ref, dot_ref, cs_ref, rd_ref, dq_ref, dk_ref, dv_ref, gb_ref, eq, ekt, bmask, spread, held, by_word):
    pair = pl.program_id(0)
    unit = unit_of(rows_k)
    units = rows_k // unit
    q_off, k_off = offs[0], offs[1]
    q_first, q_wins, firsts, wins, fits = word_spans(ids, q_off, k_off, rows_q, rows_k, unit)
    q_ids = ids_ref[:, pl.ds(pl.multiple_of(q_off, 128), rows_q)]

    def unit_ids(at):
        return ids_ref[:, pl.ds(pl.multiple_of(k_off + at * unit, 128), unit)]

    def query_words(win):
        return onehot(iota((QUERY_WORDS, rows_q), 0) + (q_first + win * QUERY_WORDS) == q_ids).T

    def key_words(at, win):
        return onehot(iota((KEY_WORDS, unit), 0) + (firsts[at] + win * KEY_WORDS) == unit_ids(at))

    def bucket_mask(at, win, q_win):
        lane = iota((32, FOLD), 1)
        ahead = jnp.where(lane < FOLD - KEY_WORDS, lane, lane - FOLD)
        shift = firsts[at] + win * KEY_WORDS - q_first - q_win * QUERY_WORDS
        return (bucketize(shift - ahead) == iota((32, FOLD), 0)).astype(F32)

    @pl.when(pair == 0)
    def _():
        eq[...] = query_words(0)
        gb_ref[...] = jnp.zeros_like(gb_ref)
        spread[...] = jnp.zeros_like(spread)
        for at in range(units):
            ekt[:, at * unit : (at + 1) * unit] = key_words(at, 0)
            bmask[at] = bucket_mask(at, 0, 0)

    def add_bias_grad(head, by_key_word, words, mask):
        spread[:, :QUERY_WORDS] = dot(by_key_word, words)
        grid = spread[...]
        half = KEY_WORDS // 2
        while half >= 8:
            grid = grid[:half, :] + pltpu.roll(grid[half:, :], FOLD - half, 1)
            half //= 2
        row = iota((8, FOLD), 0)
        for bit in (4, 2, 1):
            grid = jnp.where((row & bit) != 0, pltpu.roll(grid, FOLD - bit, 1), grid)
        folded = jnp.sum(grid, axis=0, keepdims=True)
        binned = jnp.sum(mask * folded, axis=1, keepdims=True)
        gb_ref[...] += jnp.where(iota(gb_ref.shape, 1) == head, binned, 0.0)

    def scaled_dout(side, at):
        scale = cs_ref[0, side * units + at : side * units + at + 1, :]
        return (dot_ref[64 * side : 64 * side + 64, :].astype(F32) * scale).astype(LOW)

    def grad_scores(side, at, scaled):
        rows = slice(at * unit, (at + 1) * unit)
        zero = jnp.zeros((64, rows_q), LOW)
        scale = cs_ref[0, side * units + at : side * units + at + 1, :]
        rowdot = rd_ref[pl.ds(2 * pair + side, 1), :] * scale
        right = jnp.concatenate([scaled, zero] if side == 0 else [zero, scaled], axis=0)
        grad_p = dot(v_ref[rows, :], right)
        return (p_ref[side, rows, :].astype(F32) * (grad_p - rowdot)).astype(LOW)

    for at in range(units):
        rows = slice(at * unit, (at + 1) * unit)
        scaled = [scaled_dout(side, at) for side in range(2)]
        natural = jnp.concatenate(scaled, axis=0).T
        dks, dvs = [], []
        for side in range(2):
            ds = grad_scores(side, at, scaled[side])
            dvs.append(dot(p_ref[side, rows, :], natural))
            dks.append(dot(ds, q_ref[...]))
            key_t = kt_ref[64 * side : 64 * side + 64, rows]
            both = dot(jnp.concatenate([key_t, ekt[:, rows]], axis=0), ds)
            add_bias_grad(2 * pair + side, both[64:, :].astype(LOW), eq[...], bmask[at])
            if at == 0:
                dq_ref[64 * side : 64 * side + 64, :] = both[:64, :]
            else:
                dq_ref[64 * side : 64 * side + 64, :] += both[:64, :]
        first = iota((unit, 128), 1) < 64
        dk_ref[rows, :] = jnp.where(first, dks[0], dks[1]).astype(LOW)
        dv_ref[rows, :] = jnp.where(first, dvs[0], dvs[1]).astype(LOW)

    @pl.when(jnp.logical_not(fits))
    def _():
        for at in range(units):
            for side in range(2):
                held[...] = grad_scores(side, at, scaled_dout(side, at))

                def over_keys(win, carry, at=at, side=side):
                    by_word[...] = dot(key_words(at, win), held[...]).astype(LOW)

                    def over_queries(q_win, inner):
                        add_bias_grad(2 * pair + side, by_word[...], query_words(q_win), bucket_mask(at, win, q_win))
                        return inner

                    return lax.fori_loop(jnp.where(win == 0, 1, 0), q_wins, over_queries, carry)

                lax.fori_loop(0, wins[at], over_keys, 0)


def attend_back(ids, offs, p, key_t, value, query, dout_t, scales, rowdot):
    width, rows_k = key_t.shape
    rows_q = query.shape[0]
    length = ids.shape[1]
    unit = unit_of(rows_k)
    units = rows_k // unit
    stats = scales.shape[1]
    pairs = width // 128
    return pl.pallas_call(
        functools.partial(attend_back_kernel, rows_q, rows_k),
        out_shape=[
            jax.ShapeDtypeStruct((width, rows_q), F32),
            jax.ShapeDtypeStruct((rows_k, width), LOW),
            jax.ShapeDtypeStruct((rows_k, width), LOW),
            jax.ShapeDtypeStruct((32, 128), F32),
        ],
        grid_spec=pltpu.PrefetchScalarGridSpec(
            num_scalar_prefetch=2,
            grid=(pairs,),
            in_specs=[
                full((1, length)),
                pl.BlockSpec((2, rows_k, rows_q), lambda p, *_: (p, 0, 0)),
                pl.BlockSpec((128, rows_k), lambda p, *_: (p, 0)),
                pl.BlockSpec((rows_k, 128), lambda p, *_: (0, p)),
                pl.BlockSpec((rows_q, 128), lambda p, *_: (0, p)),
                pl.BlockSpec((128, rows_q), lambda p, *_: (p, 0)),
                pl.BlockSpec((1, stats, rows_q), lambda p, *_: (p, 0, 0)),
                full(rowdot.shape),
            ],
            out_specs=[
                pl.BlockSpec((128, rows_q), lambda p, *_: (p, 0)),
                pl.BlockSpec((rows_k, 128), lambda p, *_: (0, p)),
                pl.BlockSpec((rows_k, 128), lambda p, *_: (0, p)),
                full((32, 128)),
            ],
            scratch_shapes=[
                pltpu.VMEM((rows_q, QUERY_WORDS), LOW),
                pltpu.VMEM((KEY_WORDS, rows_k), LOW),
                pltpu.VMEM((units, 32, FOLD), F32),
                pltpu.VMEM((KEY_WORDS, FOLD), F32),
                pltpu.VMEM((unit, rows_q), LOW),
                pltpu.VMEM((KEY_WORDS, rows_q), LOW),
            ],
        ),
        compiler_params=params(),
        name="attend_back",
    )(ids, offs, ids, p, key_t, value, query, dout_t, scales, rowdot)


def norm_back(v, gain, incoming):
    factor = lax.rsqrt(jnp.mean(v * v, axis=-1, keepdims=True) + 1e-06)
    scaled = incoming * gain
    inner = jnp.mean(scaled * v, axis=-1, keepdims=True)
    back = factor * scaled - v * (factor * factor * factor * inner)
    return back, jnp.sum(incoming * v * factor, axis=0, keepdims=True)


def ffn_kernel(blocks, units, *refs):
    step = pl.program_id(0)
    outs, stats = refs[:blocks], refs[blocks : 2 * blocks]
    branch_ref, out_proj_ref, gain_ref, cot_ref, wg_ref, wu_ref, wd_ref = refs[2 * blocks : 2 * blocks + 7]
    rest = refs[2 * blocks + 7 :]
    scales = rest[:blocks]
    result_ref, datt_ref, dout_ref, rd_ref, dwo_ref, dgain_ref, grads_ref = rest[blocks : blocks + 7]
    attn, attn_low, after, n2, n2t, y_acc, dn_acc = rest[blocks + 7 :]
    heads = attn.shape[0] // 64
    chunk = wg_ref.shape[1]
    rows = after.shape[0]

    @pl.when(step == 0)
    def _():
        for head in range(heads):
            pair, side = head // 2, head % 2
            peaks = [s[pair, 2 * units + side : 2 * units + side + 1, :] for s in stats]
            top = functools.reduce(jnp.maximum, peaks)
            shares = [jnp.exp(peak - top) for peak in peaks]
            sums = [s[pair, 2 * units + 2 + side : 2 * units + 3 + side, :] for s in stats]
            inverse = 1.0 / functools.reduce(jnp.add, [a * b for a, b in zip(shares, sums)])
            band = slice(64 * head, 64 * head + 64)
            attn[band, :] = functools.reduce(
                jnp.add, [o[band, :] * (share * inverse) for o, share in zip(outs, shares)]
            )
            for s, c in zip(stats, scales):
                c[pair, side * units : (side + 1) * units, :] = (
                    jnp.exp(s[pair, side * units : (side + 1) * units, :] - top) * inverse
                )
        attn_low[...] = attn[...].astype(LOW)
        joined = branch_ref[...] + dot(attn_low[...].T, out_proj_ref[...])
        after[...] = joined
        factor = lax.rsqrt(jnp.mean(joined * joined, axis=-1, keepdims=True) + 1e-06)
        normed = (joined * factor * gain_ref[...]).astype(LOW)
        n2[...] = normed
        n2t[...] = normed.T

    weights = jnp.concatenate([wg_ref[...], wu_ref[...]], axis=1)
    both = dot(n2[...], weights)
    gate, up = both[:, :chunk], both[:, chunk:]
    grad_hidden = dot_nt(cot_ref[...], wd_ref[...])
    square = gate * gate
    inner = gate * (0.7978845608028654 + (0.7978845608028654 * 0.044715) * square)
    part = 0.5 + 0.5 * jnp.tanh(inner)
    act = gate * part
    slope = part + 2.0 * act * (1.0 - part) * (
        0.7978845608028654 + (3.0 * 0.7978845608028654 * 0.044715) * square
    )
    hidden = (act * up).astype(LOW)
    grad_both = jnp.concatenate(
        [(grad_hidden * up * slope).astype(LOW), (grad_hidden * act).astype(LOW)], axis=1
    )
    y_part = dot(hidden, wd_ref[...])
    dn_part = dot_nt(grad_both, weights)

    @pl.when(step == 0)
    def _():
        y_acc[...] = y_part
        dn_acc[...] = dn_part

    @pl.when(step > 0)
    def _():
        y_acc[...] += y_part
        dn_acc[...] += dn_part

    width = after.shape[1]
    grad_w = dot(n2t[...], grad_both).astype(LOW)
    grads_ref[0, :width, :] = grad_w[:, :chunk]
    grads_ref[0, width : 2 * width, :] = grad_w[:, chunk:]
    grad_d = dot(hidden.T, cot_ref[...]).astype(LOW)
    for at in range(width // chunk):
        grads_ref[0, 2 * width + at * chunk : 2 * width + (at + 1) * chunk, :] = grad_d[:, at * chunk : (at + 1) * chunk]

    @pl.when(step == pl.num_programs(0) - 1)
    def _():
        result_ref[...] = (after[...] + y_acc[...]).astype(LOW)
        back, dgain = norm_back(after[...], gain_ref[...], dn_acc[...])
        datt = cot_ref[...].astype(F32) + back
        datt_ref[...] = datt
        dgain_ref[...] = jnp.broadcast_to(dgain, dgain_ref.shape)
        datt_low = datt.astype(LOW)
        dout = dot_nt(out_proj_ref[...], datt_low).astype(LOW)
        dout_ref[...] = dout
        dwo = dot(attn_low[...], datt_low).astype(LOW)
        for at in range(width // chunk):
            dwo_ref[at] = dwo[:, at * chunk : (at + 1) * chunk]
        prod = dout.astype(F32) * attn[...]
        for head in range(heads):
            rd_ref[head : head + 1, :] = jnp.sum(prod[64 * head : 64 * head + 64, :], axis=0, keepdims=True)


def feed_forward(outs, stats, branch, out_proj, gain, cot, w_gate_up, w_down, units):
    rows, width = branch.shape
    hidden = w_down.shape[0]
    chunk = 256
    steps = hidden // chunk
    blocks = len(outs)
    heads = width // 64
    once = lambda shape: pl.BlockSpec(shape, lambda *_: (0,) * len(shape), pipeline_mode=pl.Buffered(1))
    nat = (rows, width)
    return pl.pallas_call(
        functools.partial(ffn_kernel, blocks, units),
        grid=(steps,),
        out_shape=[jax.ShapeDtypeStruct(s.shape, F32) for s in stats]
        + [
            jax.ShapeDtypeStruct(nat, LOW),
            jax.ShapeDtypeStruct(nat, F32),
            jax.ShapeDtypeStruct((width, rows), LOW),
            jax.ShapeDtypeStruct((heads, rows), F32),
            jax.ShapeDtypeStruct((width // chunk, width, chunk), LOW),
            jax.ShapeDtypeStruct((8, width), F32),
            jax.ShapeDtypeStruct((steps, 3 * width, chunk), LOW),
        ],
        in_specs=[once(o.shape) for o in outs]
        + [once(s.shape) for s in stats]
        + [
            once(nat),
            once((width, width)),
            once((1, width)),
            once(nat),
            pl.BlockSpec((width, chunk), lambda i: (0, i)),
            pl.BlockSpec((width, chunk), lambda i: (0, i + steps)),
            pl.BlockSpec((chunk, width), lambda i: (i, 0)),
        ],
        out_specs=[once(s.shape) for s in stats]
        + [
            once(nat),
            once(nat),
            once((width, rows)),
            once((heads, rows)),
            once((width // chunk, width, chunk)),
            once((8, width)),
            pl.BlockSpec((1, 3 * width, chunk), lambda i: (i, 0, 0)),
        ],
        scratch_shapes=[
            pltpu.VMEM((width, rows), F32),
            pltpu.VMEM((width, rows), LOW),
            pltpu.VMEM(nat, F32),
            pltpu.VMEM(nat, LOW),
            pltpu.VMEM((width, rows), LOW),
            pltpu.VMEM(nat, F32),
            pltpu.VMEM(nat, F32),
        ],
        compiler_params=params(),
        name="feed_forward",
    )(*outs, *stats, branch, out_proj, gain, cot, w_gate_up, w_gate_up, w_down)


def back_other_kernel(dk_ref, dv_ref, n_ref, w_ref, dn_ref, dw_ref):
    width = n_ref.shape[1]
    both = jnp.concatenate([dk_ref[...], dv_ref[...]], axis=1)
    dn_ref[...] = dot_nt(both, w_ref[:, width:]).astype(LOW)
    part = dot(n_ref[...].T, both)

    @pl.when(pl.program_id(0) == 0)
    def _():
        dw_ref[...] = part

    @pl.when(pl.program_id(0) > 0)
    def _():
        dw_ref[...] += part


def back_other(dk, dv, normed, w_qkv):
    rows, width = dk.shape
    tile = min(512, rows)
    nat = pl.BlockSpec((tile, width), lambda i: (i, 0))
    return pl.pallas_call(
        back_other_kernel,
        grid=(rows // tile,),
        out_shape=[jax.ShapeDtypeStruct((rows, width), LOW), jax.ShapeDtypeStruct((width, 2 * width), F32)],
        in_specs=[nat, nat, nat, full(w_qkv.shape)],
        out_specs=[nat, full((width, 2 * width))],
        compiler_params=params(),
        name="back_other",
    )(dk, dv, normed, w_qkv)


def finish_kernel(blocks, off_ref, *refs):
    dqs, parts = refs[:blocks], refs[blocks : 2 * blocks - 1]
    dk_ref, dv_ref, n_ref, branch_ref, gain_ref, datt_ref, mixed_ref, conv_ref, w_ref, taps_ref, mask_ref, x_ref, halo_ref, dwkv_ref = refs[
        2 * blocks - 1 : 2 * blocks + 13
    ]
    gx_ref, ret_ref, dw_ref, dwc_ref, small_ref, ext, edge = refs[2 * blocks + 13 :]
    rows, width = dk_ref.shape
    chunk = dw_ref.shape[2]
    dq = (functools.reduce(jnp.add, [r[...] for r in dqs]) * 0.125).astype(LOW).T
    dqkv = jnp.concatenate([dq, dk_ref[...], dv_ref[...]], axis=1)
    dn = dot_nt(dqkv, w_ref[...])
    for part in parts:
        dn = dn + part[...].astype(F32)
    dw = dot(n_ref[...].T, dqkv)
    for at in range(dw_ref.shape[0]):
        piece = dw[:, at * chunk : (at + 1) * chunk]
        if at * chunk >= width:
            piece = piece + dwkv_ref[:, at * chunk - width : (at + 1) * chunk - width]
        dw_ref[at] = piece.astype(LOW)
    back, dgain = norm_back(branch_ref[...], gain_ref[...], dn)
    dbranch = datt_ref[...] + back
    dbranch_low = dbranch.astype(LOW)
    dwc = dot(mixed_ref[...].T, dbranch_low).astype(LOW)
    for at in range(dwc_ref.shape[0]):
        dwc_ref[at] = dwc[:, at * chunk : (at + 1) * chunk]
    dmixed = dot_nt(dbranch_low, conv_ref[...])
    same = mask_ref[:, pl.ds(pl.multiple_of(off_ref[0], 128), rows)].T
    ext[0:8, :] = halo_ref[...].astype(F32)
    ext[8:, :] = x_ref[...].astype(F32)
    edge[0:8, :] = jnp.zeros((8, width), F32)
    edge[8 + rows :, :] = jnp.zeros((8, width), F32)
    small_ref[...] = jnp.zeros_like(small_ref)
    small_ref[4:5, :] = dgain
    grad = dbranch + taps_ref[0:1, :] * dmixed
    small_ref[0:1, :] = jnp.sum(dmixed * ext[8:, :], axis=0, keepdims=True)
    returned = jnp.zeros((8, width), F32)
    for back_by in range(1, 4):
        masked = dmixed * same[:, back_by : back_by + 1]
        small_ref[back_by : back_by + 1, :] = jnp.sum(masked * ext[8 - back_by : 8 - back_by + rows, :], axis=0, keepdims=True)
        edge[8 : 8 + rows, :] = masked
        tap = taps_ref[back_by : back_by + 1, :]
        grad = grad + tap * edge[8 + back_by : 8 + back_by + rows, :]
        returned = returned + tap * edge[back_by : back_by + 8, :]
    gx_ref[...] = grad
    ret_ref[...] = returned


def finish(off, dqs, parts, dk, dv, normed, branch, gain, datt, mixed, conv_proj, w_qkv, taps, masks, x, halo, dw_kv):
    rows, width = dk.shape
    chunk = 256
    operands = (*dqs, *parts, dk, dv, normed, branch, gain, datt, mixed, conv_proj, w_qkv, taps, masks, x, halo, dw_kv)
    outs = [
        jax.ShapeDtypeStruct((rows, width), F32),
        jax.ShapeDtypeStruct((8, width), F32),
        jax.ShapeDtypeStruct((3 * width // chunk, width, chunk), LOW),
        jax.ShapeDtypeStruct((width // chunk, width, chunk), LOW),
        jax.ShapeDtypeStruct((8, width), F32),
    ]
    return pl.pallas_call(
        functools.partial(finish_kernel, len(dqs)),
        out_shape=outs,
        grid_spec=pltpu.PrefetchScalarGridSpec(
            num_scalar_prefetch=1,
            grid=(1,),
            in_specs=[full(o.shape) for o in operands],
            out_specs=[full(o.shape) for o in outs],
            scratch_shapes=[pltpu.VMEM((rows + 8, width), F32), pltpu.VMEM((rows + 16, width), F32)],
        ),
        compiler_params=params(),
        name="finish",
    )(off, *operands)


def hops(sizes):
    bits = [("dp", 1)]
    bits += [("seq", 1 << b) for b in range(sizes["seq"].bit_length() - 1)]
    bits += [("dp", 1 << b) for b in range(1, sizes["dp"].bit_length() - 1)]
    return bits


def swap(value, axis, bit):
    return lax.ppermute(value, axis, [(i, i ^ bit) for i in range(lax.axis_size(axis))])


def all_sum(value, order):
    for axis, bit in order:
        mine = (lax.axis_index(axis) // bit) % 2
        half = value.shape[0] // 2
        keep = lax.dynamic_slice_in_dim(value, mine * half, half, 0)
        send = lax.dynamic_slice_in_dim(value, (1 - mine) * half, half, 0)
        value = (keep.astype(F32) + swap(send, axis, bit).astype(F32)).astype(LOW)
    for axis, bit in reversed(order):
        mine = (lax.axis_index(axis) // bit) % 2
        other = swap(value, axis, bit)
        low = jnp.where(mine == 0, value, other)
        high = jnp.where(mine == 0, other, value)
        value = jnp.concatenate([low, high], axis=0)
    return value


def total(terms):
    if len(terms) == 1:
        return terms[0]
    return functools.reduce(jnp.add, [t.astype(F32) for t in terms]).astype(terms[0].dtype)


def shards(sizes, tokens, word_ids, cotangent, conv_kernels, conv_proj, gain_attn, w_qkv, rel_bias, out_proj, gain_ffn, w_gate_up, w_down):
    seqs, rows, width = tokens.shape
    heads = rel_bias.shape[1]
    ring = sizes["seq"]
    me = lax.axis_index("seq")
    kernels = conv_kernels.astype(F32)
    taps = jnp.stack(
        [
            kernels[0] + kernels[2] + kernels[5],
            kernels[1] + kernels[3] + kernels[6],
            kernels[4] + kernels[7],
            kernels[8],
        ]
        + [jnp.zeros_like(kernels[0])] * 4
    )
    gain_one = gain_attn.astype(F32)[None, :]
    gain_two = gain_ffn.astype(F32)[None, :]
    tab = jnp.pad(rel_bias.astype(F32).T, ((0, 0), (0, 128 - rel_bias.shape[0])))
    length = word_ids.shape[1]
    place = jnp.arange(length)[None, :]
    masks = jnp.stack(
        [
            ((jnp.roll(word_ids, back, axis=1) == word_ids) & (place >= back)).astype(F32)
            for back in range(4)
        ]
        + [jnp.zeros(word_ids.shape, F32)] * 4,
        axis=1,
    )
    halo = lax.ppermute(tokens[:, rows - 8 :, :], "seq", [(i, (i + 1) % ring) for i in range(ring)])
    block_tokens = [tokens] + [
        lax.ppermute(tokens, "seq", [((i + k) % ring, i) for i in range(ring)]) for k in range(1, ring)
    ]
    halos = [halo] + [b[:, rows - 8 :, :] for b in block_tokens[:-1]]
    offs = [(((me + k) % ring) * rows).astype(jnp.int32).reshape(1) for k in range(ring)]
    units = rows // unit_of(rows)

    results, gxs, rets = [], [], []
    g_ffn, g_out, g_qkv, g_conv, smalls, dgains, biases = [], [], [], [], [], [], []
    for s in range(seqs):
        ids = word_ids[s : s + 1]
        own = project(True, offs[0], tokens[s], halos[0][s], masks[s], taps, conv_proj, gain_one, w_qkv)
        branch, mixed, normed, query, query_t, key, key_t, value, value_t = own
        held = [(normed, key, key_t, value, value_t)]
        for k in range(1, ring):
            held.append(project(False, offs[k], block_tokens[k][s], halos[k][s], masks[s], taps, conv_proj, gain_one, w_qkv))
        spots = [jnp.concatenate([offs[0], offs[k]]) for k in range(ring)]
        fwd = [attend(ids, spots[k], tab, held[k][1], held[k][4], query_t) for k in range(ring)]
        ffn = feed_forward(
            [f[1] for f in fwd], [f[2] for f in fwd], branch, out_proj, gain_two, cotangent[s], w_gate_up, w_down, units
        )
        scales = ffn[:ring]
        result, datt, dout_t, rowdot, dwo, dgain, grads = ffn[ring:]
        results.append(result)
        g_ffn.append(grads)
        g_out.append(dwo)
        dgains.append(dgain[0:1])
        dqs, parts, dw_kvs = [], [], []
        for k in list(range(1, ring)) + [0]:
            dq, dk, dv, gb = attend_back(
                ids, spots[k], fwd[k][0], held[k][2], held[k][3], query, dout_t, scales[k], rowdot
            )
            dqs.append(dq)
            biases.append(gb)
            if k > 0:
                dn, dw_kv = back_other(dk, dv, held[k][0], w_qkv)
                parts.append(lax.ppermute(dn, "seq", [(i, (i + k) % ring) for i in range(ring)]))
                dw_kvs.append(dw_kv)
        dw_kv = total(dw_kvs) if dw_kvs else jnp.zeros((width, 2 * width), F32)
        gx, ret, dw, dwc, small = finish(
            offs[0], dqs, parts, dk, dv, normed, branch, gain_one, datt, mixed, conv_proj, w_qkv, taps,
            masks[s], tokens[s], halos[0][s], dw_kv,
        )
        gxs.append(gx)
        rets.append(ret)
        g_qkv.append(dw)
        g_conv.append(dwc)
        smalls.append(small)

    order = hops(sizes)
    steps = g_ffn[0].shape[0]
    summed = all_sum(total(g_ffn).reshape(-1, 256), order).reshape(steps, 3, width, 256)
    bias = total(biases)[:, :heads].reshape(1, -1)
    few = jnp.concatenate(
        [total(smalls)[:5], total(dgains), jnp.pad(bias, ((0, 0), (0, width - bias.shape[1])))]
    )
    few = few.astype(LOW).reshape(-1, 256)
    devices = sizes["seq"] * sizes["dp"]
    few = jnp.pad(few, ((0, -(few.shape[0] + 5 * width * width // 256) % devices), (0, 0)))
    rest = jnp.concatenate(
        [total(g_out).reshape(-1, 256), total(g_qkv).reshape(-1, 256), total(g_conv).reshape(-1, 256), few]
    )
    rest = all_sum(rest, order).astype(F32)
    square = width * width // 256

    def columns(part):
        return part.reshape(-1, width, 256).transpose(1, 0, 2).reshape(width, -1)

    grad_out_proj = columns(rest[:square])
    grad_w_qkv = columns(rest[square : 4 * square])
    grad_conv_proj = columns(rest[4 * square : 5 * square])
    few = rest[5 * square : 5 * square + 14].reshape(-1, width)
    ffn_sum = summed.astype(F32)
    grad_gate_up = jnp.concatenate(
        [ffn_sum[:, j].transpose(1, 0, 2).reshape(width, -1) for j in range(2)], axis=1
    )
    grad_down = ffn_sum[:, 2].reshape(steps, width // 256, 256, 256).transpose(0, 2, 1, 3).reshape(-1, width)
    g = [few[j] for j in range(4)]
    grad_kernels = jnp.stack([g[0], g[1], g[0], g[1], g[2], g[0], g[1], g[2], g[3]])
    returned = lax.ppermute(jnp.stack(rets), "seq", [(i, i - 1) for i in range(1, ring)])
    grad_tokens = jnp.stack(gxs)
    grad_tokens = grad_tokens.at[:, rows - 8 :, :].add(returned)
    return (
        jnp.stack(results),
        grad_tokens,
        grad_kernels,
        grad_conv_proj,
        few[4],
        grad_w_qkv,
        few[6, : 32 * heads].reshape(32, heads),
        grad_out_proj,
        few[5],
        grad_gate_up,
        grad_down,
    )


def solution(mesh):
    sizes = dict(mesh.shape)
    split = P("dp", "seq", None)
    in_specs = (split, P("dp", None), split) + (P(),) * 9
    out_specs = (split, split) + (P(),) * 9
    return jax.shard_map(
        functools.partial(shards, sizes), mesh=mesh, in_specs=in_specs, out_specs=out_specs, check_vma=False
    )
```

```python
import functools

import jax
import jax.numpy as jnp
from jax import lax
from jax.experimental import pallas as pl
from jax.experimental.pallas import tpu as pltpu
from jax.sharding import PartitionSpec as P

LOW = jnp.bfloat16
F32 = jnp.float32
EDGES = (1, 2, 3, 4, 5, 6, 7, 8, 11, 16, 22, 32, 45, 64, 91)
KEY_WORDS = 128
QUERY_WORDS = 256
FOLD = 512
VMEM_BYTES = 60 * 2**20


def bucketize(offsets):
    magnitude = jnp.abs(offsets)
    bucketed = jnp.where(offsets > 0, 16, 0).astype(jnp.int32)
    for edge in EDGES:
        bucketed = bucketed + (magnitude >= edge).astype(jnp.int32)
    return bucketed


def dot(a, b):
    return jnp.dot(a, b, preferred_element_type=F32)


def dot_nt(a, b):
    return lax.dot_general(a, b, (((1,), (1,)), ((), ())), preferred_element_type=F32)


def iota(shape, dim):
    return lax.broadcasted_iota(jnp.int32, shape, dim)


def onehot(mask):
    return mask.astype(F32).astype(LOW)


def params(**kw):
    return pltpu.CompilerParams(vmem_limit_bytes=VMEM_BYTES, **kw)


def cost(micros):
    return pl.CostEstimate(flops=int(micros * 1e9), bytes_accessed=int(micros * 1e6), transcendentals=0)


def full(shape):
    return pl.BlockSpec(shape, lambda *_: (0,) * len(shape))


def make_taps(kernels):
    k = kernels.astype(F32)
    return [
        k[0:1] + k[2:3] + k[5:6],
        k[1:2] + k[3:4] + k[6:7],
        k[4:5] + k[7:8],
        k[8:9],
    ]


def same_words(ids):
    place = iota(ids.shape, 1)
    rows = [
        jnp.where((pltpu.roll(ids, back, 1) == ids) & (place >= back), 1.0, 0.0) for back in range(1, 4)
    ]
    return jnp.concatenate([jnp.zeros(ids.shape, F32)] + rows + [jnp.zeros((4, ids.shape[1]), F32)], axis=0)


def project_kernel(own, at, info, x_ref, halo_ref, ids_ref, kernels_ref, conv_ref, gain_ref, w_ref, *rest):
    step = pl.program_id(0)
    tile = rest[0].shape[0]
    ext, masks = rest[-2:]
    width = x_ref.shape[1]

    @pl.when(step == 0)
    def _():
        ext[0:8, :] = halo_ref[...].astype(F32)
        ext[8:, :] = x_ref[...].astype(F32)
        masks[...] = same_words(ids_ref[...])

    start = pl.multiple_of(step * tile, tile)
    chunk = ext[pl.ds(start, tile + 8), :]
    lane = pl.multiple_of(info[at] + step * tile, tile)
    same = masks[:, pl.ds(lane, tile)].T
    taps = make_taps(kernels_ref[...])
    inputs = chunk[8:, :]
    mixed = taps[0] * inputs
    for back in range(1, 4):
        mixed = mixed + taps[back] * chunk[8 - back : 8 - back + tile, :] * same[:, back : back + 1]
    mixed_low = mixed.astype(LOW)
    branch = inputs + dot(mixed_low, conv_ref[...])
    factor = lax.rsqrt(jnp.mean(branch * branch, axis=-1, keepdims=True) + 1e-06)
    normed = (branch * factor * gain_ref[...].astype(F32)).astype(LOW)
    if own:
        branch_ref, mixed_ref, n_ref, q_ref, qt_ref, k_ref, kt_ref, v_ref, vt_ref = rest[:-2]
        qkv = dot(normed, w_ref[...]).astype(LOW)
        query = qkv[:, :width] * jnp.asarray(0.125, LOW)
        q_ref[...] = query
        qt_ref[...] = query.T
        branch_ref[...] = branch
        mixed_ref[...] = mixed_low
        key, value = qkv[:, width : 2 * width], qkv[:, 2 * width :]
    else:
        n_ref, k_ref, kt_ref, v_ref, vt_ref = rest[:-2]
        kv = dot(normed, w_ref[:, width:]).astype(LOW)
        key, value = kv[:, :width], kv[:, width:]
    n_ref[...] = normed
    k_ref[...] = key
    kt_ref[...] = key.T
    v_ref[...] = value
    vt_ref[...] = value.T


def project(own, at, info, x, halo, ids, kernels, conv_proj, gain, w_qkv):
    rows, width = x.shape
    tile = min(256, rows)
    nat = pl.BlockSpec((tile, width), lambda i, *_: (i, 0))
    tra = pl.BlockSpec((width, tile), lambda i, *_: (0, i))
    nat_low = jax.ShapeDtypeStruct((rows, width), LOW)
    tra_low = jax.ShapeDtypeStruct((width, rows), LOW)
    nat_f32 = jax.ShapeDtypeStruct((rows, width), F32)
    if own:
        outs = [(nat_f32, nat), (nat_low, nat), (nat_low, nat), (nat_low, nat), (tra_low, tra)]
    else:
        outs = [(nat_low, nat)]
    outs = outs + [(nat_low, nat), (tra_low, tra), (nat_low, nat), (tra_low, tra)]
    operands = (x, halo, ids, kernels, conv_proj, gain, w_qkv)
    return pl.pallas_call(
        functools.partial(project_kernel, own, at),
        out_shape=[s for s, _ in outs],
        grid_spec=pltpu.PrefetchScalarGridSpec(
            num_scalar_prefetch=1,
            grid=(rows // tile,),
            in_specs=[full(o.shape) for o in operands],
            out_specs=[b for _, b in outs],
            scratch_shapes=[pltpu.VMEM((rows + 8, width), F32), pltpu.VMEM((8, ids.shape[1]), F32)],
        ),
        compiler_params=params(),
        cost_estimate=cost(8 if own else 6),
        name="project_own" if own else "project_other",
    )(info, *operands)


def word_spans(ids, q_off, k_off, rows_q, rows_k, unit):
    q_first = ids[0, q_off]
    q_wins = (ids[0, q_off + rows_q - 1] - q_first) // QUERY_WORDS + 1
    firsts, wins = [], []
    for at in range(0, rows_k, unit):
        first = ids[0, k_off + at]
        firsts.append(first)
        wins.append((ids[0, k_off + at + unit - 1] - first) // KEY_WORDS + 1)
    fits = q_wins == 1
    for count in wins:
        fits = jnp.logical_and(fits, count == 1)
    return q_first, q_wins, firsts, wins, fits


def unit_of(rows_k):
    return min(512, rows_k)


def stat_rows(rows_k):
    return -(-(2 * (rows_k // unit_of(rows_k)) + 4) // 8) * 8


def attend_kernel(rows_q, rows_k, spot, ids, info, ids_ref, bias_ref, k_ref, vt_ref, qt_ref, p_ref, o_ref, stat_ref, eqt, ek, bidx, raw, tab_ref):
    pair = pl.program_id(0)
    unit = unit_of(rows_k)
    units = rows_k // unit
    q_off, k_off = info[0], info[spot]
    q_first, q_wins, firsts, wins, fits = word_spans(ids, q_off, k_off, rows_q, rows_k, unit)
    q_ids = ids_ref[:, pl.ds(pl.multiple_of(q_off, 128), rows_q)]

    def unit_ids(at):
        return ids_ref[:, pl.ds(pl.multiple_of(k_off + at * unit, 128), unit)]

    def query_words(win):
        return onehot(iota((QUERY_WORDS, rows_q), 0) + (q_first + win * QUERY_WORDS) == q_ids)

    def key_words(at, win):
        return onehot(iota((KEY_WORDS, unit), 0) + (firsts[at] + win * KEY_WORDS) == unit_ids(at)).T

    def buckets(at, win, q_win):
        shift = firsts[at] + win * KEY_WORDS - q_first - q_win * QUERY_WORDS
        shape = (KEY_WORDS, QUERY_WORDS)
        return bucketize(shift + iota(shape, 0) - iota(shape, 1))

    def window_bias(head, index):
        row = jnp.broadcast_to(tab_ref[pl.ds(head, 1), :], (KEY_WORDS, 128))
        parts = [
            jnp.take_along_axis(row, index[:, c : c + 128], axis=1) for c in range(0, QUERY_WORDS, 128)
        ]
        return jnp.concatenate(parts, axis=1).astype(LOW)

    @pl.when(pair == 0)
    def _():
        eqt[...] = query_words(0)
        tab_ref[:, : bias_ref.shape[0]] = bias_ref[...].astype(F32).T
        for at in range(units):
            ek[at * unit : (at + 1) * unit, :] = key_words(at, 0)
            bidx[at] = buckets(at, 0, 0)

    def queries(side):
        zero = jnp.zeros((64, rows_q), LOW)
        mine = qt_ref[64 * side : 64 * side + 64, :]
        return [mine, zero] if side == 0 else [zero, mine]

    def fast_scores(side, at):
        rows = slice(at * unit, (at + 1) * unit)
        bias = window_bias(2 * pair + side, bidx[at])
        spread = dot(bias, eqt[...]).astype(LOW)
        right = jnp.concatenate(queries(side) + [spread], axis=0)
        left = jnp.concatenate([k_ref[rows, :], ek[rows, :]], axis=1)
        return dot(left, right)

    def slow_scores(side, at):
        rows = slice(at * unit, (at + 1) * unit)
        raw[...] = dot(k_ref[rows, :], jnp.concatenate(queries(side), axis=0))

        def over_keys(win, carry):
            def over_queries(q_win, inner):
                bias = window_bias(2 * pair + side, buckets(at, win, q_win))
                spread = dot(bias, query_words(q_win)).astype(LOW)
                raw[...] += dot(key_words(at, win), spread)
                return inner

            return lax.fori_loop(0, q_wins, over_queries, carry)

        lax.fori_loop(0, wins[at], over_keys, 0)
        return raw[...]

    def run(scores):
        ones = jnp.ones((16, unit), LOW)
        for side in range(2):
            total = peak = None
            for at in range(units):
                rows = slice(at * unit, (at + 1) * unit)
                score = scores(side, at)
                top = jnp.max(score, axis=0, keepdims=True)
                expo = jnp.exp(score - top).astype(LOW)
                p_ref[side, rows, :] = expo
                left = jnp.concatenate([vt_ref[64 * side : 64 * side + 64, rows], ones], axis=0)
                part = dot(left, expo)
                stat_ref[0, side * units + at : side * units + at + 1, :] = top
                if total is None:
                    total, peak = part, top
                else:
                    higher = jnp.maximum(peak, top)
                    total = total * jnp.exp(peak - higher) + part * jnp.exp(top - higher)
                    peak = higher
            o_ref[64 * side : 64 * side + 64, :] = total[:64, :]
            stat_ref[0, 2 * units + side : 2 * units + side + 1, :] = peak
            stat_ref[0, 2 * units + 2 + side : 2 * units + 3 + side, :] = total[64:65, :]

    @pl.when(fits)
    def _():
        run(fast_scores)

    @pl.when(jnp.logical_not(fits))
    def _():
        run(slow_scores)


def attend(spot, ids, info, rel_bias, key, value_t, query_t):
    rows_k, width = key.shape
    rows_q = query_t.shape[1]
    length = ids.shape[1]
    unit = unit_of(rows_k)
    units = rows_k // unit
    stats = stat_rows(rows_k)
    pairs = width // 128
    return pl.pallas_call(
        functools.partial(attend_kernel, rows_q, rows_k, spot),
        out_shape=[
            jax.ShapeDtypeStruct((2 * pairs, rows_k, rows_q), LOW),
            jax.ShapeDtypeStruct((width, rows_q), F32),
            jax.ShapeDtypeStruct((pairs, stats, rows_q), F32),
        ],
        grid_spec=pltpu.PrefetchScalarGridSpec(
            num_scalar_prefetch=2,
            grid=(pairs,),
            in_specs=[
                full((1, length)),
                full(rel_bias.shape),
                pl.BlockSpec((rows_k, 128), lambda p, *_: (0, p)),
                pl.BlockSpec((128, rows_k), lambda p, *_: (p, 0)),
                pl.BlockSpec((128, rows_q), lambda p, *_: (p, 0)),
            ],
            out_specs=[
                pl.BlockSpec((2, rows_k, rows_q), lambda p, *_: (p, 0, 0)),
                pl.BlockSpec((128, rows_q), lambda p, *_: (p, 0)),
                pl.BlockSpec((1, stats, rows_q), lambda p, *_: (p, 0, 0)),
            ],
            scratch_shapes=[
                pltpu.VMEM((QUERY_WORDS, rows_q), LOW),
                pltpu.VMEM((rows_k, KEY_WORDS), LOW),
                pltpu.VMEM((units, KEY_WORDS, QUERY_WORDS), jnp.int32),
                pltpu.VMEM((unit, rows_q), F32),
                pltpu.VMEM((rel_bias.shape[1], 128), F32),
            ],
        ),
        compiler_params=params(),
        cost_estimate=cost(20),
        name="attend",
    )(ids, info, ids, rel_bias, key, value_t, query_t)


def attend_back_kernel(rows_q, rows_k, spot, pair, ids, info, ids_ref, p_ref, kt_ref, v_ref, q_ref, dot_ref, cs_ref, rd_ref, dq_ref, dk_ref, dv_ref, gb_ref, eq, ekt, bmask, spread, held, by_word):
    at = pl.program_id(0)
    unit = unit_of(rows_k)
    units = rows_k // unit
    q_off, k_off = info[0], info[spot]
    q_first = ids[0, q_off]
    q_wins = (ids[0, q_off + rows_q - 1] - q_first) // QUERY_WORDS + 1
    k_at = k_off + at * unit
    k_first = ids[0, k_at]
    k_wins = (ids[0, k_at + unit - 1] - k_first) // KEY_WORDS + 1
    q_ids = ids_ref[:, pl.ds(pl.multiple_of(q_off, 128), rows_q)]
    k_ids = ids_ref[:, pl.ds(pl.multiple_of(k_at, 128), unit)]

    def query_words(win):
        return onehot(iota((QUERY_WORDS, rows_q), 0) + (q_first + win * QUERY_WORDS) == q_ids).T

    def key_words(win):
        return onehot(iota((KEY_WORDS, unit), 0) + (k_first + win * KEY_WORDS) == k_ids)

    def bucket_mask(win, q_win):
        lane = iota((32, FOLD), 1)
        ahead = jnp.where(lane < FOLD - KEY_WORDS, lane, lane - FOLD)
        shift = k_first + win * KEY_WORDS - q_first - q_win * QUERY_WORDS
        return (bucketize(shift - ahead) == iota((32, FOLD), 0)).astype(F32)

    @pl.when(at == 0)
    def _():
        eq[...] = query_words(0)
        gb_ref[...] = jnp.zeros_like(gb_ref)
        spread[...] = jnp.zeros_like(spread)

    ekt[...] = key_words(0)
    bmask[...] = bucket_mask(0, 0)

    def add_bias_grad(head, by_key_word, words, mask):
        spread[:, :QUERY_WORDS] = dot(by_key_word, words)
        grid = spread[...]
        half = KEY_WORDS // 2
        while half >= 8:
            grid = grid[:half, :] + pltpu.roll(grid[half:, :], FOLD - half, 1)
            half //= 2
        row = iota((8, FOLD), 0)
        for bit in (4, 2, 1):
            grid = jnp.where((row & bit) != 0, pltpu.roll(grid, FOLD - bit, 1), grid)
        folded = jnp.sum(grid, axis=0, keepdims=True)
        binned = jnp.sum(mask * folded, axis=1, keepdims=True)
        gb_ref[...] += jnp.where(iota(gb_ref.shape, 1) == head, binned, 0.0)

    def scale_row(side):
        return cs_ref[0, pl.ds(side * units + at, 1), :]

    def scaled_dout(side):
        return (dot_ref[64 * side : 64 * side + 64, :].astype(F32) * scale_row(side)).astype(LOW)

    def grad_scores(side, scaled):
        zero = jnp.zeros((64, rows_q), LOW)
        rowdot = rd_ref[2 * pair + side : 2 * pair + side + 1, :] * scale_row(side)
        right = jnp.concatenate([scaled, zero] if side == 0 else [zero, scaled], axis=0)
        grad_p = dot(v_ref[...], right)
        return (p_ref[side].astype(F32) * (grad_p - rowdot)).astype(LOW)

    scaled = [scaled_dout(side) for side in range(2)]
    natural = jnp.concatenate(scaled, axis=0).T
    dks, dvs, dqs = [], [], []
    for side in range(2):
        ds = grad_scores(side, scaled[side])
        dvs.append(dot(p_ref[side], natural))
        dks.append(dot(ds, q_ref[...]))
        key_t = kt_ref[64 * side : 64 * side + 64, :]
        both = dot(jnp.concatenate([key_t, ekt[...]], axis=0), ds)
        add_bias_grad(2 * pair + side, both[64:, :].astype(LOW), eq[...], bmask[...])
        dqs.append(both[:64, :])
    first = iota((unit, 128), 1) < 64
    dk_ref[...] = jnp.where(first, dks[0], dks[1]).astype(LOW)
    dv_ref[...] = jnp.where(first, dvs[0], dvs[1]).astype(LOW)

    @pl.when(at == 0)
    def _():
        dq_ref[...] = jnp.concatenate(dqs, axis=0)

    @pl.when(at > 0)
    def _():
        dq_ref[...] += jnp.concatenate(dqs, axis=0)

    @pl.when(jnp.logical_or(q_wins > 1, k_wins > 1))
    def _():
        for side in range(2):
            held[...] = grad_scores(side, scaled_dout(side))

            def over_keys(win, carry, side=side):
                by_word[...] = dot(key_words(win), held[...]).astype(LOW)

                def over_queries(q_win, inner):
                    add_bias_grad(2 * pair + side, by_word[...], query_words(q_win), bucket_mask(win, q_win))
                    return inner

                return lax.fori_loop(jnp.where(win == 0, 1, 0), q_wins, over_queries, carry)

            lax.fori_loop(0, k_wins, over_keys, 0)


def attend_back(spot, pair, ids, info, p, key_t, value, query, dout_t, scales, rowdot):
    width, rows_k = key_t.shape
    rows_q = query.shape[0]
    length = ids.shape[1]
    unit = unit_of(rows_k)
    units = rows_k // unit
    stats = scales.shape[1]
    return pl.pallas_call(
        functools.partial(attend_back_kernel, rows_q, rows_k, spot, pair),
        out_shape=[
            jax.ShapeDtypeStruct((128, rows_q), F32),
            jax.ShapeDtypeStruct((rows_k, 128), LOW),
            jax.ShapeDtypeStruct((rows_k, 128), LOW),
            jax.ShapeDtypeStruct((32, 128), F32),
        ],
        grid_spec=pltpu.PrefetchScalarGridSpec(
            num_scalar_prefetch=2,
            grid=(units,),
            in_specs=[
                full((1, length)),
                pl.BlockSpec((2, unit, rows_q), lambda i, *_: (pair, i, 0)),
                pl.BlockSpec((128, unit), lambda i, *_: (pair, i)),
                pl.BlockSpec((unit, 128), lambda i, *_: (i, pair)),
                pl.BlockSpec((rows_q, 128), lambda i, *_: (0, pair)),
                pl.BlockSpec((128, rows_q), lambda i, *_: (pair, 0)),
                pl.BlockSpec((1, stats, rows_q), lambda i, *_: (pair, 0, 0)),
                full(rowdot.shape),
            ],
            out_specs=[
                full((128, rows_q)),
                pl.BlockSpec((unit, 128), lambda i, *_: (i, 0)),
                pl.BlockSpec((unit, 128), lambda i, *_: (i, 0)),
                full((32, 128)),
            ],
            scratch_shapes=[
                pltpu.VMEM((rows_q, QUERY_WORDS), LOW),
                pltpu.VMEM((KEY_WORDS, unit), LOW),
                pltpu.VMEM((32, FOLD), F32),
                pltpu.VMEM((KEY_WORDS, FOLD), F32),
                pltpu.VMEM((unit, rows_q), LOW),
                pltpu.VMEM((KEY_WORDS, rows_q), LOW),
            ],
        ),
        compiler_params=params(),
        cost_estimate=cost(7),
        name="attend_back",
    )(ids, info, ids, p, key_t, value, query, dout_t, scales, rowdot)


def norm_back(v, gain, incoming):
    factor = lax.rsqrt(jnp.mean(v * v, axis=-1, keepdims=True) + 1e-06)
    scaled = incoming * gain
    inner = jnp.mean(scaled * v, axis=-1, keepdims=True)
    back = factor * scaled - v * (factor * factor * factor * inner)
    return back, jnp.sum(incoming * v * factor, axis=0, keepdims=True)


def ffn_kernel(blocks, units, mes, info, *refs):
    step = pl.program_id(0)
    outs, stats = refs[:blocks], refs[blocks : 2 * blocks]
    branch_ref, out_proj_ref, gain_ref, cot_ref, wg_ref, wu_ref, wd_ref = refs[2 * blocks : 2 * blocks + 7]
    rest = refs[2 * blocks + 7 :]
    scales = rest[:blocks]
    result_ref, datt_ref, dout_ref, rd_ref, dwo_ref, dgain_ref = rest[blocks : blocks + 6]
    pieces = rest[blocks + 6 : blocks + 10]
    attn, attn_low, after, n2, n2t, y_acc, dn_acc = rest[blocks + 10 :]
    heads = attn.shape[0] // 64
    chunk = wg_ref.shape[1]
    rows = after.shape[0]

    @pl.when(step == 0)
    def _():
        for head in range(heads):
            pair, side = head // 2, head % 2
            peaks = [s[pair, 2 * units + side : 2 * units + side + 1, :] for s in stats]
            top = functools.reduce(jnp.maximum, peaks)
            shares = [jnp.exp(peak - top) for peak in peaks]
            sums = [s[pair, 2 * units + 2 + side : 2 * units + 3 + side, :] for s in stats]
            inverse = 1.0 / functools.reduce(jnp.add, [a * b for a, b in zip(shares, sums)])
            band = slice(64 * head, 64 * head + 64)
            attn[band, :] = functools.reduce(
                jnp.add, [o[band, :] * (share * inverse) for o, share in zip(outs, shares)]
            )
            for s, c in zip(stats, scales):
                c[pair, side * units : (side + 1) * units, :] = (
                    jnp.exp(s[pair, side * units : (side + 1) * units, :] - top) * inverse
                )
        attn_low[...] = attn[...].astype(LOW)
        joined = branch_ref[...] + dot(attn_low[...].T, out_proj_ref[...])
        after[...] = joined
        factor = lax.rsqrt(jnp.mean(joined * joined, axis=-1, keepdims=True) + 1e-06)
        normed = (joined * factor * gain_ref[...].astype(F32)).astype(LOW)
        n2[...] = normed
        n2t[...] = normed.T

    weights = jnp.concatenate([wg_ref[...], wu_ref[...]], axis=1)
    both = dot(n2[...], weights)
    gate, up = both[:, :chunk], both[:, chunk:]
    grad_hidden = dot_nt(cot_ref[...], wd_ref[...])
    square = gate * gate
    inner = gate * (0.7978845608028654 + (0.7978845608028654 * 0.044715) * square)
    part = 0.5 + 0.5 * jnp.tanh(inner)
    act = gate * part
    slope = part + 2.0 * act * (1.0 - part) * (
        0.7978845608028654 + (3.0 * 0.7978845608028654 * 0.044715) * square
    )
    hidden = (act * up).astype(LOW)
    grad_both = jnp.concatenate(
        [(grad_hidden * up * slope).astype(LOW), (grad_hidden * act).astype(LOW)], axis=1
    )
    y_part = dot(hidden, wd_ref[...])
    dn_part = dot_nt(grad_both, weights)

    @pl.when(step == 0)
    def _():
        y_acc[...] = y_part
        dn_acc[...] = dn_part

    @pl.when(step > 0)
    def _():
        y_acc[...] += y_part
        dn_acc[...] += dn_part

    grad_w = dot(n2t[...], grad_both).astype(LOW)
    grad_d = dot(hidden.T, cot_ref[...]).astype(LOW)
    for part in range(2):
        turn = info[mes + part] & 7
        for late in range(2):

            @pl.when(step // 2 == 2 * part + late)
            def _(part=part, late=late, turn=turn):
                out = pieces[2 * part + late]
                for k in range(8):
                    col, row = 128 * (k // 4), 128 * (k % 4)
                    spot = k ^ turn
                    out[spot, 0:128, :] = grad_w[row : row + 128, col : col + 128]
                    out[spot, 128:256, :] = grad_w[row : row + 128, chunk + col : chunk + col + 128]
                    out[spot, 256:384, :] = grad_d[col : col + 128, row : row + 128]

    @pl.when(step == pl.num_programs(0) - 1)
    def _():
        result_ref[...] = (after[...] + y_acc[...]).astype(LOW)
        back, dgain = norm_back(after[...], gain_ref[...].astype(F32), dn_acc[...])
        datt = cot_ref[...].astype(F32) + back
        datt_ref[...] = datt
        dgain_ref[...] = jnp.broadcast_to(dgain, dgain_ref.shape)
        datt_low = datt.astype(LOW)
        dout = dot_nt(out_proj_ref[...], datt_low).astype(LOW)
        dout_ref[...] = dout
        dwo_ref[...] = dot(attn_low[...], datt_low).astype(LOW)
        prod = dout.astype(F32) * attn[...]
        for head in range(heads):
            rd_ref[head : head + 1, :] = jnp.sum(prod[64 * head : 64 * head + 64, :], axis=0, keepdims=True)


def hidden_block(mes, info, part, position):
    return 4 * part + (position ^ (info[mes + part] >> 3))


def feed_forward(mes, info, outs, stats, branch, out_proj, gain, cot, w_gate_up, w_down, units):
    rows, width = branch.shape
    hidden = w_down.shape[0]
    chunk = 256
    steps = hidden // chunk
    blocks = len(outs)
    heads = width // 64
    once = lambda shape: pl.BlockSpec(shape, lambda *_: (0,) * len(shape), pipeline_mode=pl.Buffered(1))
    nat = (rows, width)

    def block(i, info):
        return hidden_block(mes, info, i // 4, (i % 4) ^ 2)

    piece = jax.ShapeDtypeStruct((16, 384, 128), LOW)
    return pl.pallas_call(
        functools.partial(ffn_kernel, blocks, units, mes),
        out_shape=[jax.ShapeDtypeStruct(s.shape, F32) for s in stats]
        + [
            jax.ShapeDtypeStruct(nat, LOW),
            jax.ShapeDtypeStruct(nat, F32),
            jax.ShapeDtypeStruct((width, rows), LOW),
            jax.ShapeDtypeStruct((heads, rows), F32),
            jax.ShapeDtypeStruct((width, width), LOW),
            jax.ShapeDtypeStruct((8, width), F32),
        ]
        + [piece] * 4,
        grid_spec=pltpu.PrefetchScalarGridSpec(
            num_scalar_prefetch=1,
            grid=(steps,),
            in_specs=[once(o.shape) for o in outs]
            + [once(s.shape) for s in stats]
            + [
                once(nat),
                once((width, width)),
                once((1, width)),
                once(nat),
                pl.BlockSpec((width, chunk), lambda i, info: (0, block(i, info))),
                pl.BlockSpec((width, chunk), lambda i, info: (0, block(i, info) + steps)),
                pl.BlockSpec((chunk, width), lambda i, info: (block(i, info), 0)),
            ],
            out_specs=[once(s.shape) for s in stats]
            + [
                once(nat),
                once(nat),
                once((width, rows)),
                once((heads, rows)),
                once((width, width)),
                once((8, width)),
            ]
            + [
                pl.BlockSpec((8, 384, 128), lambda i, info, j=j: (jnp.clip(i - 2 * j, 0, 1), 0, 0))
                for j in range(4)
            ],
            scratch_shapes=[
                pltpu.VMEM((width, rows), F32),
                pltpu.VMEM((width, rows), LOW),
                pltpu.VMEM(nat, F32),
                pltpu.VMEM(nat, LOW),
                pltpu.VMEM((width, rows), LOW),
                pltpu.VMEM(nat, F32),
                pltpu.VMEM(nat, F32),
            ],
        ),
        compiler_params=params(),
        cost_estimate=cost(35),
        name="feed_forward",
    )(info, *outs, *stats, branch, out_proj, gain, cot, w_gate_up, w_gate_up, w_down)


def back_other_kernel(pairs, *refs):
    dks, dvs = refs[:pairs], refs[pairs : 2 * pairs]
    n_ref, w_ref, dn_ref, dw_ref = refs[2 * pairs :]
    width = n_ref.shape[1]
    both = jnp.concatenate([r[...] for r in dks + dvs], axis=1)
    dn_ref[...] = dot_nt(both, w_ref[:, width:]).astype(LOW)
    part = dot(n_ref[...].T, both)

    @pl.when(pl.program_id(0) == 0)
    def _():
        dw_ref[...] = part

    @pl.when(pl.program_id(0) > 0)
    def _():
        dw_ref[...] += part


def back_other(dks, dvs, normed, w_qkv):
    rows, width = normed.shape
    tile = min(256, rows)
    nat = pl.BlockSpec((tile, width), lambda i: (i, 0))
    narrow = pl.BlockSpec((tile, 128), lambda i: (i, 0))
    return pl.pallas_call(
        functools.partial(back_other_kernel, len(dks)),
        grid=(rows // tile,),
        out_shape=[jax.ShapeDtypeStruct((rows, width), LOW), jax.ShapeDtypeStruct((width, 2 * width), F32)],
        in_specs=[narrow] * (2 * len(dks)) + [nat, full(w_qkv.shape)],
        out_specs=[nat, full((width, 2 * width))],
        compiler_params=params(),
        cost_estimate=cost(5),
        name="back_other",
    )(*dks, *dvs, normed, w_qkv)


def pack(out, at, value, me):
    rows = value.shape[0] // 32
    for g in range(32):
        for lane in range(value.shape[1] // 128):
            start = at + lane * rows
            out[g ^ me, start : start + rows, :] = value[g * rows : (g + 1) * rows, lane * 128 : (lane + 1) * 128]


def grad_qkv_kernel(mes, ring, pairs, info, *refs):
    count = ring * pairs
    dqs, dks, dvs = refs[:count], refs[count : count + pairs], refs[count + pairs : count + 2 * pairs]
    n_ref, dwkv_ref, dwo_ref, dqkv_ref, early, late, packed = refs[count + 2 * pairs :]
    width = n_ref.shape[1]
    me = info[mes]
    rows = []
    for pair in range(pairs):
        terms = [dqs[k * pairs + pair][...] for k in range(ring)]
        rows.append(functools.reduce(jnp.add, terms) * 0.125)
    dq = jnp.concatenate(rows, axis=0).astype(LOW).T
    dqkv = jnp.concatenate([dq] + [r[...] for r in dks + dvs], axis=1)
    dqkv_ref[...] = dqkv
    dw = dot(n_ref[...].T, dqkv)
    pack(packed, 0, dw[:, :width].astype(LOW), me)
    pack(packed, width // 8, (dw[:, width:] + dwkv_ref[...]).astype(LOW), me)
    pack(packed, 3 * width // 8, dwo_ref[...], me)
    early[...] = packed[16:]
    late[...] = packed[:16]


def grad_qkv(mes, info, dqs, dks, dvs, normed, dw_kv, dwo):
    rows, width = normed.shape
    pairs = len(dks)
    operands = (*dqs, *dks, *dvs, normed, dw_kv, dwo)
    outs = [jax.ShapeDtypeStruct((rows, 3 * width), LOW)] + [jax.ShapeDtypeStruct((16, width // 2, 128), LOW)] * 2
    return pl.pallas_call(
        functools.partial(grad_qkv_kernel, mes, len(dqs) // pairs, pairs),
        out_shape=outs,
        grid_spec=pltpu.PrefetchScalarGridSpec(
            num_scalar_prefetch=1,
            grid=(1,),
            in_specs=[full(o.shape) for o in operands],
            out_specs=[full(o.shape) for o in outs],
            scratch_shapes=[pltpu.VMEM((32, width // 2, 128), LOW)],
        ),
        compiler_params=params(),
        cost_estimate=cost(7),
        name="grad_qkv",
    )(info, *operands)


def finish_kernel(mes, parts_count, few, info, *refs):
    parts, gbs = refs[:parts_count], refs[parts_count : parts_count + few]
    dqkv_ref, branch_ref, gain_ref, datt_ref, mixed_ref, conv_ref, w_ref, kernels_ref, ids_ref, x_ref, halo_ref, dgain_ref = refs[
        parts_count + few : parts_count + few + 12
    ]
    gx_ref, ret_ref, early, late, ext, edge, masks, small, packed = refs[parts_count + few + 12 :]
    rows, width = branch_ref.shape
    me = info[mes]
    taps = make_taps(kernels_ref[...])
    dn = dot_nt(dqkv_ref[...], w_ref[...])
    for part in parts:
        dn = dn + part[...].astype(F32)
    back, dgain = norm_back(branch_ref[...], gain_ref[...].astype(F32), dn)
    dbranch = datt_ref[...] + back
    dbranch_low = dbranch.astype(LOW)
    pack(packed, 0, dot(mixed_ref[...].T, dbranch_low).astype(LOW), me)
    dmixed = dot_nt(dbranch_low, conv_ref[...])
    masks[...] = same_words(ids_ref[...])
    same = masks[:, pl.ds(pl.multiple_of(info[0], 128), rows)].T
    ext[0:8, :] = halo_ref[...].astype(F32)
    ext[8:, :] = x_ref[...].astype(F32)
    edge[0:8, :] = jnp.zeros((8, width), F32)
    edge[8 + rows :, :] = jnp.zeros((8, width), F32)
    small[4:5, :] = dgain
    small[5:6, :] = dgain_ref[0:1, :]
    small[6:8, :] = jnp.zeros((2, width), F32)
    grad = dbranch + taps[0] * dmixed
    small[0:1, :] = jnp.sum(dmixed * ext[8:, :], axis=0, keepdims=True)
    returned = jnp.zeros((8, width), F32)
    for back_by in range(1, 4):
        masked = dmixed * same[:, back_by : back_by + 1]
        small[back_by : back_by + 1, :] = jnp.sum(masked * ext[8 - back_by : 8 - back_by + rows, :], axis=0, keepdims=True)
        edge[8 : 8 + rows, :] = masked
        grad = grad + taps[back_by] * edge[8 + back_by : 8 + back_by + rows, :]
        returned = returned + taps[back_by] * edge[back_by : back_by + 8, :]
    gx_ref[...] = grad
    ret_ref[...] = returned
    gb = functools.reduce(jnp.add, [r[...] for r in gbs])
    for g in range(32):
        lane = 128 * (g % 4)
        line = jnp.concatenate(
            [small[g // 4 : g // 4 + 1, lane : lane + 128], gb[g : g + 1, :], jnp.zeros((14, 128), F32)], axis=0
        )
        packed[g ^ me, width // 8 : width // 8 + 16, :] = line.astype(LOW)
    early[...] = packed[16:]
    late[...] = packed[:16]


def finish(mes, info, parts, gbs, dqkv, branch, gain, datt, mixed, conv_proj, w_qkv, kernels, ids, x, halo, dgain):
    rows, width = branch.shape
    operands = (*parts, *gbs, dqkv, branch, gain, datt, mixed, conv_proj, w_qkv, kernels, ids, x, halo, dgain)
    depth = width // 8 + 16
    outs = [
        jax.ShapeDtypeStruct((rows, width), F32),
        jax.ShapeDtypeStruct((8, width), F32),
    ] + [jax.ShapeDtypeStruct((16, depth, 128), LOW)] * 2
    return pl.pallas_call(
        functools.partial(finish_kernel, mes, len(parts), len(gbs)),
        out_shape=outs,
        grid_spec=pltpu.PrefetchScalarGridSpec(
            num_scalar_prefetch=1,
            grid=(1,),
            in_specs=[full(o.shape) for o in operands],
            out_specs=[full(o.shape) for o in outs],
            scratch_shapes=[
                pltpu.VMEM((rows + 8, width), F32),
                pltpu.VMEM((rows + 16, width), F32),
                pltpu.VMEM((8, ids.shape[1]), F32),
                pltpu.VMEM((8, width), F32),
                pltpu.VMEM((32, depth, 128), LOW),
            ],
        ),
        compiler_params=params(),
        cost_estimate=cost(12),
        name="finish",
    )(info, *operands)


def spread_ffn_kernel(mes, info, own_a, other_a, own_b, other_b, gate_up_ref, down_ref):
    part, position, which = pl.program_id(0), pl.program_id(1), pl.program_id(2)
    sources = (own_a, other_a, own_b, other_b)
    for j, source in enumerate(sources):

        @pl.when((part == j // 2) & (position // 2 == j % 2))
        def _(j=j, source=source):
            turn = info[mes + j // 2] & 7
            for k in range(8):
                col, row = 128 * (k // 4), 128 * (k % 4)
                spot = k ^ turn
                gate_up_ref[row : row + 128, col : col + 128] = source[
                    spot, pl.ds(pl.multiple_of(which * 128, 128), 128), :
                ].astype(F32)
                down_ref[col : col + 128, row : row + 128] = source[spot, 256:384, :].astype(F32)


def spread_ffn(mes, info, own_a, other_a, own_b, other_b, width, hidden):
    steps = hidden // 256

    def source(j):
        def index(part, position, which, info):
            here = jnp.clip(position - 2 * (j % 2), 0, 1)
            return (jnp.where(part == j // 2, here, 1 - j // 2), 0, 0)

        return pl.BlockSpec((8, 384, 128), index)

    return pl.pallas_call(
        functools.partial(spread_ffn_kernel, mes),
        out_shape=[jax.ShapeDtypeStruct((width, 2 * hidden), F32), jax.ShapeDtypeStruct((hidden, width), F32)],
        grid_spec=pltpu.PrefetchScalarGridSpec(
            num_scalar_prefetch=1,
            grid=(2, 4, 2),
            in_specs=[source(j) for j in range(4)],
            out_specs=[
                pl.BlockSpec(
                    (width, 256), lambda p, q, w, info: (0, w * steps + hidden_block(mes, info, p, q))
                ),
                pl.BlockSpec((256, width), lambda p, q, w, info: (hidden_block(mes, info, p, q), 0)),
            ],
        ),
        compiler_params=params(),
        cost_estimate=cost(7),
        name="spread_ffn",
    )(info, own_a, other_a, own_b, other_b)


def spread_kernel(mes, widths, info, own, other, *outs):
    step = pl.program_id(0)
    turn = info[mes] & 7
    for j, source in enumerate((own, other)):

        @pl.when(step // 2 == j)
        def _(source=source):
            for k in range(8):
                spot = k ^ turn
                at = 0
                for out, columns in zip(outs, widths):
                    for lane in range(columns // 128):
                        out[16 * k : 16 * k + 16, 128 * lane : 128 * lane + 128] = source[
                            spot, at : at + 16, :
                        ].astype(F32)
                        at += 16


def spread(mes, info, own, other, widths):
    depth = own.shape[1]

    def source(j):
        return pl.BlockSpec((8, depth, 128), lambda i, info: (jnp.clip(i - 2 * j, 0, 1), 0, 0))

    return pl.pallas_call(
        functools.partial(spread_kernel, mes, widths),
        out_shape=[jax.ShapeDtypeStruct((512, c), F32) for c in widths],
        grid_spec=pltpu.PrefetchScalarGridSpec(
            num_scalar_prefetch=1,
            grid=(4,),
            in_specs=[source(0), source(1)],
            out_specs=[
                pl.BlockSpec((128, c), lambda i, info: (i ^ (info[mes] >> 3), 0)) for c in widths
            ],
        ),
        compiler_params=params(),
        cost_estimate=cost(4),
        name="spread",
    )(info, own, other)


def hop_order(sizes, first):
    seq = [("seq", 1 << b) for b in range(sizes["seq"].bit_length() - 1)]
    dp = [("dp", 1 << b) for b in range(1, sizes["dp"].bit_length() - 1)]
    hops = seq + dp if first == "seq" else dp[:1] + seq + dp[1:]
    return [("dp", 1)] + hops


def place_of(order):
    me = jnp.int32(0)
    for axis, bit in order[:5]:
        me = me * 2 + (lax.axis_index(axis) // bit) % 2
    return me


def swap(value, hop):
    axis, bit = hop
    return lax.ppermute(value, axis, [(i, i ^ bit) for i in range(lax.axis_size(axis))])


def added(a, b):
    return (a.astype(F32) + b.astype(F32)).astype(LOW)


class Sum:
    def __init__(self, order, early, late):
        self.order = order
        self.value = late
        self.flight = swap(early, order[0])
        self.stage = 0
        self.other = None

    def advance(self):
        if self.other is not None:
            return
        hops = self.order[5:]
        self.stage += 1
        stage = self.stage
        if stage < 5 + len(hops) + 1:
            self.value = added(self.value, self.flight)
        else:
            self.value = jnp.concatenate([self.value, self.flight], axis=0)
        if stage < 5:
            half = self.value.shape[0] // 2
            self.flight = swap(self.value[half:], self.order[stage])
            self.value = self.value[:half]
        elif stage < 5 + len(hops):
            self.flight = swap(self.value, hops[stage - 5])
        else:
            left = 4 - (stage - 5 - len(hops))
            self.flight = swap(self.value, self.order[left])
            if left == 0:
                self.other = self.flight

    def finish(self):
        while self.other is None:
            self.advance()
        return self.value, self.other


def total(terms):
    if len(terms) == 1:
        return terms[0]
    return functools.reduce(jnp.add, [t.astype(F32) for t in terms]).astype(terms[0].dtype)


def before(value, sums):
    for running in sums:
        running.advance()
    tied = lax.optimization_barrier((value,) + tuple(r.value for r in sums if r.other is None))
    at = 1
    for running in sums:
        if running.other is None:
            running.value = tied[at]
            at += 1
    return tied[0]


def shards(sizes, tokens, word_ids, cotangent, conv_kernels, conv_proj, gain_attn, w_qkv, rel_bias, out_proj, gain_ffn, w_gate_up, w_down):
    seqs, rows, width = tokens.shape
    heads = rel_bias.shape[1]
    pairs = heads // 2
    ring = sizes["seq"]
    me = lax.axis_index("seq")
    order_a, order_b = hop_order(sizes, "seq"), hop_order(sizes, "dp")
    info = jnp.stack(
        [((me + k) % ring) * rows for k in range(ring)] + [place_of(order_a), place_of(order_b)]
    ).astype(jnp.int32)
    mes = ring
    gain_one = gain_attn[None, :]
    gain_two = gain_ffn[None, :]
    halo = lax.ppermute(tokens[:, rows - 8 :, :], "seq", [(i, (i + 1) % ring) for i in range(ring)])
    halo, travelling = lax.optimization_barrier((halo, tokens))
    block_tokens = [tokens] + [
        lax.ppermute(travelling, "seq", [((i + k) % ring, i) for i in range(ring)]) for k in range(1, ring)
    ]
    halos = [halo] + [b[:, rows - 8 :, :] for b in block_tokens[:-1]]
    units = rows // unit_of(rows)

    parts_of = []
    for s in range(seqs):
        ids = word_ids[s : s + 1]
        own = project(True, 0, info, tokens[s], halos[0][s], ids, conv_kernels, conv_proj, gain_one, w_qkv)
        branch, mixed, normed, query, query_t, key, key_t, value, value_t = own
        held = [(normed, key, key_t, value, value_t)]
        fwd = [attend(0, ids, info, rel_bias, key, value_t, query_t)]
        for k in range(1, ring):
            held.append(
                project(False, k, info, block_tokens[k][s], halos[k][s], ids, conv_kernels, conv_proj, gain_one, w_qkv)
            )
            fwd.append(attend(k, ids, info, rel_bias, held[k][1], held[k][4], query_t))
        ffn = feed_forward(
            mes, info, [f[1] for f in fwd], [f[2] for f in fwd], branch, out_proj, gain_two, cotangent[s], w_gate_up, w_down, units
        )
        parts_of.append((ids, held, fwd, query, branch, mixed, ffn))

    pieces = [total([p[-1][ring + 6 + j] for p in parts_of]) for j in range(4)]
    sum_a = Sum(order_a, pieces[0], pieces[1])
    sum_b = Sum(order_b, pieces[2], pieces[3])
    plan = {1: True, 4: True, 6: True, 7: True, 8: True, 9: True, 10: True}
    slot = 0

    results, gxs, rets, qkv_pieces, conv_pieces = [], [], [], [], []
    for s in range(seqs):
        ids, held, fwd, query, branch, mixed, ffn = parts_of[s]
        scales = ffn[:ring]
        result, datt, dout_t, rowdot, dwo, dgain = ffn[ring : ring + 6]
        results.append(result)
        dqs, parts, dw_kvs, gbs = [None] * ring, [], [], []
        for k in list(range(1, ring)) + [0]:
            backs = []
            for pair in range(pairs):
                go = rowdot
                if slot in plan:
                    go = before(rowdot, [sum_a, sum_b])
                slot += 1
                backs.append(
                    attend_back(k, pair, ids, info, fwd[k][0], held[k][2], held[k][3], query, dout_t, scales[k], go)
                )
            dqs[k] = [b[0] for b in backs]
            dks, dvs = [b[1] for b in backs], [b[2] for b in backs]
            gbs += [b[3] for b in backs]
            if k > 0:
                last = dvs[-1]
                if slot in plan:
                    last = before(last, [sum_a, sum_b])
                slot += 1
                dn, dw_kv = back_other(dks, dvs[:-1] + [last], held[k][0], w_qkv)
                parts.append(lax.ppermute(dn, "seq", [(i, (i + k) % ring) for i in range(ring)]))
                dw_kvs.append(dw_kv)
        dw_kv = total(dw_kvs) if dw_kvs else jnp.zeros((width, 2 * width), F32)
        if slot in plan:
            dwo = before(dwo, [sum_a, sum_b])
        slot += 1
        dqkv, early, late = grad_qkv(mes, info, sum(dqs, []), dks, dvs, held[0][0], dw_kv, dwo)
        qkv_pieces.append((early, late))
        if slot in plan:
            dqkv = before(dqkv, [sum_a, sum_b])
        slot += 1
        gx, ret, early, late = finish(
            mes + 1, info, parts, gbs, dqkv, branch, gain_one, datt, mixed, conv_proj, w_qkv, conv_kernels,
            ids, tokens[s], halos[0][s], dgain,
        )
        gxs.append(gx)
        rets.append(ret)
        conv_pieces.append((early, late))

    sum_c = Sum(order_a, *[total([p[j] for p in qkv_pieces]) for j in range(2)])
    sum_d = Sum(order_b, *[total([p[j] for p in conv_pieces]) for j in range(2)])
    hidden = w_down.shape[0]
    grad_gate_up, grad_down = spread_ffn(mes, info, *sum_a.finish(), *sum_b.finish(), width, hidden)
    grad_w_qkv, grad_out_proj = spread(mes, info, *sum_c.finish(), (3 * width, width))
    grad_conv_proj, few = spread(mes + 1, info, *sum_d.finish(), (width, 128))
    few = few.reshape(32, 16, 128)
    g = few[:, 0, :].reshape(8, width)
    grad_kernels = jnp.stack([g[0], g[1], g[0], g[1], g[2], g[0], g[1], g[2], g[3]])
    returned = lax.ppermute(jnp.stack(rets), "seq", [(i, i - 1) for i in range(1, ring)])
    grad_tokens = jnp.stack(gxs)
    grad_tokens = grad_tokens.at[:, rows - 8 :, :].add(returned)
    return (
        jnp.stack(results),
        grad_tokens,
        grad_kernels,
        grad_conv_proj,
        g[4],
        grad_w_qkv,
        few[:, 1, :heads],
        grad_out_proj,
        g[5],
        grad_gate_up,
        grad_down,
    )


def solution(mesh):
    sizes = dict(mesh.shape)
    split = P("dp", "seq", None)
    in_specs = (split, P("dp", None), split) + (P(),) * 9
    out_specs = (split, split) + (P(),) * 9
    return jax.shard_map(
        functools.partial(shards, sizes), mesh=mesh, in_specs=in_specs, out_specs=out_specs, check_vma=False
    )
```

```python
import functools

import jax
import jax.numpy as jnp
from jax import lax
from jax.experimental import pallas as pl
from jax.experimental.pallas import tpu as pltpu
from jax.sharding import PartitionSpec as P

EVERY = ("seq", "dp")
LOW = jnp.bfloat16
F32 = jnp.float32
EDGES = (1, 2, 3, 4, 5, 6, 7, 8, 11, 16, 22, 32, 45, 64, 91)
KEY_WORDS = 128
QUERY_WORDS = 256
FOLD = 512
VMEM_BYTES = 60 * 2**20


def bucketize(offsets):
    magnitude = jnp.abs(offsets)
    bucketed = jnp.where(offsets > 0, 16, 0).astype(jnp.int32)
    for edge in EDGES:
        bucketed = bucketed + (magnitude >= edge).astype(jnp.int32)
    return bucketed


def dot(a, b):
    return jnp.dot(a, b, preferred_element_type=F32)


def dot_nt(a, b):
    return lax.dot_general(a, b, (((1,), (1,)), ((), ())), preferred_element_type=F32)


def iota(shape, dim):
    return lax.broadcasted_iota(jnp.int32, shape, dim)


def onehot(mask):
    return mask.astype(F32).astype(LOW)


def params(**kw):
    return pltpu.CompilerParams(vmem_limit_bytes=VMEM_BYTES, **kw)


def cost(micros):
    return pl.CostEstimate(flops=int(micros * 1e9), bytes_accessed=int(micros * 1e6), transcendentals=0)


def full(shape):
    return pl.BlockSpec(shape, lambda *_: (0,) * len(shape))


def make_taps(kernels):
    k = kernels.astype(F32)
    return [
        k[0:1] + k[2:3] + k[5:6],
        k[1:2] + k[3:4] + k[6:7],
        k[4:5] + k[7:8],
        k[8:9],
    ]


def same_words(ids):
    place = iota(ids.shape, 1)
    rows = [
        jnp.where((pltpu.roll(ids, back, 1) == ids) & (place >= back), 1.0, 0.0) for back in range(1, 4)
    ]
    return jnp.concatenate([jnp.zeros(ids.shape, F32)] + rows + [jnp.zeros((4, ids.shape[1]), F32)], axis=0)


def project_kernel(own, at, info, x_ref, halo_ref, ids_ref, kernels_ref, gain_ref, conv_ref, w_ref, *rest):
    step = pl.program_id(0)
    tile = rest[0].shape[0]
    ext, masks = rest[-2:]
    width = x_ref.shape[1]

    @pl.when(step == 0)
    def _():
        ext[0:8, :] = halo_ref[...].astype(F32)
        ext[8:, :] = x_ref[...].astype(F32)
        masks[...] = same_words(ids_ref[...])

    start = pl.multiple_of(step * tile, tile)
    chunk = ext[pl.ds(start, tile + 8), :]
    lane = pl.multiple_of(info[at] + step * tile, tile)
    same = masks[:, pl.ds(lane, tile)].T
    taps = make_taps(kernels_ref[...])
    inputs = chunk[8:, :]
    mixed = taps[0] * inputs
    for back in range(1, 4):
        mixed = mixed + taps[back] * chunk[8 - back : 8 - back + tile, :] * same[:, back : back + 1]
    mixed_low = mixed.astype(LOW)
    branch = inputs + dot(mixed_low, conv_ref[...])
    factor = lax.rsqrt(jnp.mean(branch * branch, axis=-1, keepdims=True) + 1e-06)
    normed = (branch * factor * gain_ref[...].astype(F32)).astype(LOW)
    if own:
        branch_ref, mixed_ref, n_ref, q_ref, qt_ref, k_ref, kt_ref, v_ref, vt_ref = rest[:-2]
        qkv = dot(normed, w_ref[...]).astype(LOW)
        query = qkv[:, :width] * jnp.asarray(0.125, LOW)
        q_ref[...] = query
        qt_ref[...] = query.T
        branch_ref[...] = branch
        mixed_ref[...] = mixed_low
        key, value = qkv[:, width : 2 * width], qkv[:, 2 * width :]
    else:
        n_ref, k_ref, kt_ref, v_ref, vt_ref = rest[:-2]
        kv = dot(normed, w_ref[:, width:]).astype(LOW)
        key, value = kv[:, :width], kv[:, width:]
    n_ref[...] = normed
    k_ref[...] = key
    kt_ref[...] = key.T
    v_ref[...] = value
    vt_ref[...] = value.T


def project(own, at, info, x, halo, ids, kernels, gain, conv_proj, w_qkv):
    rows, width = x.shape
    tile = min(256, rows)
    nat = pl.BlockSpec((tile, width), lambda i, *_: (i, 0))
    tra = pl.BlockSpec((width, tile), lambda i, *_: (0, i))
    nat_low = jax.ShapeDtypeStruct((rows, width), LOW)
    tra_low = jax.ShapeDtypeStruct((width, rows), LOW)
    nat_f32 = jax.ShapeDtypeStruct((rows, width), F32)
    if own:
        outs = [(nat_f32, nat), (nat_low, nat), (nat_low, nat), (nat_low, nat), (tra_low, tra)]
    else:
        outs = [(nat_low, nat)]
    outs = outs + [(nat_low, nat), (tra_low, tra), (nat_low, nat), (tra_low, tra)]
    operands = (x, halo, ids, kernels, gain, conv_proj, w_qkv)
    return pl.pallas_call(
        functools.partial(project_kernel, own, at),
        out_shape=[s for s, _ in outs],
        grid_spec=pltpu.PrefetchScalarGridSpec(
            num_scalar_prefetch=1,
            grid=(rows // tile,),
            in_specs=[full(o.shape) for o in operands],
            out_specs=[b for _, b in outs],
            scratch_shapes=[pltpu.VMEM((rows + 8, width), F32), pltpu.VMEM((8, ids.shape[1]), F32)],
        ),
        compiler_params=params(),
        cost_estimate=cost(8 if own else 6),
        name="project_own" if own else "project_other",
    )(info, *operands)


def word_spans(ids, q_off, k_off, rows_q, rows_k, unit):
    q_first = ids[0, q_off]
    q_wins = (ids[0, q_off + rows_q - 1] - q_first) // QUERY_WORDS + 1
    firsts, wins = [], []
    for at in range(0, rows_k, unit):
        first = ids[0, k_off + at]
        firsts.append(first)
        wins.append((ids[0, k_off + at + unit - 1] - first) // KEY_WORDS + 1)
    fits = q_wins == 1
    for count in wins:
        fits = jnp.logical_and(fits, count == 1)
    return q_first, q_wins, firsts, wins, fits


def unit_of(rows_k):
    return min(512, rows_k)


def stat_rows(rows_k):
    return -(-(2 * (rows_k // unit_of(rows_k)) + 4) // 8) * 8


def attend_kernel(rows_q, rows_k, spot, ids, info, ids_ref, bias_ref, k_ref, vt_ref, qt_ref, p_ref, o_ref, stat_ref, eqt, ek, bidx, raw, tab_ref, parts, flag):
    pair = pl.program_id(0)
    unit = unit_of(rows_k)
    units = rows_k // unit
    q_off, k_off = info[0], info[spot]
    q_first, q_wins, firsts, wins, fits = word_spans(ids, q_off, k_off, rows_q, rows_k, unit)
    q_ids = ids_ref[:, pl.ds(pl.multiple_of(q_off, 128), rows_q)]

    def unit_ids(at):
        return ids_ref[:, pl.ds(pl.multiple_of(k_off + at * unit, 128), unit)]

    def query_words(win):
        return onehot(iota((QUERY_WORDS, rows_q), 0) + (q_first + win * QUERY_WORDS) == q_ids)

    def key_words(at, win):
        return onehot(iota((KEY_WORDS, unit), 0) + (firsts[at] + win * KEY_WORDS) == unit_ids(at)).T

    def buckets(at, win, q_win):
        shift = firsts[at] + win * KEY_WORDS - q_first - q_win * QUERY_WORDS
        shape = (KEY_WORDS, QUERY_WORDS)
        return bucketize(shift + iota(shape, 0) - iota(shape, 1))

    def window_bias(head, index):
        row = jnp.broadcast_to(tab_ref[pl.ds(head, 1), :], (KEY_WORDS, 128))
        parts = [
            jnp.take_along_axis(row, index[:, c : c + 128], axis=1) for c in range(0, QUERY_WORDS, 128)
        ]
        return jnp.concatenate(parts, axis=1).astype(LOW)

    @pl.when(pair == 0)
    def _():
        eqt[...] = query_words(0)
        tab_ref[:, : bias_ref.shape[0]] = bias_ref[...].astype(F32).T
        for at in range(units):
            ek[at * unit : (at + 1) * unit, :] = key_words(at, 0)
            bidx[at] = buckets(at, 0, 0)

    def queries(side):
        zero = jnp.zeros((64, rows_q), LOW)
        mine = qt_ref[64 * side : 64 * side + 64, :]
        return [mine, zero] if side == 0 else [zero, mine]

    def fast_scores(side, at):
        rows = slice(at * unit, (at + 1) * unit)
        bias = window_bias(2 * pair + side, bidx[at])
        spread = dot(bias, eqt[...]).astype(LOW)
        right = jnp.concatenate(queries(side) + [spread], axis=0)
        left = jnp.concatenate([k_ref[rows, :], ek[rows, :]], axis=1)
        return dot(left, right)

    def slow_scores(side, at):
        rows = slice(at * unit, (at + 1) * unit)
        raw[...] = dot(k_ref[rows, :], jnp.concatenate(queries(side), axis=0))

        def over_keys(win, carry):
            def over_queries(q_win, inner):
                bias = window_bias(2 * pair + side, buckets(at, win, q_win))
                spread = dot(bias, query_words(q_win)).astype(LOW)
                raw[...] += dot(key_words(at, win), spread)
                return inner

            return lax.fori_loop(0, q_wins, over_queries, carry)

        lax.fori_loop(0, wins[at], over_keys, 0)
        return raw[...]

    jobs = [(side, at) for side in range(2) for at in range(units)]

    def softmax_part(job, score):
        side, at = job
        rows = slice(at * unit, (at + 1) * unit)
        top = jnp.max(score, axis=0, keepdims=True)
        expo = jnp.exp(score - top).astype(LOW)
        p_ref[side, rows, :] = expo
        left = jnp.concatenate([vt_ref[64 * side : 64 * side + 64, rows], jnp.ones((16, unit), LOW)], axis=0)
        parts[side * units + at] = dot(left, expo)
        stat_ref[0, side * units + at : side * units + at + 1, :] = top

    def merge():
        for side in range(2):
            tops = [stat_ref[0, side * units + at : side * units + at + 1, :] for at in range(units)]
            peak = functools.reduce(jnp.maximum, tops)
            total = functools.reduce(
                jnp.add, [parts[side * units + at] * jnp.exp(tops[at] - peak) for at in range(units)]
            )
            o_ref[64 * side : 64 * side + 64, :] = total[:64, :]
            stat_ref[0, 2 * units + side : 2 * units + side + 1, :] = peak
            stat_ref[0, 2 * units + 2 + side : 2 * units + 3 + side, :] = total[64:65, :]

    def run_fast():
        stat_ref[...] = jnp.zeros_like(stat_ref)
        least = most = None
        for side, at in jobs:
            rows = slice(at * unit, (at + 1) * unit)
            expo = jnp.exp(fast_scores(side, at)).astype(LOW)
            p_ref[side, rows, :] = expo
            left = jnp.concatenate([vt_ref[64 * side : 64 * side + 64, rows], jnp.ones((16, unit), LOW)], axis=0)
            part = dot(left, expo)
            parts[side * units + at] = part
            sums = part[64:65, :]
            least = sums if least is None else jnp.minimum(least, sums)
            most = sums if most is None else jnp.maximum(most, sums)
        return jnp.logical_and(jnp.min(least) > 1e-25, jnp.max(most) < 1e25)

    def run_slow():
        for job in jobs:
            softmax_part(job, slow_scores(*job))

    flag[0] = 0

    @pl.when(fits)
    def _():
        flag[0] = run_fast().astype(jnp.int32)

    @pl.when(flag[0] == 0)
    def _():
        run_slow()

    merge()


def attend(spot, ids, info, rel_bias, key, value_t, query_t):
    rows_k, width = key.shape
    rows_q = query_t.shape[1]
    length = ids.shape[1]
    unit = unit_of(rows_k)
    units = rows_k // unit
    stats = stat_rows(rows_k)
    pairs = width // 128
    return pl.pallas_call(
        functools.partial(attend_kernel, rows_q, rows_k, spot),
        out_shape=[
            jax.ShapeDtypeStruct((2 * pairs, rows_k, rows_q), LOW),
            jax.ShapeDtypeStruct((width, rows_q), F32),
            jax.ShapeDtypeStruct((pairs, stats, rows_q), F32),
        ],
        grid_spec=pltpu.PrefetchScalarGridSpec(
            num_scalar_prefetch=2,
            grid=(pairs,),
            in_specs=[
                full((1, length)),
                full(rel_bias.shape),
                pl.BlockSpec((rows_k, 128), lambda p, *_: (0, p)),
                pl.BlockSpec((128, rows_k), lambda p, *_: (p, 0)),
                pl.BlockSpec((128, rows_q), lambda p, *_: (p, 0)),
            ],
            out_specs=[
                pl.BlockSpec((2, rows_k, rows_q), lambda p, *_: (p, 0, 0)),
                pl.BlockSpec((128, rows_q), lambda p, *_: (p, 0)),
                pl.BlockSpec((1, stats, rows_q), lambda p, *_: (p, 0, 0)),
            ],
            scratch_shapes=[
                pltpu.VMEM((QUERY_WORDS, rows_q), LOW),
                pltpu.VMEM((rows_k, KEY_WORDS), LOW),
                pltpu.VMEM((units, KEY_WORDS, QUERY_WORDS), jnp.int32),
                pltpu.VMEM((unit, rows_q), F32),
                pltpu.VMEM((2 * pairs, 128), F32),
                pltpu.VMEM((2 * units, 80, rows_q), F32),
                pltpu.SMEM((1,), jnp.int32),
            ],
        ),
        compiler_params=params(),
        cost_estimate=cost(20),
        name="attend",
    )(ids, info, ids, rel_bias, key, value_t, query_t)


def attend_back_kernel(rows_q, rows_k, spot, first_pair, last, ids, info, ids_ref, p_ref, kt_ref, v_ref, q_ref, dot_ref, cs_ref, rd_ref, *rest):
    if last:
        so_far_ref, rest = rest[0], rest[1:]
    dq_ref, dk_ref, dv_ref, gb_ref, eq, ekt, bmask, spread, held, by_word = rest[:10]
    dq_acc = rest[10] if last else dq_ref
    at = pl.program_id(1)
    pair = first_pair + pl.program_id(0)
    unit = unit_of(rows_k)
    units = rows_k // unit
    q_off, k_off = info[0], info[spot]
    q_first = ids[0, q_off]
    q_wins = (ids[0, q_off + rows_q - 1] - q_first) // QUERY_WORDS + 1
    q_ids = ids_ref[:, pl.ds(pl.multiple_of(q_off, 128), rows_q)]

    def query_words(win):
        return onehot(iota((QUERY_WORDS, rows_q), 0) + (q_first + win * QUERY_WORDS) == q_ids).T

    def first_word(index):
        return ids[0, k_off + index * unit]

    def key_words(index, win):
        k_ids = ids_ref[:, pl.ds(pl.multiple_of(k_off + index * unit, 128), unit)]
        return onehot(iota((KEY_WORDS, unit), 0) + (first_word(index) + win * KEY_WORDS) == k_ids)

    def bucket_mask(index, win, q_win):
        lane = iota((32, FOLD), 1)
        ahead = jnp.where(lane < FOLD - KEY_WORDS, lane, lane - FOLD)
        shift = first_word(index) + win * KEY_WORDS - q_first - q_win * QUERY_WORDS
        return (bucketize(shift - ahead) == iota((32, FOLD), 0)).astype(F32)

    @pl.when(jnp.logical_and(at == 0, pl.program_id(0) == 0))
    def _():
        eq[...] = query_words(0)
        gb_ref[...] = jnp.zeros_like(gb_ref)
        spread[...] = jnp.zeros_like(spread)
        for index in range(units):
            ekt[index] = key_words(index, 0)
            bmask[index] = bucket_mask(index, 0, 0)

    def fold(grids, mask, heads):
        half = KEY_WORDS // 2
        while half >= 8:
            grids = [g[:half, :] + pltpu.roll(g[half:, :], FOLD - half, 1) for g in grids]
            half //= 2
        row = iota((8, FOLD), 0)
        for bit in (4, 2, 1):
            grids = [jnp.where((row & bit) != 0, pltpu.roll(g, FOLD - bit, 1), g) for g in grids]
        sums = [jnp.sum(mask * jnp.sum(g, axis=0, keepdims=True), axis=1, keepdims=True) for g in grids]
        place = iota(gb_ref.shape, 1)
        gb_ref[...] += functools.reduce(
            jnp.add, [jnp.where(place == head, s, 0.0) for head, s in zip(heads, sums)]
        )

    def scale_row(side):
        return cs_ref[0, pl.ds(side * units + at, 1), :]

    def scaled_dout(side):
        return (dot_ref[64 * side : 64 * side + 64, :].astype(F32) * scale_row(side)).astype(LOW)

    def grad_scores(side, scaled):
        zero = jnp.zeros((64, rows_q), LOW)
        rowdot = rd_ref[pl.ds(2 * pair + side, 1), :] * scale_row(side)
        right = jnp.concatenate([scaled, zero] if side == 0 else [zero, scaled], axis=0)
        grad_p = dot(v_ref[...], right)
        return (p_ref[side].astype(F32) * (grad_p - rowdot)).astype(LOW)

    scaled = [scaled_dout(side) for side in range(2)]
    natural = jnp.concatenate(scaled, axis=0).T
    dks, dvs, dqs, by_words = [], [], [], []
    for side in range(2):
        ds = grad_scores(side, scaled[side])
        key_t = kt_ref[64 * side : 64 * side + 64, :]
        both = dot(jnp.concatenate([key_t, ekt[at]], axis=0), ds)
        dqs.append(both[:64, :])
        by_words.append(both[64:, :].astype(LOW))
        dvs.append(dot(p_ref[side], natural))
        dks.append(dot(ds, q_ref[...]))
    grid = dot(jnp.concatenate(by_words, axis=0), eq[...])
    grid = jnp.concatenate([grid, jnp.zeros((2 * KEY_WORDS, FOLD - QUERY_WORDS), F32)], axis=1)
    fold([grid[:KEY_WORDS, :], grid[KEY_WORDS:, :]], bmask[at], [2 * pair, 2 * pair + 1])
    first = iota((unit, 128), 1) < 64
    dk_ref[...] = jnp.where(first, dks[0], dks[1]).astype(LOW)
    dv_ref[...] = jnp.where(first, dvs[0], dvs[1]).astype(LOW)

    @pl.when(at == 0)
    def _():
        grads = jnp.concatenate(dqs, axis=0)
        dq_acc[...] = so_far_ref[...] + grads if last else grads

    @pl.when(at > 0)
    def _():
        dq_acc[...] += jnp.concatenate(dqs, axis=0)

    if last:

        @pl.when(at == units - 1)
        def _():
            dq_ref[...] = (dq_acc[...] * 0.125).astype(LOW)

    k_wins = (ids[0, k_off + at * unit + unit - 1] - first_word(at)) // KEY_WORDS + 1

    @pl.when(jnp.logical_or(q_wins > 1, k_wins > 1))
    def _():
        for side in range(2):
            held[...] = grad_scores(side, scaled_dout(side))

            def over_keys(win, carry, side=side):
                by_word[...] = dot(key_words(at, win), held[...]).astype(LOW)

                def over_queries(q_win, inner):
                    spread[:, :QUERY_WORDS] = dot(by_word[...], query_words(q_win))
                    fold([spread[...]], bucket_mask(at, win, q_win), [2 * pair + side])
                    return inner

                return lax.fori_loop(jnp.where(win == 0, 1, 0), q_wins, over_queries, carry)

            lax.fori_loop(0, k_wins, over_keys, 0)


def attend_back(spot, first_pair, pairs, ids, info, p, key_t, value, query, dout_t, scales, rowdot, so_far=None):
    width, rows_k = key_t.shape
    rows_q = query.shape[0]
    length = ids.shape[1]
    unit = unit_of(rows_k)
    units = rows_k // unit
    stats = scales.shape[1]
    last = so_far is not None
    so_far, skip = so_far if last else (None, 0)
    dq_spec = pl.BlockSpec((128, rows_q), lambda g, i, *_: (g, 0))
    return pl.pallas_call(
        functools.partial(attend_back_kernel, rows_q, rows_k, spot, first_pair, last),
        out_shape=[
            jax.ShapeDtypeStruct((128 * pairs, rows_q), LOW if last else F32),
            jax.ShapeDtypeStruct((rows_k, 128 * pairs), LOW),
            jax.ShapeDtypeStruct((rows_k, 128 * pairs), LOW),
            jax.ShapeDtypeStruct((32, 128), F32),
        ],
        grid_spec=pltpu.PrefetchScalarGridSpec(
            num_scalar_prefetch=2,
            grid=(pairs, units),
            in_specs=[
                full((1, length)),
                pl.BlockSpec((2, unit, rows_q), lambda g, i, *_: (first_pair + g, i, 0)),
                pl.BlockSpec((128, unit), lambda g, i, *_: (first_pair + g, i)),
                pl.BlockSpec((unit, 128), lambda g, i, *_: (i, first_pair + g)),
                pl.BlockSpec((rows_q, 128), lambda g, i, *_: (0, first_pair + g)),
                pl.BlockSpec((128, rows_q), lambda g, i, *_: (first_pair + g, 0)),
                pl.BlockSpec((1, stats, rows_q), lambda g, i, *_: (first_pair + g, 0, 0)),
                full(rowdot.shape),
            ]
            + [pl.BlockSpec((128, rows_q), lambda g, i, *_: (skip + g, 0))] * last,
            out_specs=[
                dq_spec,
                pl.BlockSpec((unit, 128), lambda g, i, *_: (i, g)),
                pl.BlockSpec((unit, 128), lambda g, i, *_: (i, g)),
                full((32, 128)),
            ],
            scratch_shapes=[
                pltpu.VMEM((rows_q, QUERY_WORDS), LOW),
                pltpu.VMEM((units, KEY_WORDS, unit), LOW),
                pltpu.VMEM((units, 32, FOLD), F32),
                pltpu.VMEM((KEY_WORDS, FOLD), F32),
                pltpu.VMEM((unit, rows_q), LOW),
                pltpu.VMEM((KEY_WORDS, rows_q), LOW),
            ]
            + [pltpu.VMEM((128, rows_q), F32)] * last,
        ),
        compiler_params=params(),
        cost_estimate=cost(7 * pairs),
        name="attend_back",
    )(*((ids, info, ids, p, key_t, value, query, dout_t, scales, rowdot) + ((so_far,) if last else ())))


def norm_back(v, gain, incoming):
    factor = lax.rsqrt(jnp.mean(v * v, axis=-1, keepdims=True) + 1e-06)
    scaled = incoming * gain
    inner = jnp.mean(scaled * v, axis=-1, keepdims=True)
    back = factor * scaled - v * (factor * factor * factor * inner)
    return back, jnp.sum(incoming * v * factor, axis=0, keepdims=True)


def ffn_kernel(blocks, units, mes, info, *refs):
    step = pl.program_id(0)
    outs, stats = refs[:blocks], refs[blocks : 2 * blocks]
    branch_ref, out_proj_ref, gain_ref, cot_ref, wg_ref, wu_ref, wd_ref = refs[2 * blocks : 2 * blocks + 7]
    rest = refs[2 * blocks + 7 :]
    scales = rest[:blocks]
    result_ref, datt_ref, dout_ref, rd_ref, dgain_ref = rest[blocks : blocks + 5]
    pieces = rest[blocks + 5 : blocks + 7]
    attn, attn_low, after, n2, n2t, y_acc, dn_acc, packed, held, sems = rest[blocks + 7 :]
    heads = attn.shape[0] // 64
    chunk = wg_ref.shape[1]
    rows = after.shape[0]

    @pl.when(step == 0)
    def _():
        for head in range(heads):
            pair, side = head // 2, head % 2
            peaks = [s[pair, 2 * units + side : 2 * units + side + 1, :] for s in stats]
            top = functools.reduce(jnp.maximum, peaks)
            shares = [jnp.exp(peak - top) for peak in peaks]
            sums = [s[pair, 2 * units + 2 + side : 2 * units + 3 + side, :] for s in stats]
            inverse = 1.0 / functools.reduce(jnp.add, [a * b for a, b in zip(shares, sums)])
            band = slice(64 * head, 64 * head + 64)
            attn[band, :] = functools.reduce(
                jnp.add, [o[band, :] * (share * inverse) for o, share in zip(outs, shares)]
            )
            for s, c in zip(stats, scales):
                c[pair, side * units : (side + 1) * units, :] = (
                    jnp.exp(s[pair, side * units : (side + 1) * units, :] - top) * inverse
                )
        attn_low[...] = attn[...].astype(LOW)
        joined = branch_ref[...] + dot(attn_low[...].T, out_proj_ref[...])
        after[...] = joined
        factor = lax.rsqrt(jnp.mean(joined * joined, axis=-1, keepdims=True) + 1e-06)
        normed = (joined * factor * gain_ref[...].astype(F32)).astype(LOW)
        n2[...] = normed
        n2t[...] = normed.T

    weights = jnp.concatenate([wg_ref[...], wu_ref[...]], axis=1)
    both = dot(n2[...], weights)
    gate, up = both[:, :chunk], both[:, chunk:]
    grad_hidden = dot_nt(cot_ref[...], wd_ref[...])
    square = gate * gate
    inner = gate * (0.7978845608028654 + (0.7978845608028654 * 0.044715) * square)
    part = 0.5 + 0.5 * jnp.tanh(inner)
    act = gate * part
    slope = part + 2.0 * act * (1.0 - part) * (
        0.7978845608028654 + (3.0 * 0.7978845608028654 * 0.044715) * square
    )
    hidden = (act * up).astype(LOW)
    grad_both = jnp.concatenate(
        [(grad_hidden * up * slope).astype(LOW), (grad_hidden * act).astype(LOW)], axis=1
    )
    y_part = dot(hidden, wd_ref[...])
    dn_part = dot_nt(grad_both, weights)

    @pl.when(step == 0)
    def _():
        y_acc[...] = y_part
        dn_acc[...] = dn_part

    @pl.when(step > 0)
    def _():
        y_acc[...] += y_part
        dn_acc[...] += dn_part

    grad_w = dot(n2t[...], grad_both).astype(LOW)
    grad_d = dot(hidden.T, cot_ref[...]).astype(LOW)
    turn = info[mes + 1 - step // 2] & 7

    def leaving(j):
        target = pieces[j // 2].at[8 * (j % 2) : 8 * (j % 2) + 8, 0:768, :]
        return pltpu.make_async_copy(held.at[j % 2], target, sems.at[j % 2])

    for j in range(4):

        @pl.when(step == j)
        def _(j=j):
            if j >= 2:
                leaving(j - 2).wait()
            for k in range(8):
                col, row = 128 * (k // 2), 256 * (k % 2)
                spot = k ^ turn
                held[j % 2, spot, 0:256, :] = grad_w[row : row + 256, col : col + 128]
                held[j % 2, spot, 256:512, :] = grad_w[row : row + 256, chunk + col : chunk + col + 128]
                held[j % 2, spot, 512:640, :] = grad_d[col : col + 128, row : row + 128]
                held[j % 2, spot, 640:768, :] = grad_d[col : col + 128, row + 128 : row + 256]
            leaving(j).start()

    @pl.when(step == pl.num_programs(0) - 1)
    def _():
        result_ref[...] = (after[...] + y_acc[...]).astype(LOW)
        back, dgain = norm_back(after[...], gain_ref[...].astype(F32), dn_acc[...])
        datt = cot_ref[...].astype(F32) + back
        datt_ref[...] = datt
        dgain_ref[...] = jnp.broadcast_to(dgain, dgain_ref.shape)
        datt_low = datt.astype(LOW)
        dout = dot_nt(out_proj_ref[...], datt_low).astype(LOW)
        dout_ref[...] = dout
        pack(packed, 0, dot(attn_low[...], datt_low).astype(LOW), mes, info)
        rest_of = [
            pltpu.make_async_copy(packed.at[16 - 16 * j : 32 - 16 * j], pieces[j].at[:, 768:, :], sems.at[2 + j])
            for j in range(2)
        ]
        for copy in rest_of:
            copy.start()
        prod = dout.astype(F32) * attn[...]
        for head in range(heads):
            rd_ref[head : head + 1, :] = jnp.sum(prod[64 * head : 64 * head + 64, :], axis=0, keepdims=True)
        for copy in rest_of + [leaving(2), leaving(3)]:
            copy.wait()


def hidden_block(mes, info, away, position):
    place = info[mes + away] >> 3
    return 2 * (place >> 1) + (position ^ (place & 1))


def feed_forward(mes, info, outs, stats, branch, out_proj, gain, cot, w_gate_up, w_down, units):
    rows, width = branch.shape
    hidden = w_down.shape[0]
    chunk = 512
    steps = hidden // chunk
    blocks = len(outs)
    heads = width // 64
    once = lambda shape: pl.BlockSpec(shape, lambda *_: (0,) * len(shape), pipeline_mode=pl.Buffered(1))
    nat = (rows, width)

    def block(i, info):
        return hidden_block(mes, info, 1 - i // 2, i % 2)

    pieces = [(16, 768 + width // 8, 128)] * 2
    return pl.pallas_call(
        functools.partial(ffn_kernel, blocks, units, mes),
        out_shape=[jax.ShapeDtypeStruct(s.shape, F32) for s in stats]
        + [
            jax.ShapeDtypeStruct(nat, LOW),
            jax.ShapeDtypeStruct(nat, F32),
            jax.ShapeDtypeStruct((width, rows), LOW),
            jax.ShapeDtypeStruct((heads, rows), F32),
            jax.ShapeDtypeStruct((8, width), F32),
        ]
        + [jax.ShapeDtypeStruct(p, LOW) for p in pieces],
        grid_spec=pltpu.PrefetchScalarGridSpec(
            num_scalar_prefetch=1,
            grid=(steps,),
            in_specs=[once(o.shape) for o in outs]
            + [once(s.shape) for s in stats]
            + [
                once(nat),
                once((width, width)),
                once(gain.shape),
                once(nat),
                pl.BlockSpec((width, chunk), lambda i, info: (0, block(i, info))),
                pl.BlockSpec((width, chunk), lambda i, info: (0, block(i, info) + steps)),
                pl.BlockSpec((chunk, width), lambda i, info: (block(i, info), 0)),
            ],
            out_specs=[once(s.shape) for s in stats]
            + [
                once(nat),
                once(nat),
                once((width, rows)),
                once((heads, rows)),
                once((8, width)),
            ]
            + [pl.BlockSpec(memory_space=pl.ANY)] * len(pieces),
            scratch_shapes=[
                pltpu.VMEM((width, rows), F32),
                pltpu.VMEM((width, rows), LOW),
                pltpu.VMEM(nat, F32),
                pltpu.VMEM(nat, LOW),
                pltpu.VMEM((width, rows), LOW),
                pltpu.VMEM(nat, F32),
                pltpu.VMEM(nat, F32),
                pltpu.VMEM((32, width // 8, 128), LOW),
                pltpu.VMEM((2, 8, 768, 128), LOW),
                pltpu.SemaphoreType.DMA((4,)),
            ],
        ),
        compiler_params=params(),
        cost_estimate=cost(35),
        name="feed_forward",
    )(info, *outs, *stats, branch, out_proj, gain, cot, w_gate_up, w_gate_up, w_down)


def back_other_kernel(count, *refs):
    dks, dvs = refs[:count], refs[count : 2 * count]
    n_ref, w_ref, dn_ref, dw_ref, acc = refs[2 * count :]
    width = n_ref.shape[1]
    both = jnp.concatenate([r[...] for r in dks + dvs], axis=1)
    dn_ref[...] = dot_nt(both, w_ref[:, width:]).astype(LOW)
    part = dot(n_ref[...].T, both)

    @pl.when(pl.program_id(0) == 0)
    def _():
        acc[...] = part

    @pl.when(pl.program_id(0) > 0)
    def _():
        acc[...] += part

    @pl.when(pl.program_id(0) == pl.num_programs(0) - 1)
    def _():
        dw_ref[...] = acc[...].astype(LOW)


def back_other(dks, dvs, normed, w_qkv):
    rows, width = normed.shape
    tile = min(512, rows)
    nat = pl.BlockSpec((tile, width), lambda i: (i, 0))
    return pl.pallas_call(
        functools.partial(back_other_kernel, len(dks)),
        grid=(rows // tile,),
        out_shape=[jax.ShapeDtypeStruct((rows, width), LOW), jax.ShapeDtypeStruct((width, 2 * width), LOW)],
        in_specs=[pl.BlockSpec((tile, d.shape[1]), lambda i: (i, 0)) for d in dks + dvs] + [nat, full(w_qkv.shape)],
        out_specs=[nat, full((width, 2 * width))],
        scratch_shapes=[pltpu.VMEM((width, 2 * width), F32)],
        compiler_params=params(),
        cost_estimate=cost(5),
        name="back_other",
    )(*dks, *dvs, normed, w_qkv)


def packed_at(g, mes, info):
    here = g ^ info[mes]
    return jnp.where(here < 16, here, 16 + (g ^ info[mes + 1]))


def pack(out, at, value, mes, info):
    rows = value.shape[0] // 32
    for g in range(32):
        for lane in range(value.shape[1] // 128):
            start = at + lane * rows
            out[packed_at(g, mes, info), start : start + rows, :] = value[g * rows : (g + 1) * rows, lane * 128 : (lane + 1) * 128]


def finish_kernel(mes, parts_count, few, calls, info, *refs):
    parts, gbs = refs[:parts_count], refs[parts_count : parts_count + few]
    at = parts_count + few
    dqs, dks, dvs = (refs[at + calls * j : at + calls * (j + 1)] for j in range(3))
    rest = refs[at + 3 * calls :]
    dwkv_ref, n_ref, branch_ref, datt_ref, mixed_ref, conv_ref, w_ref, kernels_ref, gain_ref, ids_ref, x_ref, halo_ref, dgain_ref = rest[:13]
    gx_ref, ret_ref, early, late, ext, edge, masks, small, packed, dw_acc, conv_acc = rest[13:]
    step = pl.program_id(0)
    steps = pl.num_programs(0)
    tile, width = branch_ref.shape
    taps = make_taps(kernels_ref[...])

    @pl.when(step == 0)
    def _():
        masks[...] = same_words(ids_ref[...])
        ext[0:8, :] = halo_ref[...].astype(F32)
        ext[8:, :] = x_ref[...].astype(F32)
        for j in range(3):
            edge[j, tile + 8 :, :] = jnp.zeros((8, width), F32)
            edge[j, 0:8, :] = jnp.zeros((8, width), F32)
        small[...] = jnp.zeros_like(small)
        small[5:6, :] = dgain_ref[0:1, :]
        conv_acc[...] = jnp.zeros_like(conv_acc)

    dq = jnp.concatenate([r[...] for r in dqs], axis=0).T
    dqkv = jnp.concatenate([dq] + [r[...] for r in dks + dvs], axis=1)
    dn = dot_nt(dqkv, w_ref[...])
    for part in parts:
        dn = dn + part[...].astype(F32)
    dw = dot(n_ref[...].T, dqkv)

    @pl.when(step == 0)
    def _():
        dw_acc[...] = dw

    @pl.when(step > 0)
    def _():
        dw_acc[...] += dw

    back, dgain = norm_back(branch_ref[...], gain_ref[...].astype(F32), dn)
    dbranch = datt_ref[...] + back
    dbranch_low = dbranch.astype(LOW)
    conv_acc[...] += dot(mixed_ref[...].T, dbranch_low)
    dmixed = dot_nt(dbranch_low, conv_ref[...])
    at = pl.multiple_of((steps - 1 - step) * tile, tile)
    same = masks[:, pl.ds(pl.multiple_of(info[0] + at, 128), tile)].T
    inputs = ext[pl.ds(at, tile + 8), :]
    small[4:5, :] += dgain
    grad = dbranch + taps[0] * dmixed
    small[0:1, :] += jnp.sum(dmixed * inputs[8:, :], axis=0, keepdims=True)
    returned = jnp.zeros((8, width), F32)
    for back_by in range(1, 4):
        masked = dmixed * same[:, back_by : back_by + 1]
        small[back_by : back_by + 1, :] += jnp.sum(masked * inputs[8 - back_by : 8 - back_by + tile, :], axis=0, keepdims=True)
        j = back_by - 1
        edge[j, 8 : 8 + tile, :] = masked
        grad = grad + taps[back_by] * edge[j, 8 + back_by : 8 + back_by + tile, :]
        returned = returned + taps[back_by] * edge[j, back_by : back_by + 8, :]
        edge[j, tile + 8 :, :] = masked[0:8, :]
    gx_ref[...] = grad
    ret_ref[...] = returned

    @pl.when(step == steps - 1)
    def _():
        pack(packed, 0, dw_acc[:, :width].astype(LOW), mes, info)
        pack(packed, width // 8, (dw_acc[:, width:] + dwkv_ref[...].astype(F32)).astype(LOW), mes, info)
        depth = 3 * width // 8
        pack(packed, depth, conv_acc[...].astype(LOW), mes, info)
        depth += width // 8
        gb = functools.reduce(jnp.add, [r[...] for r in gbs])
        for g in range(32):
            lane = 128 * (g % 4)
            line = jnp.concatenate(
                [small[g // 4 : g // 4 + 1, lane : lane + 128], gb[g : g + 1, :], jnp.zeros((14, 128), F32)], axis=0
            )
            packed[packed_at(g, mes, info), depth : depth + 16, :] = line.astype(LOW)
        early[...] = packed[16:]
        late[...] = packed[:16]


def finish(mes, info, parts, gbs, dqs, dks, dvs, dw_kv, normed, branch, datt, mixed, conv_proj, w_qkv, kernels, gain, ids, x, halo, dgain):
    rows, width = branch.shape
    tile = min(512, rows)
    steps = rows // tile
    depth = 4 * width // 8 + 16
    nat = pl.BlockSpec((tile, width), lambda i, *_: (steps - 1 - i, 0))
    operands = (*parts, *gbs, *dqs, *dks, *dvs, dw_kv, normed, branch, datt, mixed, conv_proj, w_qkv, kernels, gain, ids, x, halo, dgain)
    specs = (
        [nat] * len(parts)
        + [full(g.shape) for g in gbs]
        + [pl.BlockSpec((d.shape[0], tile), lambda i, *_: (0, steps - 1 - i)) for d in dqs]
        + [pl.BlockSpec((tile, d.shape[1]), lambda i, *_: (steps - 1 - i, 0)) for d in dks + dvs]
        + [full(dw_kv.shape)]
        + [nat] * 4
        + [full(o.shape) for o in (conv_proj, w_qkv, kernels, gain, ids, x, halo, dgain)]
    )
    outs = [
        jax.ShapeDtypeStruct((rows, width), F32),
        jax.ShapeDtypeStruct((8, width), F32),
    ] + [jax.ShapeDtypeStruct((16, depth, 128), LOW)] * 2
    return pl.pallas_call(
        functools.partial(finish_kernel, mes, len(parts), len(gbs), len(dqs)),
        out_shape=outs,
        grid_spec=pltpu.PrefetchScalarGridSpec(
            num_scalar_prefetch=1,
            grid=(steps,),
            in_specs=specs,
            out_specs=[nat] + [full(o.shape) for o in outs[1:]],
            scratch_shapes=[
                pltpu.VMEM((rows + 8, width), F32),
                pltpu.VMEM((3, tile + 16, width), F32),
                pltpu.VMEM((8, ids.shape[1]), F32),
                pltpu.VMEM((8, width), F32),
                pltpu.VMEM((32, depth, 128), LOW),
                pltpu.VMEM((width, 3 * width), F32),
                pltpu.VMEM((width, width), F32),
            ],
        ),
        compiler_params=params(),
        cost_estimate=cost(12),
        name="finish",
    )(info, *operands)


def spread_ffn_kernel(mes, away, info, source, *rest):
    gate_up_ref, down_ref = rest[-2:]
    which = pl.program_id(1)
    turn = info[mes + away] & 7
    for k in range(8):
        col, row = 128 * (k // 2), 256 * (k % 2)
        gate_up_ref[row : row + 256, col : col + 128] = source[
            k ^ turn, pl.ds(pl.multiple_of(which * 256, 256), 256), :
        ].astype(F32)

    @pl.when(which == 0)
    def _():
        for k in range(8):
            col, row = 128 * (k // 2), 256 * (k % 2)
            for part in range(2):
                lane = row + 128 * part
                down_ref[col : col + 128, lane : lane + 128] = source[
                    k ^ turn, 512 + 128 * part : 640 + 128 * part, :
                ].astype(F32)


def spread_ffn(mes, away, info, pieces, width, hidden, into=()):
    steps = hidden // 512
    return pl.pallas_call(
        functools.partial(spread_ffn_kernel, mes, away),
        out_shape=[jax.ShapeDtypeStruct((width, 2 * hidden), F32), jax.ShapeDtypeStruct((hidden, width), F32)],
        grid_spec=pltpu.PrefetchScalarGridSpec(
            num_scalar_prefetch=1,
            grid=(2, 2),
            in_specs=[pl.BlockSpec((8,) + pieces.shape[1:], lambda i, w, info: (i, 0, 0))]
            + [pl.BlockSpec(memory_space=pl.ANY)] * len(into),
            out_specs=[
                pl.BlockSpec((width, 512), lambda i, w, info: (0, w * steps + hidden_block(mes, info, away, i))),
                pl.BlockSpec((512, width), lambda i, w, info: (hidden_block(mes, info, away, i), 0)),
            ],
        ),
        input_output_aliases={2 + j: j for j in range(len(into))},
        compiler_params=params(),
        cost_estimate=cost(5),
        name="spread_ffn",
    )(info, pieces, *into)


def group_of(mes, info, step):
    return (step & 1) ^ (info[mes + step // 2] >> 3)


def spread_kernel(mes, info, own_c, other_c, own_e, other_e, qkv_ref, out_ref, conv_ref, taps_ref, gain_a_ref, gain_f_ref, bias_ref, few):
    step = pl.program_id(0)
    turn = info[mes + step // 2] & 7
    group = group_of(mes, info, step)
    width = out_ref.shape[1]
    places = [(out_ref, 0, width)]
    places_e = [(qkv_ref, 0, 3 * width), (conv_ref, 0, width)]
    for j, pair in enumerate(((own_c, own_e), (other_c, other_e))):

        @pl.when(step // 2 == j)
        def _(pair=pair):
            for source, targets in zip(pair, (places, places_e)):
                for k in range(8):
                    spot = k ^ (info[mes - 2 + step // 2] & 7) if targets is places else k ^ turn
                    at = 0
                    for out, column, columns in targets:
                        for lane in range(column, column + columns, 128):
                            out[16 * k : 16 * k + 16, lane : lane + 128] = source[spot, at : at + 16, :].astype(F32)
                            at += 16
                    if targets is places_e:
                        few[group, k] = source[spot, at : at + 16, :].astype(F32)

    @pl.when(step == 3)
    def _():
        lines = [
            jnp.concatenate([few[(4 * r + c) // 8, (4 * r + c) % 8, 0:1, :] for c in range(4)], axis=1)
            for r in range(6)
        ]
        for row, line in enumerate((0, 1, 0, 1, 2, 0, 1, 2, 3)):
            taps_ref[row : row + 1, :] = lines[line]
        gain_a_ref[...] = lines[4]
        gain_f_ref[...] = lines[5]
        heads = bias_ref.shape[1]
        for g in range(32):
            bias_ref[g : g + 1, :] = few[g // 8, g % 8, 1:2, :][:, :heads]


def spread(mes, info, own_c, other_c, own_e, other_e, width, heads):
    def source(depth, at, j):
        def index(i, info):
            plain = group_of(mes, info, i) & 1
            used = plain if at else i & 1
            return (jnp.where(i // 2 == j, used, 1 - j), at, 0)

        return pl.BlockSpec((8, depth, 128), index)

    deep = own_e.shape[1]
    out_at = own_c.shape[1] * 8 // width - 1

    columns = (3 * width, width, width)
    small = [(9, width), (1, width), (1, width), (32, heads)]
    return pl.pallas_call(
        functools.partial(spread_kernel, mes),
        out_shape=[jax.ShapeDtypeStruct((width, c), F32) for c in columns]
        + [jax.ShapeDtypeStruct(shape, F32) for shape in small],
        grid_spec=pltpu.PrefetchScalarGridSpec(
            num_scalar_prefetch=1,
            grid=(4,),
            in_specs=[source(width // 8, out_at, j) for j in range(2)] + [source(deep, 0, j) for j in range(2)],
            out_specs=[pl.BlockSpec((width // 4, c), lambda i, info: (group_of(mes, info, i), 0)) for c in columns]
            + [full(shape) for shape in small],
            scratch_shapes=[pltpu.VMEM((4, 8, 16, 128), F32)],
        ),
        compiler_params=params(),
        cost_estimate=cost(5),
        name="spread",
    )(info, own_c, other_c, own_e, other_e)


def hop_masks(sizes):
    seq = [sizes["dp"] << b for b in range(sizes["seq"].bit_length() - 1)]
    dp = [1 << b for b in range(1, sizes["dp"].bit_length() - 1)]
    return [1] + seq + dp


def place_of(masks):
    here = lax.axis_index(EVERY)
    me = jnp.int32(0)
    for mask in masks[:5]:
        me = me * 2 + jnp.where((here & mask) != 0, 1, 0)
    return me


def swap(value, mask):
    count = lax.axis_size(EVERY)
    return lax.ppermute(value, EVERY, [(i, i ^ mask) for i in range(count)])


def partners(phase):
    masks = [0]
    for mask in phase:
        masks = [m ^ extra for m in masks for extra in (0, mask)]
    return masks[1:]


def groups_of(masks, count):
    rest = [i for i in range(count) if all((i & m) == 0 for m in masks)]
    return [[i ^ m for m in [0] + partners(masks)] for i in rest]


def added(a, b):
    return (a.astype(F32) + b.astype(F32)).astype(LOW)


class Sum:
    def __init__(self, masks, sizes, early, late):
        phases, at = [], 0
        for size in sizes:
            phases.append(masks[at : at + size])
            at += size
        self.down = phases
        self.across = masks[at:]
        self.value = late
        self.leaving = list(early)
        self.flights = []
        self.stage = 0
        self.other = None

    def combine(self):
        self.stage += 1
        stage, down, across = self.stage, len(self.down), len(self.across)
        if stage <= down + across:
            self.value = functools.reduce(
                jnp.add, [v.astype(F32) for v in [self.value] + self.flights]
            ).astype(LOW)
        else:
            self.value = jnp.concatenate([self.value] + self.flights, axis=0)
        if stage < down:
            count = 1 << len(self.down[stage])
            share = self.value.shape[0] // count
            pieces = [self.value[j * share : (j + 1) * share] for j in range(count)]
            self.value, self.leaving = pieces[0], pieces[1:]

    def launch(self):
        stage, down, across = self.stage, len(self.down), len(self.across)
        if stage < down:
            self.flights = [swap(v, m) for v, m in zip(self.leaving, partners(self.down[stage]))]
        elif stage < down + across:
            self.flights = [swap(self.value, self.across[stage - down])]
        else:
            left = down - 1 - (stage - down - across)
            self.flights = [swap(self.value, m) for m in partners(self.down[left])]
            if left == 0:
                self.other = self.flights[0]

    def finish(self):
        while self.other is None:
            step_on([self])

    def held(self):
        sending = self.stage < len(self.down)
        return [self.value] + (self.leaving if sending else [])

    def hold(self, values):
        self.value = values[0]
        if self.stage < len(self.down):
            self.leaving = list(values[1:])


def step_on(sums, fresh=(), ties=(), after=()):
    if after:
        flat = lax.optimization_barrier(tuple(v for r in sums for v in r.flights) + tuple(after))
        at = 0
        for running in sums:
            running.flights = list(flat[at : at + len(running.flights)])
            at += len(running.flights)
        ties = tuple(ties) + tuple(flat[at:])
    for running in sums:
        running.combine()
    moving = list(sums) + list(fresh)
    groups = [running.held() for running in moving]
    flat = lax.optimization_barrier(tuple(v for g in groups for v in g) + tuple(ties))
    at = 0
    for running, group in zip(moving, groups):
        running.hold(flat[at : at + len(group)])
        at += len(group)
        running.launch()
    return flat[at:]


def total(terms):
    if len(terms) == 1:
        return terms[0]
    return functools.reduce(jnp.add, [t.astype(F32) for t in terms]).astype(terms[0].dtype)


def shards(sizes, tokens, word_ids, cotangent, conv_kernels, conv_proj, gain_attn, w_qkv, rel_bias, out_proj, gain_ffn, w_gate_up, w_down):
    seqs, rows, width = tokens.shape
    heads = rel_bias.shape[1]
    pairs = heads // 2
    ring = sizes["seq"]
    me = lax.axis_index("seq")
    masks = hop_masks(sizes)
    count = sizes["seq"] * sizes["dp"]
    core = lax.axis_index("dp") & 1
    place = place_of(masks)
    info = jnp.stack(
        [((me + k) % ring) * rows for k in range(ring)] + [16 * core + (place & 3), 16 - 16 * core + (place & 3), place, place ^ 16]
    ).astype(jnp.int32)
    mes = ring
    gain_one, gain_two = gain_attn[None, :], gain_ffn[None, :]
    halo = lax.ppermute(tokens[:, rows - 8 :, :], "seq", [(i, (i + 1) % ring) for i in range(ring)])
    halo, travelling = lax.optimization_barrier((halo, tokens))
    block_tokens = [tokens] + [
        lax.ppermute(travelling, "seq", [((i + k) % ring, i) for i in range(ring)]) for k in range(1, ring)
    ]
    halos = [halo] + [b[:, rows - 8 :, :] for b in block_tokens[:-1]]
    units = rows // unit_of(rows)

    parts_of = []
    for s in range(seqs):
        ids = word_ids[s : s + 1]
        own = project(True, 0, info, tokens[s], halos[0][s], ids, conv_kernels, gain_one, conv_proj, w_qkv)
        branch, mixed, normed, query, query_t, key, key_t, value, value_t = own
        held = [(normed, key, key_t, value, value_t)]
        fwd = [attend(0, ids, info, rel_bias, key, value_t, query_t)]
        for k in range(1, ring):
            held.append(
                project(False, k, info, block_tokens[k][s], halos[k][s], ids, conv_kernels, gain_one, conv_proj, w_qkv)
            )
            fwd.append(attend(k, ids, info, rel_bias, held[k][1], held[k][4], query_t))
        ffn = feed_forward(
            mes, info, [f[1] for f in fwd], [f[2] for f in fwd], branch, out_proj, gain_two, cotangent[s], w_gate_up, w_down, units
        )
        parts_of.append((ids, held, fwd, query, branch, mixed, ffn))

    pieces = [total([p[-1][ring + 5 + j] for p in parts_of]) for j in range(2)]
    flight = swap(pieces[0], masks[0])

    chips = None
    near = groups_of(masks[1:3], count)
    results, gxs, rets, last_pieces = [], [], [], []
    for s in range(seqs):
        ids, held, fwd, query, branch, mixed, ffn = parts_of[s]
        scales = ffn[:ring]
        result, datt, dout_t, rowdot, dgain = ffn[ring : ring + 5]
        results.append(result)
        def run_back(k, first, count, go, so_far=None):
            return attend_back(
                k, first, count, ids, info, fwd[k][0], held[k][2], held[k][3], query, dout_t, scales[k], go, so_far
            )

        parts, dw_kvs, gbs, dq_sum = [], [], [], None
        for k in range(1, ring):
            go = rowdot
            if chips is None:
                chips, go = lax.optimization_barrier((added(pieces[1], flight), rowdot))
                chips = lax.psum_scatter(chips, EVERY, scatter_dimension=0, tiled=True, axis_index_groups=near)
            low = run_back(k, 0, pairs // 2, go)
            high = run_back(k, pairs // 2, pairs - pairs // 2, rowdot)
            dq_k = [low[0], high[0]]
            dq_sum = dq_k if dq_sum is None else [a + b for a, b in zip(dq_sum, dq_k)]
            gbs += [low[3], high[3]]
            dn, dw_kv = back_other([low[1], high[1]], [low[2], high[2]], held[k][0], w_qkv)
            parts.append(lax.ppermute(dn, "seq", [(i, (i + k) % ring) for i in range(ring)]))
            dw_kvs.append(dw_kv)
        if dq_sum is None:
            dq_sum = [jnp.zeros((width // 2, rows), F32)] * 2
        dw_kv = total(dw_kvs) if dw_kvs else jnp.zeros((width, 2 * width), LOW)
        own = [run_back(0, 0, pairs // 2, rowdot, (dq_sum[0], 0))]
        gb, go, taps = own[0][3], rowdot, conv_kernels
        final = s == seqs - 1
        if final:
            chips, gb = lax.optimization_barrier((chips, gb))
            share = chips.shape[0] // 4
            quarters = [chips[j * share : (j + 1) * share] for j in range(4)]
            sum_z = Sum(masks[3:], (2,), quarters[1:], quarters[0])
            (go,) = step_on([], [sum_z], (rowdot,))
        own.append(run_back(0, pairs // 2, pairs - pairs // 2, go, (dq_sum[1], 0)))
        last_gb = own[1][3]
        if final:
            taps, last_gb = step_on([sum_z], (), (conv_kernels,), (last_gb,))
        gbs += [gb, last_gb]
        gx, ret, early, late = finish(
            mes + 2, info, parts, gbs, [o[0] for o in own], [o[1] for o in own], [o[2] for o in own], dw_kv,
            held[0][0], branch, datt, mixed, conv_proj, w_qkv, taps, gain_one, ids, tokens[s], halos[0][s], dgain,
        )
        gxs.append(gx)
        rets.append(ret)
        last_pieces.append((early, late))

    early, late = [total([p[j] for p in last_pieces]) for j in range(2)]
    sum_e = Sum(masks, (1, 2, 2), [early], late)
    hidden = w_down.shape[0]
    gxs, rets = jnp.stack(gxs), jnp.stack(rets)
    while sum_z.stage < 1 + len(sum_z.across):
        step_on([sum_z])
    flat = lax.optimization_barrier(tuple(sum_z.flights) + (rets,))
    sum_z.flights, rets = list(flat[:-1]), flat[-1]
    sum_z.combine()
    chips, gxs, ret = step_on([], [sum_e], (sum_z.value, gxs, rets))
    chips = lax.all_gather(chips, EVERY, axis=0, tiled=True, axis_index_groups=near)
    returned = lax.ppermute(ret, "seq", [(i, i - 1) for i in range(1, ring)])
    step_on([sum_e])
    grad_tokens = gxs.at[:, rows - 8 :, :].add(returned)
    (grad_tokens,) = step_on([sum_e], (), (grad_tokens,))
    while sum_e.stage < 2 * len(sum_e.down) + len(sum_e.across) - 3:
        step_on([sum_e])
    (chips,) = step_on([sum_e], (), (chips,))
    other = swap(chips, masks[0])
    grads = spread_ffn(mes, 0, info, chips, width, hidden)
    grad_gate_up, grad_down = spread_ffn(mes, 1, info, other, width, hidden, grads)
    grad_gate_up, grad_down = step_on([sum_e], (), (), (grad_gate_up, grad_down))
    sum_e.finish()
    grad_w_qkv, grad_out_proj, grad_conv_proj, grad_kernels, grad_gain_a, grad_gain_f, grad_bias = spread(
        mes + 2, info, chips, other, sum_e.value, sum_e.other, width, heads
    )
    return (
        jnp.stack(results),
        grad_tokens,
        grad_kernels,
        grad_conv_proj,
        grad_gain_a.reshape(-1),
        grad_w_qkv,
        grad_bias,
        grad_out_proj,
        grad_gain_f.reshape(-1),
        grad_gate_up,
        grad_down,
    )


def solution(mesh):
    sizes = dict(mesh.shape)
    split = P("dp", "seq", None)
    in_specs = (split, P("dp", None), split) + (P(),) * 9
    out_specs = (split, split) + (P(),) * 9
    return jax.shard_map(
        functools.partial(shards, sizes), mesh=mesh, in_specs=in_specs, out_specs=out_specs, check_vma=False
    )
```

```python
import functools

import jax
import jax.numpy as jnp
from jax import lax
from jax.experimental import pallas as pl
from jax.experimental.pallas import tpu as pltpu
from jax.sharding import PartitionSpec as P

EVERY = ("seq", "dp")
LOW = jnp.bfloat16
F32 = jnp.float32
EDGES = (1, 2, 3, 4, 5, 6, 7, 8, 11, 16, 22, 32, 45, 64, 91)
KEY_WORDS = 128
QUERY_WORDS = 256
FOLD = 512
VMEM_BYTES = 60 * 2**20


def bucketize(offsets):
    magnitude = jnp.abs(offsets)
    bucketed = jnp.where(offsets > 0, 16, 0).astype(jnp.int32)
    for edge in EDGES:
        bucketed = bucketed + (magnitude >= edge).astype(jnp.int32)
    return bucketed


def dot(a, b):
    return jnp.dot(a, b, preferred_element_type=F32)


def dot_nt(a, b):
    return lax.dot_general(a, b, (((1,), (1,)), ((), ())), preferred_element_type=F32)


def iota(shape, dim):
    return lax.broadcasted_iota(jnp.int32, shape, dim)


def onehot(mask):
    return mask.astype(F32).astype(LOW)


def params(**kw):
    return pltpu.CompilerParams(vmem_limit_bytes=VMEM_BYTES, **kw)


def cost(micros):
    return pl.CostEstimate(flops=int(micros * 1e7), bytes_accessed=int(micros * 1e4), transcendentals=0)


def full(shape):
    return pl.BlockSpec(shape, lambda *_: (0,) * len(shape))


def make_taps(kernels):
    k = kernels.astype(F32)
    return [
        k[0:1] + k[2:3] + k[5:6],
        k[1:2] + k[3:4] + k[6:7],
        k[4:5] + k[7:8],
        k[8:9],
    ]


def same_words(ids):
    place = iota(ids.shape, 1)
    rows = [
        jnp.where((pltpu.roll(ids, back, 1) == ids) & (place >= back), 1.0, 0.0) for back in range(1, 4)
    ]
    return jnp.concatenate([jnp.zeros(ids.shape, F32)] + rows + [jnp.zeros((4, ids.shape[1]), F32)], axis=0)


def project_kernel(own, at, info, x_ref, halo_ref, ids_ref, kernels_ref, gain_ref, conv_ref, w_ref, *rest):
    step = pl.program_id(0)
    tile = rest[0].shape[0]
    ext, masks = rest[-2:]
    width = x_ref.shape[1]

    @pl.when(step == 0)
    def _():
        ext[0:8, :] = halo_ref[...].astype(F32)
        ext[8:, :] = x_ref[...].astype(F32)
        masks[...] = same_words(ids_ref[...])

    start = pl.multiple_of(step * tile, tile)
    chunk = ext[pl.ds(start, tile + 8), :]
    lane = pl.multiple_of(info[at] + step * tile, tile)
    same = masks[:, pl.ds(lane, tile)].T
    taps = make_taps(kernels_ref[...])
    inputs = chunk[8:, :]
    mixed = taps[0] * inputs
    for back in range(1, 4):
        mixed = mixed + taps[back] * chunk[8 - back : 8 - back + tile, :] * same[:, back : back + 1]
    mixed_low = mixed.astype(LOW)
    branch = inputs + dot(mixed_low, conv_ref[...])
    factor = lax.rsqrt(jnp.mean(branch * branch, axis=-1, keepdims=True) + 1e-06)
    normed = (branch * factor * gain_ref[...].astype(F32)).astype(LOW)
    if own:
        branch_ref, mixed_ref, n_ref, q_ref, qt_ref, k_ref, kt_ref, v_ref, vt_ref = rest[:-2]
        qkv = dot(normed, w_ref[...]).astype(LOW)
        query = qkv[:, :width] * jnp.asarray(0.125, LOW)
        q_ref[...] = query
        qt_ref[...] = query.T
        branch_ref[...] = branch
        mixed_ref[...] = mixed_low
        key, value = qkv[:, width : 2 * width], qkv[:, 2 * width :]
    else:
        n_ref, k_ref, kt_ref, v_ref, vt_ref = rest[:-2]
        kv = dot(normed, w_ref[:, width:]).astype(LOW)
        key, value = kv[:, :width], kv[:, width:]
    n_ref[...] = normed
    k_ref[...] = key
    kt_ref[...] = key.T
    v_ref[...] = value
    vt_ref[...] = value.T


def project(own, at, info, x, halo, ids, kernels, gain, conv_proj, w_qkv):
    rows, width = x.shape
    tile = min(256, rows)
    nat = pl.BlockSpec((tile, width), lambda i, *_: (i, 0))
    tra = pl.BlockSpec((width, tile), lambda i, *_: (0, i))
    nat_low = jax.ShapeDtypeStruct((rows, width), LOW)
    tra_low = jax.ShapeDtypeStruct((width, rows), LOW)
    nat_f32 = jax.ShapeDtypeStruct((rows, width), F32)
    if own:
        outs = [(nat_f32, nat), (nat_low, nat), (nat_low, nat), (nat_low, nat), (tra_low, tra)]
    else:
        outs = [(nat_low, nat)]
    outs = outs + [(nat_low, nat), (tra_low, tra), (nat_low, nat), (tra_low, tra)]
    operands = (x, halo, ids, kernels, gain, conv_proj, w_qkv)
    return pl.pallas_call(
        functools.partial(project_kernel, own, at),
        out_shape=[s for s, _ in outs],
        grid_spec=pltpu.PrefetchScalarGridSpec(
            num_scalar_prefetch=1,
            grid=(rows // tile,),
            in_specs=[full(o.shape) for o in operands],
            out_specs=[b for _, b in outs],
            scratch_shapes=[pltpu.VMEM((rows + 8, width), F32), pltpu.VMEM((8, ids.shape[1]), F32)],
        ),
        compiler_params=params(),
        cost_estimate=cost(8 if own else 6),
        name="project_own" if own else "project_other",
    )(info, *operands)


def word_spans(ids, q_off, k_off, rows_q, rows_k, unit):
    q_first = ids[0, q_off]
    q_wins = (ids[0, q_off + rows_q - 1] - q_first) // QUERY_WORDS + 1
    firsts, wins = [], []
    for at in range(0, rows_k, unit):
        first = ids[0, k_off + at]
        firsts.append(first)
        wins.append((ids[0, k_off + at + unit - 1] - first) // KEY_WORDS + 1)
    fits = q_wins == 1
    for count in wins:
        fits = jnp.logical_and(fits, count == 1)
    return q_first, q_wins, firsts, wins, fits


def unit_of(rows_k):
    return min(512, rows_k)


def stat_rows(rows_k):
    return -(-(2 * (rows_k // unit_of(rows_k)) + 4) // 8) * 8


def attend_kernel(rows_q, rows_k, spot, ids, info, ids_ref, bias_ref, k_ref, vt_ref, qt_ref, p_ref, o_ref, stat_ref, eqt, ek, bidx, raw, tab_ref, parts, flag):
    pair = pl.program_id(0)
    unit = unit_of(rows_k)
    units = rows_k // unit
    q_off, k_off = info[0], info[spot]
    q_first, q_wins, firsts, wins, fits = word_spans(ids, q_off, k_off, rows_q, rows_k, unit)
    q_ids = ids_ref[:, pl.ds(pl.multiple_of(q_off, 128), rows_q)]

    def unit_ids(at):
        return ids_ref[:, pl.ds(pl.multiple_of(k_off + at * unit, 128), unit)]

    def query_words(win):
        return onehot(iota((QUERY_WORDS, rows_q), 0) + (q_first + win * QUERY_WORDS) == q_ids)

    def key_words(at, win):
        return onehot(iota((KEY_WORDS, unit), 0) + (firsts[at] + win * KEY_WORDS) == unit_ids(at)).T

    def buckets(at, win, q_win):
        shift = firsts[at] + win * KEY_WORDS - q_first - q_win * QUERY_WORDS
        shape = (KEY_WORDS, QUERY_WORDS)
        return bucketize(shift + iota(shape, 0) - iota(shape, 1))

    def window_bias(head, index):
        row = jnp.broadcast_to(tab_ref[pl.ds(head, 1), :], (KEY_WORDS, 128))
        parts = [
            jnp.take_along_axis(row, index[:, c : c + 128], axis=1) for c in range(0, QUERY_WORDS, 128)
        ]
        return jnp.concatenate(parts, axis=1).astype(LOW)

    @pl.when(pair == 0)
    def _():
        eqt[...] = query_words(0)
        tab_ref[:, : bias_ref.shape[1]] = bias_ref[...].astype(F32)
        for at in range(units):
            ek[at * unit : (at + 1) * unit, :] = key_words(at, 0)
            bidx[at] = buckets(at, 0, 0)

    def queries(side):
        zero = jnp.zeros((64, rows_q), LOW)
        mine = qt_ref[64 * side : 64 * side + 64, :]
        return [mine, zero] if side == 0 else [zero, mine]

    def fast_scores(side, at):
        rows = slice(at * unit, (at + 1) * unit)
        bias = window_bias(2 * pair + side, bidx[at])
        spread = dot(bias, eqt[...]).astype(LOW)
        right = jnp.concatenate(queries(side) + [spread], axis=0)
        left = jnp.concatenate([k_ref[rows, :], ek[rows, :]], axis=1)
        return dot(left, right)

    def slow_scores(side, at):
        rows = slice(at * unit, (at + 1) * unit)
        raw[...] = dot(k_ref[rows, :], jnp.concatenate(queries(side), axis=0))

        def over_keys(win, carry):
            def over_queries(q_win, inner):
                bias = window_bias(2 * pair + side, buckets(at, win, q_win))
                spread = dot(bias, query_words(q_win)).astype(LOW)
                raw[...] += dot(key_words(at, win), spread)
                return inner

            return lax.fori_loop(0, q_wins, over_queries, carry)

        lax.fori_loop(0, wins[at], over_keys, 0)
        return raw[...]

    jobs = [(side, at) for side in range(2) for at in range(units)]

    def softmax_part(job, score):
        side, at = job
        rows = slice(at * unit, (at + 1) * unit)
        top = jnp.max(score, axis=0, keepdims=True)
        expo = jnp.exp(score - top).astype(LOW)
        p_ref[side, rows, :] = expo
        left = jnp.concatenate([vt_ref[64 * side : 64 * side + 64, rows], jnp.ones((16, unit), LOW)], axis=0)
        parts[side * units + at] = dot(left, expo)
        stat_ref[0, side * units + at : side * units + at + 1, :] = top

    def merge():
        for side in range(2):
            tops = [stat_ref[0, side * units + at : side * units + at + 1, :] for at in range(units)]
            peak = functools.reduce(jnp.maximum, tops)
            total = functools.reduce(
                jnp.add, [parts[side * units + at] * jnp.exp(tops[at] - peak) for at in range(units)]
            )
            o_ref[64 * side : 64 * side + 64, :] = total[:64, :]
            stat_ref[0, 2 * units + side : 2 * units + side + 1, :] = peak
            stat_ref[0, 2 * units + 2 + side : 2 * units + 3 + side, :] = total[64:65, :]

    def run_fast():
        stat_ref[...] = jnp.zeros_like(stat_ref)
        least = most = None
        for side, at in jobs:
            rows = slice(at * unit, (at + 1) * unit)
            expo = jnp.exp(fast_scores(side, at)).astype(LOW)
            p_ref[side, rows, :] = expo
            left = jnp.concatenate([vt_ref[64 * side : 64 * side + 64, rows], jnp.ones((16, unit), LOW)], axis=0)
            part = dot(left, expo)
            parts[side * units + at] = part
            sums = part[64:65, :]
            least = sums if least is None else jnp.minimum(least, sums)
            most = sums if most is None else jnp.maximum(most, sums)
        return jnp.logical_and(jnp.min(least) > 1e-25, jnp.max(most) < 1e25)

    def run_slow():
        for job in jobs:
            softmax_part(job, slow_scores(*job))

    flag[0] = 0

    @pl.when(fits)
    def _():
        flag[0] = run_fast().astype(jnp.int32)

    @pl.when(flag[0] == 0)
    def _():
        run_slow()

    merge()


def attend(spot, ids, info, rel_bias, key, value_t, query_t):
    rows_k, width = key.shape
    rows_q = query_t.shape[1]
    length = ids.shape[1]
    unit = unit_of(rows_k)
    units = rows_k // unit
    stats = stat_rows(rows_k)
    pairs = width // 128
    return pl.pallas_call(
        functools.partial(attend_kernel, rows_q, rows_k, spot),
        out_shape=[
            jax.ShapeDtypeStruct((2 * pairs, rows_k, rows_q), LOW),
            jax.ShapeDtypeStruct((width, rows_q), F32),
            jax.ShapeDtypeStruct((pairs, stats, rows_q), F32),
        ],
        grid_spec=pltpu.PrefetchScalarGridSpec(
            num_scalar_prefetch=2,
            grid=(pairs,),
            in_specs=[
                full((1, length)),
                full(rel_bias.shape),
                pl.BlockSpec((rows_k, 128), lambda p, *_: (0, p)),
                pl.BlockSpec((128, rows_k), lambda p, *_: (p, 0)),
                pl.BlockSpec((128, rows_q), lambda p, *_: (p, 0)),
            ],
            out_specs=[
                pl.BlockSpec((2, rows_k, rows_q), lambda p, *_: (p, 0, 0)),
                pl.BlockSpec((128, rows_q), lambda p, *_: (p, 0)),
                pl.BlockSpec((1, stats, rows_q), lambda p, *_: (p, 0, 0)),
            ],
            scratch_shapes=[
                pltpu.VMEM((QUERY_WORDS, rows_q), LOW),
                pltpu.VMEM((rows_k, KEY_WORDS), LOW),
                pltpu.VMEM((units, KEY_WORDS, QUERY_WORDS), jnp.int32),
                pltpu.VMEM((unit, rows_q), F32),
                pltpu.VMEM((2 * pairs, 128), F32),
                pltpu.VMEM((2 * units, 80, rows_q), F32),
                pltpu.SMEM((1,), jnp.int32),
            ],
        ),
        compiler_params=params(),
        cost_estimate=cost(20),
        name="attend",
    )(ids, info, ids, rel_bias, key, value_t, query_t)


def attend_back_kernel(rows_q, rows_k, spot, first_pair, last, ids, info, ids_ref, p_ref, kt_ref, v_ref, q_ref, dot_ref, cs_ref, rd_ref, *rest):
    if last:
        so_far_ref, rest = rest[0], rest[1:]
    dq_ref, dk_ref, dv_ref, gb_ref, eq, ekt, bmask, spread, held, by_word = rest[:10]
    dq_acc = rest[10] if last else dq_ref
    at = pl.program_id(1)
    pair = first_pair + pl.program_id(0)
    unit = unit_of(rows_k)
    units = rows_k // unit
    q_off, k_off = info[0], info[spot]
    q_first = ids[0, q_off]
    q_wins = (ids[0, q_off + rows_q - 1] - q_first) // QUERY_WORDS + 1
    q_ids = ids_ref[:, pl.ds(pl.multiple_of(q_off, 128), rows_q)]

    def query_words(win):
        return onehot(iota((QUERY_WORDS, rows_q), 0) + (q_first + win * QUERY_WORDS) == q_ids).T

    def first_word(index):
        return ids[0, k_off + index * unit]

    def key_words(index, win):
        k_ids = ids_ref[:, pl.ds(pl.multiple_of(k_off + index * unit, 128), unit)]
        return onehot(iota((KEY_WORDS, unit), 0) + (first_word(index) + win * KEY_WORDS) == k_ids)

    def bucket_mask(index, win, q_win):
        lane = iota((32, FOLD), 1)
        ahead = jnp.where(lane < FOLD - KEY_WORDS, lane, lane - FOLD)
        shift = first_word(index) + win * KEY_WORDS - q_first - q_win * QUERY_WORDS
        return (bucketize(shift - ahead) == iota((32, FOLD), 0)).astype(F32)

    @pl.when(jnp.logical_and(at == 0, pl.program_id(0) == 0))
    def _():
        eq[...] = query_words(0)
        gb_ref[...] = jnp.zeros_like(gb_ref)
        spread[...] = jnp.zeros_like(spread)
        for index in range(units):
            ekt[index] = key_words(index, 0)
            bmask[index] = bucket_mask(index, 0, 0)

    def fold(grids, mask, heads):
        half = KEY_WORDS // 2
        while half >= 8:
            grids = [g[:half, :] + pltpu.roll(g[half:, :], FOLD - half, 1) for g in grids]
            half //= 2
        row = iota((8, FOLD), 0)
        for bit in (4, 2, 1):
            grids = [jnp.where((row & bit) != 0, pltpu.roll(g, FOLD - bit, 1), g) for g in grids]
        sums = [jnp.sum(mask * jnp.sum(g, axis=0, keepdims=True), axis=1, keepdims=True) for g in grids]
        place = iota(gb_ref.shape, 1)
        gb_ref[...] += functools.reduce(
            jnp.add, [jnp.where(place == head, s, 0.0) for head, s in zip(heads, sums)]
        )

    def scale_row(side):
        return cs_ref[0, pl.ds(side * units + at, 1), :]

    def scaled_dout(side):
        return (dot_ref[64 * side : 64 * side + 64, :].astype(F32) * scale_row(side)).astype(LOW)

    def grad_scores(side, scaled):
        zero = jnp.zeros((64, rows_q), LOW)
        rowdot = rd_ref[pl.ds(2 * pair + side, 1), :] * scale_row(side)
        right = jnp.concatenate([scaled, zero] if side == 0 else [zero, scaled], axis=0)
        grad_p = dot(v_ref[...], right)
        return (p_ref[side].astype(F32) * (grad_p - rowdot)).astype(LOW)

    scaled = [scaled_dout(side) for side in range(2)]
    natural = jnp.concatenate(scaled, axis=0).T
    dks, dvs, dqs, by_words = [], [], [], []
    for side in range(2):
        ds = grad_scores(side, scaled[side])
        key_t = kt_ref[64 * side : 64 * side + 64, :]
        both = dot(jnp.concatenate([key_t, ekt[at]], axis=0), ds)
        dqs.append(both[:64, :])
        by_words.append(both[64:, :].astype(LOW))
        dvs.append(dot(p_ref[side], natural))
        dks.append(dot(ds, q_ref[...]))
    grid = dot(jnp.concatenate(by_words, axis=0), eq[...])
    grid = jnp.concatenate([grid, jnp.zeros((2 * KEY_WORDS, FOLD - QUERY_WORDS), F32)], axis=1)
    fold([grid[:KEY_WORDS, :], grid[KEY_WORDS:, :]], bmask[at], [2 * pair, 2 * pair + 1])
    first = iota((unit, 128), 1) < 64
    dk_ref[...] = jnp.where(first, dks[0], dks[1]).astype(LOW)
    dv_ref[...] = jnp.where(first, dvs[0], dvs[1]).astype(LOW)

    @pl.when(at == 0)
    def _():
        grads = jnp.concatenate(dqs, axis=0)
        dq_acc[...] = so_far_ref[...] + grads if last else grads

    @pl.when(at > 0)
    def _():
        dq_acc[...] += jnp.concatenate(dqs, axis=0)

    if last:

        @pl.when(at == units - 1)
        def _():
            dq_ref[...] = (dq_acc[...] * 0.125).astype(LOW)

    k_wins = (ids[0, k_off + at * unit + unit - 1] - first_word(at)) // KEY_WORDS + 1

    @pl.when(jnp.logical_or(q_wins > 1, k_wins > 1))
    def _():
        for side in range(2):
            held[...] = grad_scores(side, scaled_dout(side))

            def over_keys(win, carry, side=side):
                by_word[...] = dot(key_words(at, win), held[...]).astype(LOW)

                def over_queries(q_win, inner):
                    spread[:, :QUERY_WORDS] = dot(by_word[...], query_words(q_win))
                    fold([spread[...]], bucket_mask(at, win, q_win), [2 * pair + side])
                    return inner

                return lax.fori_loop(jnp.where(win == 0, 1, 0), q_wins, over_queries, carry)

            lax.fori_loop(0, k_wins, over_keys, 0)


def attend_back(spot, first_pair, pairs, ids, info, p, key_t, value, query, dout_t, scales, rowdot, so_far=None):
    width, rows_k = key_t.shape
    rows_q = query.shape[0]
    length = ids.shape[1]
    unit = unit_of(rows_k)
    units = rows_k // unit
    stats = scales.shape[1]
    last = so_far is not None
    so_far, skip = so_far if last else (None, 0)
    dq_spec = pl.BlockSpec((128, rows_q), lambda g, i, *_: (g, 0))
    return pl.pallas_call(
        functools.partial(attend_back_kernel, rows_q, rows_k, spot, first_pair, last),
        out_shape=[
            jax.ShapeDtypeStruct((128 * pairs, rows_q), LOW if last else F32),
            jax.ShapeDtypeStruct((rows_k, 128 * pairs), LOW),
            jax.ShapeDtypeStruct((rows_k, 128 * pairs), LOW),
            jax.ShapeDtypeStruct((32, 128), F32),
        ],
        grid_spec=pltpu.PrefetchScalarGridSpec(
            num_scalar_prefetch=2,
            grid=(pairs, units),
            in_specs=[
                full((1, length)),
                pl.BlockSpec((2, unit, rows_q), lambda g, i, *_: (first_pair + g, i, 0)),
                pl.BlockSpec((128, unit), lambda g, i, *_: (first_pair + g, i)),
                pl.BlockSpec((unit, 128), lambda g, i, *_: (i, first_pair + g)),
                pl.BlockSpec((rows_q, 128), lambda g, i, *_: (0, first_pair + g)),
                pl.BlockSpec((128, rows_q), lambda g, i, *_: (first_pair + g, 0)),
                pl.BlockSpec((1, stats, rows_q), lambda g, i, *_: (first_pair + g, 0, 0)),
                full(rowdot.shape),
            ]
            + [pl.BlockSpec((128, rows_q), lambda g, i, *_: (skip + g, 0))] * last,
            out_specs=[
                dq_spec,
                pl.BlockSpec((unit, 128), lambda g, i, *_: (i, g)),
                pl.BlockSpec((unit, 128), lambda g, i, *_: (i, g)),
                full((32, 128)),
            ],
            scratch_shapes=[
                pltpu.VMEM((rows_q, QUERY_WORDS), LOW),
                pltpu.VMEM((units, KEY_WORDS, unit), LOW),
                pltpu.VMEM((units, 32, FOLD), F32),
                pltpu.VMEM((KEY_WORDS, FOLD), F32),
                pltpu.VMEM((unit, rows_q), LOW),
                pltpu.VMEM((KEY_WORDS, rows_q), LOW),
            ]
            + [pltpu.VMEM((128, rows_q), F32)] * last,
        ),
        compiler_params=params(),
        cost_estimate=cost(7 * pairs),
        name="attend_back",
    )(*((ids, info, ids, p, key_t, value, query, dout_t, scales, rowdot) + ((so_far,) if last else ())))


def norm_back(v, gain, incoming):
    factor = lax.rsqrt(jnp.mean(v * v, axis=-1, keepdims=True) + 1e-06)
    scaled = incoming * gain
    inner = jnp.mean(scaled * v, axis=-1, keepdims=True)
    back = factor * scaled - v * (factor * factor * factor * inner)
    return back, jnp.sum(incoming * v * factor, axis=0, keepdims=True)


def ffn_kernel(blocks, units, mes, info, *refs):
    step = pl.program_id(0)
    outs, stats = refs[:blocks], refs[blocks : 2 * blocks]
    branch_ref, out_proj_ref, gain_ref, cot_ref, wg_ref, wu_ref, wd_ref = refs[2 * blocks : 2 * blocks + 7]
    rest = refs[2 * blocks + 7 :]
    scales = rest[:blocks]
    result_ref, datt_ref, dout_ref, rd_ref, dgain_ref = rest[blocks : blocks + 5]
    pieces = rest[blocks + 5 : blocks + 7]
    attn, attn_low, after, n2, n2t, y_acc, dn_acc, packed, held, sems = rest[blocks + 7 :]
    heads = attn.shape[0] // 64
    chunk = wg_ref.shape[1]
    rows = after.shape[0]

    @pl.when(step == 0)
    def _():
        for head in range(heads):
            pair, side = head // 2, head % 2
            peaks = [s[pair, 2 * units + side : 2 * units + side + 1, :] for s in stats]
            top = functools.reduce(jnp.maximum, peaks)
            shares = [jnp.exp(peak - top) for peak in peaks]
            sums = [s[pair, 2 * units + 2 + side : 2 * units + 3 + side, :] for s in stats]
            inverse = 1.0 / functools.reduce(jnp.add, [a * b for a, b in zip(shares, sums)])
            band = slice(64 * head, 64 * head + 64)
            attn[band, :] = functools.reduce(
                jnp.add, [o[band, :] * (share * inverse) for o, share in zip(outs, shares)]
            )
            for s, c in zip(stats, scales):
                c[pair, side * units : (side + 1) * units, :] = (
                    jnp.exp(s[pair, side * units : (side + 1) * units, :] - top) * inverse
                )
        attn_low[...] = attn[...].astype(LOW)
        joined = branch_ref[...] + dot(attn_low[...].T, out_proj_ref[...])
        after[...] = joined
        factor = lax.rsqrt(jnp.mean(joined * joined, axis=-1, keepdims=True) + 1e-06)
        normed = (joined * factor * gain_ref[...].astype(F32)).astype(LOW)
        n2[...] = normed
        n2t[...] = normed.T

    weights = jnp.concatenate([wg_ref[...], wu_ref[...]], axis=1)
    both = dot(n2[...], weights)
    gate, up = both[:, :chunk], both[:, chunk:]
    grad_hidden = dot_nt(cot_ref[...], wd_ref[...])
    square = gate * gate
    inner = gate * (0.7978845608028654 + (0.7978845608028654 * 0.044715) * square)
    part = 0.5 + 0.5 * jnp.tanh(inner)
    act = gate * part
    slope = part + 2.0 * act * (1.0 - part) * (
        0.7978845608028654 + (3.0 * 0.7978845608028654 * 0.044715) * square
    )
    hidden = (act * up).astype(LOW)
    grad_both = jnp.concatenate(
        [(grad_hidden * up * slope).astype(LOW), (grad_hidden * act).astype(LOW)], axis=1
    )
    y_part = dot(hidden, wd_ref[...])
    dn_part = dot_nt(grad_both, weights)

    @pl.when(step == 0)
    def _():
        y_acc[...] = y_part
        dn_acc[...] = dn_part

    @pl.when(step > 0)
    def _():
        y_acc[...] += y_part
        dn_acc[...] += dn_part

    grad_w = dot(n2t[...], grad_both).astype(LOW)
    grad_d = dot(hidden.T, cot_ref[...]).astype(LOW)
    turn = info[mes + 1 - step // 2] & 7

    def leaving(j):
        target = pieces[j // 2].at[8 * (j % 2) : 8 * (j % 2) + 8, 0:768, :]
        return pltpu.make_async_copy(held.at[j % 2], target, sems.at[j % 2])

    for j in range(4):

        @pl.when(step == j)
        def _(j=j):
            if j >= 2:
                leaving(j - 2).wait()
            for k in range(8):
                col, row = 128 * (k // 2), 256 * (k % 2)
                spot = k ^ turn
                held[j % 2, spot, 0:256, :] = grad_w[row : row + 256, col : col + 128]
                held[j % 2, spot, 256:512, :] = grad_w[row : row + 256, chunk + col : chunk + col + 128]
                held[j % 2, spot, 512:640, :] = grad_d[col : col + 128, row : row + 128]
                held[j % 2, spot, 640:768, :] = grad_d[col : col + 128, row + 128 : row + 256]
            leaving(j).start()

    @pl.when(step == pl.num_programs(0) - 1)
    def _():
        result_ref[...] = (after[...] + y_acc[...]).astype(LOW)
        back, dgain = norm_back(after[...], gain_ref[...].astype(F32), dn_acc[...])
        datt = cot_ref[...].astype(F32) + back
        datt_ref[...] = datt
        dgain_ref[...] = jnp.broadcast_to(dgain, dgain_ref.shape)
        datt_low = datt.astype(LOW)
        dout = dot_nt(out_proj_ref[...], datt_low).astype(LOW)
        dout_ref[...] = dout
        pack(packed, 0, dot(attn_low[...], datt_low).astype(LOW), mes, info)
        rest_of = [
            pltpu.make_async_copy(packed.at[16 - 16 * j : 32 - 16 * j], pieces[j].at[:, 768:, :], sems.at[2 + j])
            for j in range(2)
        ]
        for copy in rest_of:
            copy.start()
        prod = dout.astype(F32) * attn[...]
        for head in range(heads):
            rd_ref[head : head + 1, :] = jnp.sum(prod[64 * head : 64 * head + 64, :], axis=0, keepdims=True)
        for copy in rest_of + [leaving(2), leaving(3)]:
            copy.wait()


def hidden_block(mes, info, away, position):
    place = info[mes + away] >> 3
    return 2 * (place >> 1) + (position ^ (place & 1))


def feed_forward(mes, info, outs, stats, branch, out_proj, gain, cot, w_gate_up, w_down, units):
    rows, width = branch.shape
    hidden = w_down.shape[0]
    chunk = 512
    steps = hidden // chunk
    blocks = len(outs)
    heads = width // 64
    once = lambda shape: pl.BlockSpec(shape, lambda *_: (0,) * len(shape), pipeline_mode=pl.Buffered(1))
    nat = (rows, width)

    def block(i, info):
        return hidden_block(mes, info, 1 - i // 2, i % 2)

    pieces = [(16, 768 + width // 8, 128)] * 2
    return pl.pallas_call(
        functools.partial(ffn_kernel, blocks, units, mes),
        out_shape=[jax.ShapeDtypeStruct(s.shape, F32) for s in stats]
        + [
            jax.ShapeDtypeStruct(nat, LOW),
            jax.ShapeDtypeStruct(nat, F32),
            jax.ShapeDtypeStruct((width, rows), LOW),
            jax.ShapeDtypeStruct((heads, rows), F32),
            jax.ShapeDtypeStruct((8, width), F32),
        ]
        + [jax.ShapeDtypeStruct(p, LOW) for p in pieces],
        grid_spec=pltpu.PrefetchScalarGridSpec(
            num_scalar_prefetch=1,
            grid=(steps,),
            in_specs=[once(o.shape) for o in outs]
            + [once(s.shape) for s in stats]
            + [
                once(nat),
                once((width, width)),
                once(gain.shape),
                once(nat),
                pl.BlockSpec((width, chunk), lambda i, info: (0, block(i, info))),
                pl.BlockSpec((width, chunk), lambda i, info: (0, block(i, info) + steps)),
                pl.BlockSpec((chunk, width), lambda i, info: (block(i, info), 0)),
            ],
            out_specs=[once(s.shape) for s in stats]
            + [
                once(nat),
                once(nat),
                once((width, rows)),
                once((heads, rows)),
                once((8, width)),
            ]
            + [pl.BlockSpec(memory_space=pl.ANY)] * len(pieces),
            scratch_shapes=[
                pltpu.VMEM((width, rows), F32),
                pltpu.VMEM((width, rows), LOW),
                pltpu.VMEM(nat, F32),
                pltpu.VMEM(nat, LOW),
                pltpu.VMEM((width, rows), LOW),
                pltpu.VMEM(nat, F32),
                pltpu.VMEM(nat, F32),
                pltpu.VMEM((32, width // 8, 128), LOW),
                pltpu.VMEM((2, 8, 768, 128), LOW),
                pltpu.SemaphoreType.DMA((4,)),
            ],
        ),
        compiler_params=params(),
        cost_estimate=cost(35),
        name="feed_forward",
    )(info, *outs, *stats, branch, out_proj, gain, cot, w_gate_up, w_gate_up, w_down)


def back_other_kernel(count, *refs):
    dks, dvs = refs[:count], refs[count : 2 * count]
    n_ref, w_ref, dn_ref, dw_ref, acc = refs[2 * count :]
    width = n_ref.shape[1]
    both = jnp.concatenate([r[...] for r in dks + dvs], axis=1)
    dn_ref[...] = dot_nt(both, w_ref[:, width:]).astype(LOW)
    part = dot(n_ref[...].T, both)

    @pl.when(pl.program_id(0) == 0)
    def _():
        acc[...] = part

    @pl.when(pl.program_id(0) > 0)
    def _():
        acc[...] += part

    @pl.when(pl.program_id(0) == pl.num_programs(0) - 1)
    def _():
        dw_ref[...] = acc[...].astype(LOW)


def back_other(dks, dvs, normed, w_qkv):
    rows, width = normed.shape
    tile = min(512, rows)
    nat = pl.BlockSpec((tile, width), lambda i: (i, 0))
    return pl.pallas_call(
        functools.partial(back_other_kernel, len(dks)),
        grid=(rows // tile,),
        out_shape=[jax.ShapeDtypeStruct((rows, width), LOW), jax.ShapeDtypeStruct((width, 2 * width), LOW)],
        in_specs=[pl.BlockSpec((tile, d.shape[1]), lambda i: (i, 0)) for d in dks + dvs] + [nat, full(w_qkv.shape)],
        out_specs=[nat, full((width, 2 * width))],
        scratch_shapes=[pltpu.VMEM((width, 2 * width), F32)],
        compiler_params=params(),
        cost_estimate=cost(5),
        name="back_other",
    )(*dks, *dvs, normed, w_qkv)


def packed_at(g, mes, info):
    here = g ^ info[mes]
    return jnp.where(here < 16, here, 16 + (g ^ info[mes + 1]))


def pack(out, at, value, mes, info):
    rows = value.shape[0] // 32
    for g in range(32):
        for lane in range(value.shape[1] // 128):
            start = at + lane * rows
            out[packed_at(g, mes, info), start : start + rows, :] = value[g * rows : (g + 1) * rows, lane * 128 : (lane + 1) * 128]


def finish_kernel(mes, parts_count, few, calls, info, *refs):
    parts, gbs = refs[:parts_count], refs[parts_count : parts_count + few]
    at = parts_count + few
    dqs, dks, dvs = (refs[at + calls * j : at + calls * (j + 1)] for j in range(3))
    rest = refs[at + 3 * calls :]
    dwkv_ref, n_ref, branch_ref, datt_ref, mixed_ref, conv_ref, w_ref, kernels_ref, gain_ref, ids_ref, x_ref, halo_ref, dgain_ref = rest[:13]
    gx_ref, ret_ref, early, late, ext, edge, masks, small, packed, dw_acc, conv_acc = rest[13:]
    step = pl.program_id(0)
    steps = pl.num_programs(0)
    tile, width = branch_ref.shape
    taps = make_taps(kernels_ref[...])

    @pl.when(step == 0)
    def _():
        masks[...] = same_words(ids_ref[...])
        ext[0:8, :] = halo_ref[...].astype(F32)
        ext[8:, :] = x_ref[...].astype(F32)
        for j in range(3):
            edge[j, tile + 8 :, :] = jnp.zeros((8, width), F32)
            edge[j, 0:8, :] = jnp.zeros((8, width), F32)
        small[...] = jnp.zeros_like(small)
        small[5:6, :] = dgain_ref[0:1, :]
        conv_acc[...] = jnp.zeros_like(conv_acc)

    dq = jnp.concatenate([r[...] for r in dqs], axis=0).T
    dqkv = jnp.concatenate([dq] + [r[...] for r in dks + dvs], axis=1)
    dn = dot_nt(dqkv, w_ref[...])
    for part in parts:
        dn = dn + part[...].astype(F32)
    dw = dot(n_ref[...].T, dqkv)

    @pl.when(step == 0)
    def _():
        dw_acc[...] = dw

    @pl.when(step > 0)
    def _():
        dw_acc[...] += dw

    back, dgain = norm_back(branch_ref[...], gain_ref[...].astype(F32), dn)
    dbranch = datt_ref[...] + back
    dbranch_low = dbranch.astype(LOW)
    conv_acc[...] += dot(mixed_ref[...].T, dbranch_low)
    dmixed = dot_nt(dbranch_low, conv_ref[...])
    at = pl.multiple_of((steps - 1 - step) * tile, tile)
    same = masks[:, pl.ds(pl.multiple_of(info[0] + at, 128), tile)].T
    inputs = ext[pl.ds(at, tile + 8), :]
    small[4:5, :] += dgain
    grad = dbranch + taps[0] * dmixed
    small[0:1, :] += jnp.sum(dmixed * inputs[8:, :], axis=0, keepdims=True)
    returned = jnp.zeros((8, width), F32)
    for back_by in range(1, 4):
        masked = dmixed * same[:, back_by : back_by + 1]
        small[back_by : back_by + 1, :] += jnp.sum(masked * inputs[8 - back_by : 8 - back_by + tile, :], axis=0, keepdims=True)
        j = back_by - 1
        edge[j, 8 : 8 + tile, :] = masked
        grad = grad + taps[back_by] * edge[j, 8 + back_by : 8 + back_by + tile, :]
        returned = returned + taps[back_by] * edge[j, back_by : back_by + 8, :]
        edge[j, tile + 8 :, :] = masked[0:8, :]
    gx_ref[...] = grad
    ret_ref[...] = returned

    @pl.when(step == steps - 1)
    def _():
        pack(packed, 0, dw_acc[:, :width].astype(LOW), mes, info)
        pack(packed, width // 8, (dw_acc[:, width:] + dwkv_ref[...].astype(F32)).astype(LOW), mes, info)
        depth = 3 * width // 8
        pack(packed, depth, conv_acc[...].astype(LOW), mes, info)
        depth += width // 8
        gb = functools.reduce(jnp.add, [r[...] for r in gbs])
        for g in range(32):
            lane = 128 * (g % 4)
            line = jnp.concatenate(
                [small[g // 4 : g // 4 + 1, lane : lane + 128], gb[g : g + 1, :], jnp.zeros((14, 128), F32)], axis=0
            )
            packed[packed_at(g, mes, info), depth : depth + 16, :] = line.astype(LOW)
        early[...] = packed[16:]
        late[...] = packed[:16]


def finish(mes, info, parts, gbs, dqs, dks, dvs, dw_kv, normed, branch, datt, mixed, conv_proj, w_qkv, kernels, gain, ids, x, halo, dgain):
    rows, width = branch.shape
    tile = min(1024, rows)
    steps = rows // tile
    depth = 4 * width // 8 + 16
    nat = pl.BlockSpec((tile, width), lambda i, *_: (steps - 1 - i, 0))
    operands = (*parts, *gbs, *dqs, *dks, *dvs, dw_kv, normed, branch, datt, mixed, conv_proj, w_qkv, kernels, gain, ids, x, halo, dgain)
    specs = (
        [nat] * len(parts)
        + [full(g.shape) for g in gbs]
        + [pl.BlockSpec((d.shape[0], tile), lambda i, *_: (0, steps - 1 - i)) for d in dqs]
        + [pl.BlockSpec((tile, d.shape[1]), lambda i, *_: (steps - 1 - i, 0)) for d in dks + dvs]
        + [full(dw_kv.shape)]
        + [nat] * 4
        + [full(o.shape) for o in (conv_proj, w_qkv, kernels, gain, ids, x, halo, dgain)]
    )
    outs = [
        jax.ShapeDtypeStruct((rows, width), F32),
        jax.ShapeDtypeStruct((8, width), F32),
    ] + [jax.ShapeDtypeStruct((16, depth, 128), LOW)] * 2
    return pl.pallas_call(
        functools.partial(finish_kernel, mes, len(parts), len(gbs), len(dqs)),
        out_shape=outs,
        grid_spec=pltpu.PrefetchScalarGridSpec(
            num_scalar_prefetch=1,
            grid=(steps,),
            in_specs=specs,
            out_specs=[nat] + [full(o.shape) for o in outs[1:]],
            scratch_shapes=[
                pltpu.VMEM((rows + 8, width), F32),
                pltpu.VMEM((3, tile + 16, width), F32),
                pltpu.VMEM((8, ids.shape[1]), F32),
                pltpu.VMEM((8, width), F32),
                pltpu.VMEM((32, depth, 128), LOW),
                pltpu.VMEM((width, 3 * width), F32),
                pltpu.VMEM((width, width), F32),
            ],
        ),
        compiler_params=params(),
        cost_estimate=cost(12),
        name="finish",
    )(info, *operands)


def spread_ffn_kernel(mes, away, info, source, *rest):
    gate_up_ref, down_ref = rest[-2:]
    which = pl.program_id(1)
    turn = info[mes + away] & 7
    for k in range(8):
        col, row = 128 * (k // 2), 256 * (k % 2)
        gate_up_ref[row : row + 256, col : col + 128] = source[
            k ^ turn, pl.ds(pl.multiple_of(which * 256, 256), 256), :
        ].astype(F32)

    @pl.when(which == 0)
    def _():
        for k in range(8):
            col, row = 128 * (k // 2), 256 * (k % 2)
            for part in range(2):
                lane = row + 128 * part
                down_ref[col : col + 128, lane : lane + 128] = source[
                    k ^ turn, 512 + 128 * part : 640 + 128 * part, :
                ].astype(F32)


def spread_ffn(mes, away, info, pieces, width, hidden, into=()):
    steps = hidden // 512
    return pl.pallas_call(
        functools.partial(spread_ffn_kernel, mes, away),
        out_shape=[jax.ShapeDtypeStruct((width, 2 * hidden), F32), jax.ShapeDtypeStruct((hidden, width), F32)],
        grid_spec=pltpu.PrefetchScalarGridSpec(
            num_scalar_prefetch=1,
            grid=(2, 2),
            in_specs=[pl.BlockSpec((8,) + pieces.shape[1:], lambda i, w, info: (i, 0, 0))]
            + [pl.BlockSpec(memory_space=pl.ANY)] * len(into),
            out_specs=[
                pl.BlockSpec((width, 512), lambda i, w, info: (0, w * steps + hidden_block(mes, info, away, i))),
                pl.BlockSpec((512, width), lambda i, w, info: (hidden_block(mes, info, away, i), 0)),
            ],
        ),
        input_output_aliases={2 + j: j for j in range(len(into))},
        compiler_params=params(),
        cost_estimate=cost(5),
        name="spread_ffn",
    )(info, pieces, *into)


def group_of(mes, info, step):
    return (step & 1) ^ (info[mes + step // 2] >> 3)


def spread_kernel(mes, info, own_c, other_c, own_e, other_e, qkv_ref, out_ref, conv_ref, taps_ref, gain_a_ref, gain_f_ref, bias_ref, few):
    step = pl.program_id(0)
    turn = info[mes + step // 2] & 7
    group = group_of(mes, info, step)
    width = out_ref.shape[1]
    places = [(out_ref, 0, width)]
    places_e = [(qkv_ref, 0, 3 * width), (conv_ref, 0, width)]
    for j, pair in enumerate(((own_c, own_e), (other_c, other_e))):

        @pl.when(step // 2 == j)
        def _(pair=pair):
            for source, targets in zip(pair, (places, places_e)):
                for k in range(8):
                    spot = k ^ turn
                    at = 0
                    for out, column, columns in targets:
                        for lane in range(column, column + columns, 128):
                            out[16 * k : 16 * k + 16, lane : lane + 128] = source[spot, at : at + 16, :].astype(F32)
                            at += 16
                    if targets is places_e:
                        few[group, k] = source[spot, at : at + 16, :].astype(F32)

    @pl.when(step == 3)
    def _():
        lines = [
            jnp.concatenate([few[(4 * r + c) // 8, (4 * r + c) % 8, 0:1, :] for c in range(4)], axis=1)
            for r in range(6)
        ]
        for row, line in enumerate((0, 1, 0, 1, 2, 0, 1, 2, 3)):
            taps_ref[row : row + 1, :] = lines[line]
        gain_a_ref[...] = lines[4]
        gain_f_ref[...] = lines[5]
        rows = jnp.concatenate([few[g // 8, g % 8, 1:2, :] for g in range(32)], axis=0)
        bias_ref[...] = rows.T[: bias_ref.shape[0], :]


def spread(mes, info, own_c, other_c, own_e, other_e, width, heads):
    def source(depth, at, j):
        return pl.BlockSpec((8, depth, 128), lambda i, info: (jnp.clip(i - 2 * j, 0, 1), at, 0))

    deep = own_e.shape[1]
    out_at = own_c.shape[1] * 8 // width - 1

    columns = (3 * width, width, width)
    small = [(9, width), (1, width), (1, width), (heads, 32)]
    return pl.pallas_call(
        functools.partial(spread_kernel, mes),
        out_shape=[jax.ShapeDtypeStruct((width, c), F32) for c in columns]
        + [jax.ShapeDtypeStruct(shape, F32) for shape in small],
        grid_spec=pltpu.PrefetchScalarGridSpec(
            num_scalar_prefetch=1,
            grid=(4,),
            in_specs=[source(width // 8, out_at, j) for j in range(2)] + [source(deep, 0, j) for j in range(2)],
            out_specs=[pl.BlockSpec((width // 4, c), lambda i, info: (group_of(mes, info, i), 0)) for c in columns]
            + [full(shape) for shape in small],
            scratch_shapes=[pltpu.VMEM((4, 8, 16, 128), F32)],
        ),
        compiler_params=params(),
        cost_estimate=cost(5),
        name="spread",
    )(info, own_c, other_c, own_e, other_e)


def hop_tables(sizes):
    seq = [sizes["dp"] << b for b in range(sizes["seq"].bit_length() - 1)]
    dp = [1 << b for b in range(1, sizes["dp"].bit_length() - 1)]
    return [1] + seq + dp, [1] + dp[:1] + seq + dp[1:]


def place_of(tables):
    here = lax.axis_index(("seq", "dp"))
    places = []
    for masks in tables:
        me = jnp.int32(0)
        for mask in masks[:5]:
            me = me * 2 + jnp.where((here & mask) != 0, 1, 0)
        places.append(me)
    even = (here & 1) == 0
    return [jnp.where(even, places[0], places[1]), jnp.where(even, places[1], places[0]) ^ 16]


def swap(value, tables, hops):
    count = lax.axis_size(("seq", "dp"))
    masks = [functools.reduce(lambda x, h: x ^ table[h], hops, 0) for table in tables]
    return lax.ppermute(value, ("seq", "dp"), [(i, i ^ masks[i & 1]) for i in range(count)])


def partners(phase):
    sets = [()]
    for hop in phase:
        sets = [s + extra for s in sets for extra in ((), (hop,))]
    return sets[1:]


class Sum:
    def __init__(self, tables, sizes, early, late):
        phases, at = [], 0
        for size in sizes:
            phases.append(tuple(range(at, at + size)))
            at += size
        self.tables = tables
        self.down = phases
        self.across = range(at, len(tables[0]))
        self.value = late
        self.leaving = list(early)
        self.flights = []
        self.stage = 0
        self.other = None

    def combine(self):
        self.stage += 1
        stage, down, across = self.stage, len(self.down), len(self.across)
        if stage <= down + across:
            self.value = functools.reduce(
                jnp.add, [v.astype(F32) for v in [self.value] + self.flights]
            ).astype(LOW)
        else:
            self.value = jnp.concatenate([self.value] + self.flights, axis=0)
        if stage < down:
            count = 1 << len(self.down[stage])
            share = self.value.shape[0] // count
            pieces = [self.value[j * share : (j + 1) * share] for j in range(count)]
            self.value, self.leaving = pieces[0], pieces[1:]

    def launch(self):
        stage, down, across = self.stage, len(self.down), len(self.across)
        if stage < down:
            self.flights = [swap(v, self.tables, m) for v, m in zip(self.leaving, partners(self.down[stage]))]
        elif stage < down + across:
            self.flights = [swap(self.value, self.tables, (self.across[stage - down],))]
        else:
            left = down - 1 - (stage - down - across)
            self.flights = [swap(self.value, self.tables, m) for m in partners(self.down[left])]
            if left == 0:
                self.other = self.flights[0]

    def finish(self):
        while self.other is None:
            step_on([self])

    def held(self):
        sending = self.stage < len(self.down)
        return [self.value] + (self.leaving if sending else [])

    def hold(self, values):
        self.value = values[0]
        if self.stage < len(self.down):
            self.leaving = list(values[1:])


def step_on(sums, fresh=(), ties=(), after=()):
    if after:
        flat = lax.optimization_barrier(tuple(v for r in sums for v in r.flights) + tuple(after))
        at = 0
        for running in sums:
            running.flights = list(flat[at : at + len(running.flights)])
            at += len(running.flights)
        ties = tuple(ties) + tuple(flat[at:])
    for running in sums:
        running.combine()
    moving = list(sums) + list(fresh)
    groups = [running.held() for running in moving]
    flat = lax.optimization_barrier(tuple(v for g in groups for v in g) + tuple(ties))
    at = 0
    for running, group in zip(moving, groups):
        running.hold(flat[at : at + len(group)])
        at += len(group)
        running.launch()
    return flat[at:]


def total(terms):
    if len(terms) == 1:
        return terms[0]
    return functools.reduce(jnp.add, [t.astype(F32) for t in terms]).astype(terms[0].dtype)


def shards(sizes, tokens, word_ids, cotangent, conv_kernels, conv_proj, gain_attn, w_qkv, rel_bias, out_proj, gain_ffn, w_gate_up, w_down):
    seqs, rows, width = tokens.shape
    heads = rel_bias.shape[1]
    pairs = heads // 2
    ring = sizes["seq"]
    me = lax.axis_index("seq")
    tables = hop_tables(sizes)
    info = jnp.stack(
        [((me + k) % ring) * rows for k in range(ring)] + place_of(tables)
    ).astype(jnp.int32)
    mes = ring
    gain_one, gain_two = gain_attn[None, :], gain_ffn[None, :]
    halo = lax.ppermute(tokens[:, rows - 8 :, :], "seq", [(i, (i + 1) % ring) for i in range(ring)])
    halo, travelling = lax.optimization_barrier((halo, tokens))
    block_tokens = [tokens] + [
        lax.ppermute(travelling, "seq", [((i + k) % ring, i) for i in range(ring)]) for k in range(1, ring)
    ]
    halos = [halo] + [b[:, rows - 8 :, :] for b in block_tokens[:-1]]
    units = rows // unit_of(rows)

    parts_of = []
    for s in range(seqs):
        ids = word_ids[s : s + 1]
        own = project(True, 0, info, tokens[s], halos[0][s], ids, conv_kernels, gain_one, conv_proj, w_qkv)
        branch, mixed, normed, query, query_t, key, key_t, value, value_t = own
        held = [(normed, key, key_t, value, value_t)]
        fwd = [attend(0, ids, info, rel_bias.T, key, value_t, query_t)]
        for k in range(1, ring):
            held.append(
                project(False, k, info, block_tokens[k][s], halos[k][s], ids, conv_kernels, gain_one, conv_proj, w_qkv)
            )
            fwd.append(attend(k, ids, info, rel_bias.T, held[k][1], held[k][4], query_t))
        ffn = feed_forward(
            mes, info, [f[1] for f in fwd], [f[2] for f in fwd], branch, out_proj, gain_two, cotangent[s], w_gate_up, w_down, units
        )
        parts_of.append((ids, held, fwd, query, branch, mixed, ffn))

    pieces = [total([p[-1][ring + 5 + j] for p in parts_of]) for j in range(2)]
    sum_a = Sum(tables, (1, 1, 1, 2), [pieces[0]], pieces[1])
    step_on([], [sum_a])

    results, gxs, rets, last_pieces = [], [], [], []
    for s in range(seqs):
        ids, held, fwd, query, branch, mixed, ffn = parts_of[s]
        scales = ffn[:ring]
        result, datt, dout_t, rowdot, dgain = ffn[ring : ring + 5]
        results.append(result)
        def run_back(k, first, count, go, so_far=None):
            return attend_back(
                k, first, count, ids, info, fwd[k][0], held[k][2], held[k][3], query, dout_t, scales[k], go, so_far
            )

        final = s == seqs - 1

        def moved(value, after=()):
            return step_on([sum_a], (), (value,), after) if final else (value,) + tuple(after)

        parts, dw_kvs, gbs, dq_sum = [], [], [], None
        go = moved(rowdot)[0]
        for k in range(1, ring):
            low = run_back(k, 0, pairs - 1, go)
            go, gb_low = rowdot, low[3]
            if k == 1:
                go, gb_low = moved(rowdot, (gb_low,))
            high = run_back(k, pairs - 1, 1, go)
            go = rowdot
            dq_k = [low[0], high[0]]
            dq_sum = dq_k if dq_sum is None else [a + b for a, b in zip(dq_sum, dq_k)]
            dv, gb = low[2], high[3]
            if k == ring - 1:
                dv, gb = moved(dv, (gb,))
            gbs += [gb_low, gb]
            dn, dw_kv = back_other([low[1], high[1]], [dv, high[2]], held[k][0], w_qkv)
            if k == ring - 1:
                dn, go = lax.optimization_barrier((dn, rowdot))
            parts.append(lax.ppermute(dn, "seq", [(i, (i + k) % ring) for i in range(ring)]))
            dw_kvs.append(dw_kv)
        if dq_sum is None:
            dq_sum = [jnp.zeros((width - 128, rows), F32), jnp.zeros((128, rows), F32)]
        dw_kv = total(dw_kvs) if dw_kvs else jnp.zeros((width, 2 * width), LOW)
        own = [run_back(0, 0, 1, go, (dq_sum[0], 0))]
        go, gb = moved(rowdot, (own[0][3],))
        own.append(run_back(0, 1, pairs - 2, go, (dq_sum[0], 1)))
        go, gb_next = moved(rowdot, (own[1][3],))
        own.append(run_back(0, pairs - 1, 1, go, (dq_sum[1], 0)))
        taps, gb_last = moved(conv_kernels, (own[2][3],))
        gbs += [gb, gb_next, gb_last]
        gx, ret, early, late = finish(
            mes, info, parts, gbs, [o[0] for o in own], [o[1] for o in own], [o[2] for o in own], dw_kv,
            held[0][0], branch, datt, mixed, conv_proj, w_qkv, taps, gain_one, ids, tokens[s], halos[0][s], dgain,
        )
        gxs.append(gx)
        rets.append(ret)
        last_pieces.append((early, late))

    early, late = [total([p[j] for p in last_pieces]) for j in range(2)]
    sum_e = Sum(tables, (1, 2, 2), [early], late)
    hidden = w_down.shape[0]
    gxs, ret = step_on([], [sum_e], (jnp.stack(gxs), jnp.stack(rets)))
    returned = lax.ppermute(ret, "seq", [(i, i - 1) for i in range(1, ring)])
    while sum_a.other is None:
        step_on([sum_e, sum_a])
    grads = spread_ffn(mes, 0, info, sum_a.value, width, hidden)
    grads = step_on([sum_e], (), (), grads)
    grad_tokens = gxs.at[:, rows - 8 :, :].add(returned)
    (grad_tokens,) = step_on([sum_e], (), (grad_tokens,))
    last = 2 * len(sum_e.down) + len(sum_e.across) - 1
    while sum_e.stage < last - 1:
        step_on([sum_e])
    grads = spread_ffn(mes, 1, info, sum_a.other, width, hidden, grads)
    grad_gate_up, grad_down = step_on([sum_e], (), (), grads)
    sum_e.finish()
    grad_w_qkv, grad_out_proj, grad_conv_proj, grad_kernels, grad_gain_a, grad_gain_f, grad_bias = spread(
        mes, info, sum_a.value, sum_a.other, sum_e.value, sum_e.other, width, heads
    )
    return (
        jnp.stack(results),
        grad_tokens,
        grad_kernels,
        grad_conv_proj,
        grad_gain_a.reshape(-1),
        grad_w_qkv,
        grad_bias.T,
        grad_out_proj,
        grad_gain_f.reshape(-1),
        grad_gate_up,
        grad_down,
    )


def solution(mesh):
    sizes = dict(mesh.shape)
    split = P("dp", "seq", None)
    in_specs = (split, P("dp", None), split) + (P(),) * 9
    out_specs = (split, split) + (P(),) * 9
    return jax.shard_map(
        functools.partial(shards, sizes), mesh=mesh, in_specs=in_specs, out_specs=out_specs, check_vma=False
    )
```

```python
import functools

import jax
import jax.numpy as jnp
from jax import lax
from jax.experimental import pallas as pl
from jax.experimental.pallas import tpu as pltpu
from jax.sharding import PartitionSpec as P

EVERY = ("seq", "dp")
LOW = jnp.bfloat16
F32 = jnp.float32
EDGES = (1, 2, 3, 4, 5, 6, 7, 8, 11, 16, 22, 32, 45, 64, 91)
KEY_WORDS = 128
QUERY_WORDS = 256
FOLD = 512
VMEM_BYTES = 60 * 2**20


def bucketize(offsets):
    magnitude = jnp.abs(offsets)
    bucketed = jnp.where(offsets > 0, 16, 0).astype(jnp.int32)
    for edge in EDGES:
        bucketed = bucketed + (magnitude >= edge).astype(jnp.int32)
    return bucketed


def dot(a, b):
    return jnp.dot(a, b, preferred_element_type=F32)


def dot_nt(a, b):
    return lax.dot_general(a, b, (((1,), (1,)), ((), ())), preferred_element_type=F32)


def iota(shape, dim):
    return lax.broadcasted_iota(jnp.int32, shape, dim)


def onehot(mask):
    return mask.astype(F32).astype(LOW)


def params(**kw):
    return pltpu.CompilerParams(vmem_limit_bytes=VMEM_BYTES, **kw)


def cost(micros):
    return pl.CostEstimate(flops=int(micros * 1e7), bytes_accessed=int(micros * 1e4), transcendentals=0)


def full(shape):
    return pl.BlockSpec(shape, lambda *_: (0,) * len(shape))


def make_taps(kernels):
    k = kernels.astype(F32)
    return [
        k[0:1] + k[2:3] + k[5:6],
        k[1:2] + k[3:4] + k[6:7],
        k[4:5] + k[7:8],
        k[8:9],
    ]


def same_words(ids):
    place = iota(ids.shape, 1)
    rows = [
        jnp.where((pltpu.roll(ids, back, 1) == ids) & (place >= back), 1.0, 0.0) for back in range(1, 4)
    ]
    return jnp.concatenate([jnp.zeros(ids.shape, F32)] + rows + [jnp.zeros((4, ids.shape[1]), F32)], axis=0)


def project_kernel(own, at, info, x_ref, halo_ref, ids_ref, kernels_ref, gain_ref, conv_ref, w_ref, *rest):
    step = pl.program_id(0)
    tile = rest[0].shape[0]
    ext, masks = rest[-2:]
    width = x_ref.shape[1]

    @pl.when(step == 0)
    def _():
        ext[0:8, :] = halo_ref[...].astype(F32)
        ext[8:, :] = x_ref[...].astype(F32)
        masks[...] = same_words(ids_ref[...])

    start = pl.multiple_of(step * tile, tile)
    chunk = ext[pl.ds(start, tile + 8), :]
    lane = pl.multiple_of(info[at] + step * tile, tile)
    same = masks[:, pl.ds(lane, tile)].T
    taps = make_taps(kernels_ref[...])
    inputs = chunk[8:, :]
    mixed = taps[0] * inputs
    for back in range(1, 4):
        mixed = mixed + taps[back] * chunk[8 - back : 8 - back + tile, :] * same[:, back : back + 1]
    mixed_low = mixed.astype(LOW)
    branch = inputs + dot(mixed_low, conv_ref[...])
    factor = lax.rsqrt(jnp.mean(branch * branch, axis=-1, keepdims=True) + 1e-06)
    normed = (branch * factor * gain_ref[...].astype(F32)[0:1, :]).astype(LOW)
    if own:
        branch_ref, mixed_ref, n_ref, q_ref, qt_ref, k_ref, kt_ref, v_ref, vt_ref = rest[:-2]
        qkv = dot(normed, w_ref[...]).astype(LOW)
        query = qkv[:, :width] * jnp.asarray(0.125, LOW)
        q_ref[...] = query
        qt_ref[...] = query.T
        branch_ref[...] = branch
        mixed_ref[...] = mixed_low
        key, value = qkv[:, width : 2 * width], qkv[:, 2 * width :]
    else:
        n_ref, k_ref, kt_ref, v_ref, vt_ref = rest[:-2]
        kv = dot(normed, w_ref[:, width:]).astype(LOW)
        key, value = kv[:, :width], kv[:, width:]
    n_ref[...] = normed
    k_ref[...] = key
    kt_ref[...] = key.T
    v_ref[...] = value
    vt_ref[...] = value.T


def project(own, at, info, x, halo, ids, kernels, gain, conv_proj, w_qkv):
    rows, width = x.shape
    tile = min(512, rows)
    nat = pl.BlockSpec((tile, width), lambda i, *_: (i, 0))
    tra = pl.BlockSpec((width, tile), lambda i, *_: (0, i))
    nat_low = jax.ShapeDtypeStruct((rows, width), LOW)
    tra_low = jax.ShapeDtypeStruct((width, rows), LOW)
    nat_f32 = jax.ShapeDtypeStruct((rows, width), F32)
    if own:
        outs = [(nat_f32, nat), (nat_low, nat), (nat_low, nat), (nat_low, nat), (tra_low, tra)]
    else:
        outs = [(nat_low, nat)]
    outs = outs + [(nat_low, nat), (tra_low, tra), (nat_low, nat), (tra_low, tra)]
    operands = (x, halo, ids, kernels, gain, conv_proj, w_qkv)
    return pl.pallas_call(
        functools.partial(project_kernel, own, at),
        out_shape=[s for s, _ in outs],
        grid_spec=pltpu.PrefetchScalarGridSpec(
            num_scalar_prefetch=1,
            grid=(rows // tile,),
            in_specs=[full(o.shape) for o in operands],
            out_specs=[b for _, b in outs],
            scratch_shapes=[pltpu.VMEM((rows + 8, width), F32), pltpu.VMEM((8, ids.shape[1]), F32)],
        ),
        compiler_params=params(),
        cost_estimate=cost(8 if own else 6),
        name="project_own" if own else "project_other",
    )(info, *operands)


def word_spans(ids, q_off, k_off, rows_q, rows_k, unit):
    q_first = ids[0, q_off]
    q_wins = (ids[0, q_off + rows_q - 1] - q_first) // QUERY_WORDS + 1
    firsts, wins = [], []
    for at in range(0, rows_k, unit):
        first = ids[0, k_off + at]
        firsts.append(first)
        wins.append((ids[0, k_off + at + unit - 1] - first) // KEY_WORDS + 1)
    fits = q_wins == 1
    for count in wins:
        fits = jnp.logical_and(fits, count == 1)
    return q_first, q_wins, firsts, wins, fits


def unit_of(rows_k):
    return min(512, rows_k)


def stat_rows(rows_k):
    return -(-(2 * (rows_k // unit_of(rows_k)) + 4) // 8) * 8


def attend_kernel(rows_q, rows_k, spot, ids, info, ids_ref, bias_ref, k_ref, vt_ref, qt_ref, p_ref, o_ref, stat_ref, eqt, ek, bidx, raw, tab_ref, parts, flag):
    pair = pl.program_id(0)
    unit = unit_of(rows_k)
    units = rows_k // unit
    q_off, k_off = info[0], info[spot]
    q_first, q_wins, firsts, wins, fits = word_spans(ids, q_off, k_off, rows_q, rows_k, unit)
    q_ids = ids_ref[:, pl.ds(pl.multiple_of(q_off, 128), rows_q)]

    def unit_ids(at):
        return ids_ref[:, pl.ds(pl.multiple_of(k_off + at * unit, 128), unit)]

    def query_words(win):
        return onehot(iota((QUERY_WORDS, rows_q), 0) + (q_first + win * QUERY_WORDS) == q_ids)

    def key_words(at, win):
        return onehot(iota((KEY_WORDS, unit), 0) + (firsts[at] + win * KEY_WORDS) == unit_ids(at)).T

    def buckets(at, win, q_win):
        shift = firsts[at] + win * KEY_WORDS - q_first - q_win * QUERY_WORDS
        shape = (KEY_WORDS, QUERY_WORDS)
        return bucketize(shift + iota(shape, 0) - iota(shape, 1))

    def window_bias(head, index):
        row = jnp.broadcast_to(tab_ref[pl.ds(head, 1), :], (KEY_WORDS, 128))
        parts = [
            jnp.take_along_axis(row, index[:, c : c + 128], axis=1) for c in range(0, QUERY_WORDS, 128)
        ]
        return jnp.concatenate(parts, axis=1).astype(LOW)

    @pl.when(pair == 0)
    def _():
        eqt[...] = query_words(0)
        tab_ref[:, : bias_ref.shape[1]] = bias_ref[...].astype(F32)
        for at in range(units):
            ek[at * unit : (at + 1) * unit, :] = key_words(at, 0)
            bidx[at] = buckets(at, 0, 0)

    def queries(side):
        zero = jnp.zeros((64, rows_q), LOW)
        mine = qt_ref[64 * side : 64 * side + 64, :]
        return [mine, zero] if side == 0 else [zero, mine]

    def window_rows(at):
        bias = jnp.concatenate([window_bias(2 * pair + side, bidx[at]) for side in range(2)], axis=0)
        return dot(bias, eqt[...]).astype(LOW)

    def fast_scores(side, at, spread):
        rows = slice(at * unit, (at + 1) * unit)
        mine = spread[KEY_WORDS * side : KEY_WORDS * side + KEY_WORDS, :]
        right = jnp.concatenate(queries(side) + [mine], axis=0)
        left = jnp.concatenate([k_ref[rows, :], ek[rows, :]], axis=1)
        return dot(left, right)

    def slow_scores(side, at):
        rows = slice(at * unit, (at + 1) * unit)
        raw[...] = dot(k_ref[rows, :], jnp.concatenate(queries(side), axis=0))

        def over_keys(win, carry):
            def over_queries(q_win, inner):
                bias = window_bias(2 * pair + side, buckets(at, win, q_win))
                spread = dot(bias, query_words(q_win)).astype(LOW)
                raw[...] += dot(key_words(at, win), spread)
                return inner

            return lax.fori_loop(0, q_wins, over_queries, carry)

        lax.fori_loop(0, wins[at], over_keys, 0)
        return raw[...]

    jobs = [(side, at) for side in range(2) for at in range(units)]

    def softmax_part(job, score):
        side, at = job
        rows = slice(at * unit, (at + 1) * unit)
        top = jnp.max(score, axis=0, keepdims=True)
        expo = jnp.exp(score - top).astype(LOW)
        p_ref[side, rows, :] = expo
        left = jnp.concatenate([vt_ref[64 * side : 64 * side + 64, rows], jnp.ones((16, unit), LOW)], axis=0)
        parts[side * units + at] = dot(left, expo)
        stat_ref[0, side * units + at : side * units + at + 1, :] = top

    def merge():
        for side in range(2):
            tops = [stat_ref[0, side * units + at : side * units + at + 1, :] for at in range(units)]
            peak = functools.reduce(jnp.maximum, tops)
            total = functools.reduce(
                jnp.add, [parts[side * units + at] * jnp.exp(tops[at] - peak) for at in range(units)]
            )
            o_ref[64 * side : 64 * side + 64, :] = total[:64, :]
            stat_ref[0, 2 * units + side : 2 * units + side + 1, :] = peak
            stat_ref[0, 2 * units + 2 + side : 2 * units + 3 + side, :] = total[64:65, :]

    def run_fast():
        stat_ref[...] = jnp.zeros_like(stat_ref)
        least = most = None
        spreads = [window_rows(at) for at in range(units)]
        for side, at in jobs:
            rows = slice(at * unit, (at + 1) * unit)
            expo = jnp.exp(fast_scores(side, at, spreads[at])).astype(LOW)
            p_ref[side, rows, :] = expo
            left = jnp.concatenate([vt_ref[64 * side : 64 * side + 64, rows], jnp.ones((16, unit), LOW)], axis=0)
            part = dot(left, expo)
            parts[side * units + at] = part
            sums = part[64:65, :]
            least = sums if least is None else jnp.minimum(least, sums)
            most = sums if most is None else jnp.maximum(most, sums)
        return jnp.logical_and(jnp.min(least) > 1e-25, jnp.max(most) < 1e25)

    def run_slow():
        for job in jobs:
            softmax_part(job, slow_scores(*job))

    flag[0] = 0

    @pl.when(fits)
    def _():
        flag[0] = run_fast().astype(jnp.int32)

    @pl.when(flag[0] == 0)
    def _():
        run_slow()

    merge()


def attend(spot, ids, info, rel_bias, key, value_t, query_t):
    rows_k, width = key.shape
    rows_q = query_t.shape[1]
    length = ids.shape[1]
    unit = unit_of(rows_k)
    units = rows_k // unit
    stats = stat_rows(rows_k)
    pairs = width // 128
    return pl.pallas_call(
        functools.partial(attend_kernel, rows_q, rows_k, spot),
        out_shape=[
            jax.ShapeDtypeStruct((2 * pairs, rows_k, rows_q), LOW),
            jax.ShapeDtypeStruct((width, rows_q), F32),
            jax.ShapeDtypeStruct((pairs, stats, rows_q), F32),
        ],
        grid_spec=pltpu.PrefetchScalarGridSpec(
            num_scalar_prefetch=2,
            grid=(pairs,),
            in_specs=[
                full((1, length)),
                full(rel_bias.shape),
                pl.BlockSpec((rows_k, 128), lambda p, *_: (0, p)),
                pl.BlockSpec((128, rows_k), lambda p, *_: (p, 0)),
                pl.BlockSpec((128, rows_q), lambda p, *_: (p, 0)),
            ],
            out_specs=[
                pl.BlockSpec((2, rows_k, rows_q), lambda p, *_: (p, 0, 0)),
                pl.BlockSpec((128, rows_q), lambda p, *_: (p, 0)),
                pl.BlockSpec((1, stats, rows_q), lambda p, *_: (p, 0, 0)),
            ],
            scratch_shapes=[
                pltpu.VMEM((QUERY_WORDS, rows_q), LOW),
                pltpu.VMEM((rows_k, KEY_WORDS), LOW),
                pltpu.VMEM((units, KEY_WORDS, QUERY_WORDS), jnp.int32),
                pltpu.VMEM((unit, rows_q), F32),
                pltpu.VMEM((2 * pairs, 128), F32),
                pltpu.VMEM((2 * units, 80, rows_q), F32),
                pltpu.SMEM((1,), jnp.int32),
            ],
        ),
        compiler_params=params(),
        cost_estimate=cost(20),
        name="attend",
    )(ids, info, ids, rel_bias, key, value_t, query_t)


def attend_back_kernel(rows_q, rows_k, spot, first_pair, last, ids, info, ids_ref, p_ref, kt_ref, v_ref, q_ref, dot_ref, cs_ref, rd_ref, *rest):
    if last:
        so_far_ref, rest = rest[0], rest[1:]
    dq_ref, dk_ref, dv_ref, gb_ref, eq, ekt, bmask, spread, held, by_word = rest[:10]
    dq_acc = rest[10] if last else dq_ref
    at = pl.program_id(1)
    pair = first_pair + pl.program_id(0)
    unit = unit_of(rows_k)
    units = rows_k // unit
    q_off, k_off = info[0], info[spot]
    q_first = ids[0, q_off]
    q_wins = (ids[0, q_off + rows_q - 1] - q_first) // QUERY_WORDS + 1
    q_ids = ids_ref[:, pl.ds(pl.multiple_of(q_off, 128), rows_q)]

    def query_words(win):
        return onehot(iota((QUERY_WORDS, rows_q), 0) + (q_first + win * QUERY_WORDS) == q_ids).T

    def first_word(index):
        return ids[0, k_off + index * unit]

    def key_words(index, win):
        k_ids = ids_ref[:, pl.ds(pl.multiple_of(k_off + index * unit, 128), unit)]
        return onehot(iota((KEY_WORDS, unit), 0) + (first_word(index) + win * KEY_WORDS) == k_ids)

    def bucket_mask(index, win, q_win):
        lane = iota((32, FOLD), 1)
        ahead = jnp.where(lane < FOLD - KEY_WORDS, lane, lane - FOLD)
        shift = first_word(index) + win * KEY_WORDS - q_first - q_win * QUERY_WORDS
        return (bucketize(shift - ahead) == iota((32, FOLD), 0)).astype(F32)

    @pl.when(jnp.logical_and(at == 0, pl.program_id(0) == 0))
    def _():
        eq[...] = query_words(0)
        gb_ref[...] = jnp.zeros_like(gb_ref)
        spread[...] = jnp.zeros_like(spread)
        for index in range(units):
            ekt[index] = key_words(index, 0)
            bmask[index] = bucket_mask(index, 0, 0)

    def fold(grids, mask, heads):
        half = KEY_WORDS // 2
        while half >= 8:
            grids = [g[:half, :] + pltpu.roll(g[half:, :], FOLD - half, 1) for g in grids]
            half //= 2
        row = iota((8, FOLD), 0)
        for bit in (4, 2, 1):
            grids = [jnp.where((row & bit) != 0, pltpu.roll(g, FOLD - bit, 1), g) for g in grids]
        sums = [jnp.sum(mask * jnp.sum(g, axis=0, keepdims=True), axis=1, keepdims=True) for g in grids]
        place = iota(gb_ref.shape, 1)
        gb_ref[...] += functools.reduce(
            jnp.add, [jnp.where(place == head, s, 0.0) for head, s in zip(heads, sums)]
        )

    def scale_row(side):
        return cs_ref[0, pl.ds(side * units + at, 1), :]

    def scaled_dout(side):
        return (dot_ref[64 * side : 64 * side + 64, :].astype(F32) * scale_row(side)).astype(LOW)

    def grad_scores(side, scaled):
        zero = jnp.zeros((64, rows_q), LOW)
        rowdot = rd_ref[pl.ds(2 * pair + side, 1), :] * scale_row(side)
        right = jnp.concatenate([scaled, zero] if side == 0 else [zero, scaled], axis=0)
        grad_p = dot(v_ref[...], right)
        return (p_ref[side].astype(F32) * (grad_p - rowdot)).astype(LOW)

    scaled = [scaled_dout(side) for side in range(2)]
    natural = jnp.concatenate(scaled, axis=0).T
    dks, dvs, dqs, by_words = [], [], [], []
    for side in range(2):
        ds = grad_scores(side, scaled[side])
        key_t = kt_ref[64 * side : 64 * side + 64, :]
        both = dot(jnp.concatenate([key_t, ekt[at]], axis=0), ds)
        dqs.append(both[:64, :])
        by_words.append(both[64:, :].astype(LOW))
        dvs.append(dot(p_ref[side], natural))
        dks.append(dot(ds, q_ref[...]))
    grid = dot(jnp.concatenate(by_words, axis=0), eq[...])
    grid = jnp.concatenate([grid, jnp.zeros((2 * KEY_WORDS, FOLD - QUERY_WORDS), F32)], axis=1)
    fold([grid[:KEY_WORDS, :], grid[KEY_WORDS:, :]], bmask[at], [2 * pair, 2 * pair + 1])
    first = iota((unit, 128), 1) < 64
    dk_ref[...] = jnp.where(first, dks[0], dks[1]).astype(LOW)
    dv_ref[...] = jnp.where(first, dvs[0], dvs[1]).astype(LOW)

    @pl.when(at == 0)
    def _():
        grads = jnp.concatenate(dqs, axis=0)
        dq_acc[...] = so_far_ref[...] + grads if last else grads

    @pl.when(at > 0)
    def _():
        dq_acc[...] += jnp.concatenate(dqs, axis=0)

    if last:

        @pl.when(at == units - 1)
        def _():
            dq_ref[...] = (dq_acc[...] * 0.125).astype(LOW)

    k_wins = (ids[0, k_off + at * unit + unit - 1] - first_word(at)) // KEY_WORDS + 1

    @pl.when(jnp.logical_or(q_wins > 1, k_wins > 1))
    def _():
        for side in range(2):
            held[...] = grad_scores(side, scaled_dout(side))

            def over_keys(win, carry, side=side):
                by_word[...] = dot(key_words(at, win), held[...]).astype(LOW)

                def over_queries(q_win, inner):
                    spread[:, :QUERY_WORDS] = dot(by_word[...], query_words(q_win))
                    fold([spread[...]], bucket_mask(at, win, q_win), [2 * pair + side])
                    return inner

                return lax.fori_loop(jnp.where(win == 0, 1, 0), q_wins, over_queries, carry)

            lax.fori_loop(0, k_wins, over_keys, 0)


def attend_back(spot, first_pair, pairs, ids, info, p, key_t, value, query, dout_t, scales, rowdot, so_far=None):
    width, rows_k = key_t.shape
    rows_q = query.shape[0]
    length = ids.shape[1]
    unit = unit_of(rows_k)
    units = rows_k // unit
    stats = scales.shape[1]
    last = so_far is not None
    so_far, skip = so_far if last else (None, 0)
    dq_spec = pl.BlockSpec((128, rows_q), lambda g, i, *_: (g, 0))
    return pl.pallas_call(
        functools.partial(attend_back_kernel, rows_q, rows_k, spot, first_pair, last),
        out_shape=[
            jax.ShapeDtypeStruct((128 * pairs, rows_q), LOW if last else F32),
            jax.ShapeDtypeStruct((rows_k, 128 * pairs), LOW),
            jax.ShapeDtypeStruct((rows_k, 128 * pairs), LOW),
            jax.ShapeDtypeStruct((32, 128), F32),
        ],
        grid_spec=pltpu.PrefetchScalarGridSpec(
            num_scalar_prefetch=2,
            grid=(pairs, units),
            in_specs=[
                full((1, length)),
                pl.BlockSpec((2, unit, rows_q), lambda g, i, *_: (first_pair + g, i, 0)),
                pl.BlockSpec((128, unit), lambda g, i, *_: (first_pair + g, i)),
                pl.BlockSpec((unit, 128), lambda g, i, *_: (i, first_pair + g)),
                pl.BlockSpec((rows_q, 128), lambda g, i, *_: (0, first_pair + g)),
                pl.BlockSpec((128, rows_q), lambda g, i, *_: (first_pair + g, 0)),
                pl.BlockSpec((1, stats, rows_q), lambda g, i, *_: (first_pair + g, 0, 0)),
                full(rowdot.shape),
            ]
            + [pl.BlockSpec((128, rows_q), lambda g, i, *_: (skip + g, 0))] * last,
            out_specs=[
                dq_spec,
                pl.BlockSpec((unit, 128), lambda g, i, *_: (i, g)),
                pl.BlockSpec((unit, 128), lambda g, i, *_: (i, g)),
                full((32, 128)),
            ],
            scratch_shapes=[
                pltpu.VMEM((rows_q, QUERY_WORDS), LOW),
                pltpu.VMEM((units, KEY_WORDS, unit), LOW),
                pltpu.VMEM((units, 32, FOLD), F32),
                pltpu.VMEM((KEY_WORDS, FOLD), F32),
                pltpu.VMEM((unit, rows_q), LOW),
                pltpu.VMEM((KEY_WORDS, rows_q), LOW),
            ]
            + [pltpu.VMEM((128, rows_q), F32)] * last,
        ),
        compiler_params=params(),
        cost_estimate=cost(7 * pairs),
        name="attend_back",
    )(*((ids, info, ids, p, key_t, value, query, dout_t, scales, rowdot) + ((so_far,) if last else ())))


def norm_back(v, gain, incoming):
    factor = lax.rsqrt(jnp.mean(v * v, axis=-1, keepdims=True) + 1e-06)
    scaled = incoming * gain
    inner = jnp.mean(scaled * v, axis=-1, keepdims=True)
    back = factor * scaled - v * (factor * factor * factor * inner)
    return back, jnp.sum(incoming * v * factor, axis=0, keepdims=True)


def ffn_kernel(blocks, units, mes, info, *refs):
    step = pl.program_id(0)
    outs, stats = refs[:blocks], refs[blocks : 2 * blocks]
    branch_ref, out_proj_ref, gain_ref, cot_ref, wg_ref, wu_ref, wd_ref = refs[2 * blocks : 2 * blocks + 7]
    rest = refs[2 * blocks + 7 :]
    scales = rest[:blocks]
    result_ref, datt_ref, dout_ref, rd_ref, dgain_ref = rest[blocks : blocks + 5]
    pieces = rest[blocks + 5 : blocks + 7]
    attn, attn_low, after, n2, n2t, y_acc, dn_acc, packed, held, sems = rest[blocks + 7 :]
    heads = attn.shape[0] // 64
    chunk = wg_ref.shape[1]
    rows = after.shape[0]

    @pl.when(step == 0)
    def _():
        for head in range(heads):
            pair, side = head // 2, head % 2
            peaks = [s[pair, 2 * units + side : 2 * units + side + 1, :] for s in stats]
            top = functools.reduce(jnp.maximum, peaks)
            shares = [jnp.exp(peak - top) for peak in peaks]
            sums = [s[pair, 2 * units + 2 + side : 2 * units + 3 + side, :] for s in stats]
            inverse = 1.0 / functools.reduce(jnp.add, [a * b for a, b in zip(shares, sums)])
            band = slice(64 * head, 64 * head + 64)
            attn[band, :] = functools.reduce(
                jnp.add, [o[band, :] * (share * inverse) for o, share in zip(outs, shares)]
            )
            for s, c in zip(stats, scales):
                c[pair, side * units : (side + 1) * units, :] = (
                    jnp.exp(s[pair, side * units : (side + 1) * units, :] - top) * inverse
                )
        attn_low[...] = attn[...].astype(LOW)
        joined = branch_ref[...] + dot(attn_low[...].T, out_proj_ref[...])
        after[...] = joined
        factor = lax.rsqrt(jnp.mean(joined * joined, axis=-1, keepdims=True) + 1e-06)
        normed = (joined * factor * gain_ref[...].astype(F32)[1:2, :]).astype(LOW)
        n2[...] = normed
        n2t[...] = normed.T

    weights = jnp.concatenate([wg_ref[...], wu_ref[...]], axis=1)
    both = dot(n2[...], weights)
    gate, up = both[:, :chunk], both[:, chunk:]
    grad_hidden = dot_nt(cot_ref[...], wd_ref[...])
    square = gate * gate
    inner = gate * (0.7978845608028654 + (0.7978845608028654 * 0.044715) * square)
    part = 0.5 + 0.5 * jnp.tanh(inner)
    act = gate * part
    slope = part + 2.0 * act * (1.0 - part) * (
        0.7978845608028654 + (3.0 * 0.7978845608028654 * 0.044715) * square
    )
    hidden = (act * up).astype(LOW)
    grad_both = jnp.concatenate(
        [(grad_hidden * up * slope).astype(LOW), (grad_hidden * act).astype(LOW)], axis=1
    )
    y_part = dot(hidden, wd_ref[...])
    dn_part = dot_nt(grad_both, weights)

    @pl.when(step == 0)
    def _():
        y_acc[...] = y_part
        dn_acc[...] = dn_part

    @pl.when(step > 0)
    def _():
        y_acc[...] += y_part
        dn_acc[...] += dn_part

    grad_w = dot(n2t[...], grad_both).astype(LOW)
    grad_d = dot(hidden.T, cot_ref[...]).astype(LOW)
    turn = info[mes + 1 - step // 2] & 7

    def leaving(j):
        target = pieces[j // 2].at[8 * (j % 2) : 8 * (j % 2) + 8, 0:768, :]
        return pltpu.make_async_copy(held.at[j % 2], target, sems.at[j % 2])

    for j in range(4):

        @pl.when(step == j)
        def _(j=j):
            if j >= 2:
                leaving(j - 2).wait()
            for k in range(8):
                col, row = 128 * (k // 2), 256 * (k % 2)
                spot = k ^ turn
                held[j % 2, spot, 0:256, :] = grad_w[row : row + 256, col : col + 128]
                held[j % 2, spot, 256:512, :] = grad_w[row : row + 256, chunk + col : chunk + col + 128]
                held[j % 2, spot, 512:640, :] = grad_d[col : col + 128, row : row + 128]
                held[j % 2, spot, 640:768, :] = grad_d[col : col + 128, row + 128 : row + 256]
            leaving(j).start()

    @pl.when(step == pl.num_programs(0) - 1)
    def _():
        result_ref[...] = (after[...] + y_acc[...]).astype(LOW)
        back, dgain = norm_back(after[...], gain_ref[...].astype(F32)[1:2, :], dn_acc[...])
        datt = cot_ref[...].astype(F32) + back
        datt_ref[...] = datt
        dgain_ref[...] = jnp.broadcast_to(dgain, dgain_ref.shape)
        datt_low = datt.astype(LOW)
        dout = dot_nt(out_proj_ref[...], datt_low).astype(LOW)
        dout_ref[...] = dout
        pack(packed, 0, dot(attn_low[...], datt_low).astype(LOW), mes, info)
        rest_of = [
            pltpu.make_async_copy(packed.at[16 - 16 * j : 32 - 16 * j], pieces[j].at[:, 768:, :], sems.at[2 + j])
            for j in range(2)
        ]
        for copy in rest_of:
            copy.start()
        prod = dout.astype(F32) * attn[...]
        for head in range(heads):
            rd_ref[head : head + 1, :] = jnp.sum(prod[64 * head : 64 * head + 64, :], axis=0, keepdims=True)
        for copy in rest_of + [leaving(2), leaving(3)]:
            copy.wait()


def hidden_block(mes, info, away, position):
    place = info[mes + away] >> 3
    return 2 * (place >> 1) + (position ^ (place & 1))


def feed_forward(mes, info, outs, stats, branch, out_proj, gain, cot, w_gate_up, w_down, units):
    rows, width = branch.shape
    hidden = w_down.shape[0]
    chunk = 512
    steps = hidden // chunk
    blocks = len(outs)
    heads = width // 64
    once = lambda shape: pl.BlockSpec(shape, lambda *_: (0,) * len(shape), pipeline_mode=pl.Buffered(1))
    nat = (rows, width)

    def block(i, info):
        return hidden_block(mes, info, 1 - i // 2, i % 2)

    pieces = [(16, 768 + width // 8, 128)] * 2
    return pl.pallas_call(
        functools.partial(ffn_kernel, blocks, units, mes),
        out_shape=[jax.ShapeDtypeStruct(s.shape, F32) for s in stats]
        + [
            jax.ShapeDtypeStruct(nat, LOW),
            jax.ShapeDtypeStruct(nat, F32),
            jax.ShapeDtypeStruct((width, rows), LOW),
            jax.ShapeDtypeStruct((heads, rows), F32),
            jax.ShapeDtypeStruct((8, width), F32),
        ]
        + [jax.ShapeDtypeStruct(p, LOW) for p in pieces],
        grid_spec=pltpu.PrefetchScalarGridSpec(
            num_scalar_prefetch=1,
            grid=(steps,),
            in_specs=[once(o.shape) for o in outs]
            + [once(s.shape) for s in stats]
            + [
                once(nat),
                once((width, width)),
                once(gain.shape),
                once(nat),
                pl.BlockSpec((width, chunk), lambda i, info: (0, block(i, info))),
                pl.BlockSpec((width, chunk), lambda i, info: (0, block(i, info) + steps)),
                pl.BlockSpec((chunk, width), lambda i, info: (block(i, info), 0)),
            ],
            out_specs=[once(s.shape) for s in stats]
            + [
                once(nat),
                once(nat),
                once((width, rows)),
                once((heads, rows)),
                once((8, width)),
            ]
            + [pl.BlockSpec(memory_space=pl.ANY)] * len(pieces),
            scratch_shapes=[
                pltpu.VMEM((width, rows), F32),
                pltpu.VMEM((width, rows), LOW),
                pltpu.VMEM(nat, F32),
                pltpu.VMEM(nat, LOW),
                pltpu.VMEM((width, rows), LOW),
                pltpu.VMEM(nat, F32),
                pltpu.VMEM(nat, F32),
                pltpu.VMEM((32, width // 8, 128), LOW),
                pltpu.VMEM((2, 8, 768, 128), LOW),
                pltpu.SemaphoreType.DMA((4,)),
            ],
        ),
        compiler_params=params(),
        cost_estimate=cost(35),
        name="feed_forward",
    )(info, *outs, *stats, branch, out_proj, gain, cot, w_gate_up, w_gate_up, w_down)


def back_other_kernel(count, *refs):
    dks, dvs = refs[:count], refs[count : 2 * count]
    n_ref, w_ref, dn_ref, dw_ref, acc = refs[2 * count :]
    width = n_ref.shape[1]
    both = jnp.concatenate([r[...] for r in dks + dvs], axis=1)
    dn_ref[...] = dot_nt(both, w_ref[:, width:]).astype(LOW)
    part = dot(n_ref[...].T, both)

    @pl.when(pl.program_id(0) == 0)
    def _():
        acc[...] = part

    @pl.when(pl.program_id(0) > 0)
    def _():
        acc[...] += part

    @pl.when(pl.program_id(0) == pl.num_programs(0) - 1)
    def _():
        dw_ref[...] = acc[...].astype(LOW)


def back_other(dks, dvs, normed, w_qkv):
    rows, width = normed.shape
    tile = min(512, rows)
    nat = pl.BlockSpec((tile, width), lambda i: (i, 0))
    return pl.pallas_call(
        functools.partial(back_other_kernel, len(dks)),
        grid=(rows // tile,),
        out_shape=[jax.ShapeDtypeStruct((rows, width), LOW), jax.ShapeDtypeStruct((width, 2 * width), LOW)],
        in_specs=[pl.BlockSpec((tile, d.shape[1]), lambda i: (i, 0)) for d in dks + dvs] + [nat, full(w_qkv.shape)],
        out_specs=[nat, full((width, 2 * width))],
        scratch_shapes=[pltpu.VMEM((width, 2 * width), F32)],
        compiler_params=params(),
        cost_estimate=cost(5),
        name="back_other",
    )(*dks, *dvs, normed, w_qkv)


def packed_at(g, mes, info):
    here = g ^ info[mes]
    return jnp.where(here < 16, here, 16 + (g ^ info[mes + 1]))


def pack(out, at, value, mes, info):
    rows = value.shape[0] // 32
    for g in range(32):
        for lane in range(value.shape[1] // 128):
            start = at + lane * rows
            out[packed_at(g, mes, info), start : start + rows, :] = value[g * rows : (g + 1) * rows, lane * 128 : (lane + 1) * 128]


def finish_kernel(mes, parts_count, few, calls, info, *refs):
    parts, gbs = refs[:parts_count], refs[parts_count : parts_count + few]
    at = parts_count + few
    dqs, dks, dvs = (refs[at + calls * j : at + calls * (j + 1)] for j in range(3))
    rest = refs[at + 3 * calls :]
    dwkv_ref, n_ref, branch_ref, datt_ref, mixed_ref, conv_ref, w_ref, kernels_ref, gain_ref, ids_ref, x_ref, halo_ref, dgain_ref = rest[:13]
    gx_ref, ret_ref, early, late, ext, edge, masks, small, packed, dw_acc, conv_acc = rest[13:]
    step = pl.program_id(0)
    steps = pl.num_programs(0)
    tile, width = branch_ref.shape
    taps = make_taps(kernels_ref[...])

    @pl.when(step == 0)
    def _():
        masks[...] = same_words(ids_ref[...])
        ext[0:8, :] = halo_ref[...].astype(F32)
        ext[8:, :] = x_ref[...].astype(F32)
        for j in range(3):
            edge[j, tile + 8 :, :] = jnp.zeros((8, width), F32)
            edge[j, 0:8, :] = jnp.zeros((8, width), F32)
        small[...] = jnp.zeros_like(small)
        small[5:6, :] = dgain_ref[0:1, :]
        conv_acc[...] = jnp.zeros_like(conv_acc)

    dq = jnp.concatenate([r[...] for r in dqs], axis=0).T
    dqkv = jnp.concatenate([dq] + [r[...] for r in dks + dvs], axis=1)
    dn = dot_nt(dqkv, w_ref[...])
    for part in parts:
        dn = dn + part[...].astype(F32)
    dw = dot(n_ref[...].T, dqkv)

    @pl.when(step == 0)
    def _():
        dw_acc[...] = dw

    @pl.when(step > 0)
    def _():
        dw_acc[...] += dw

    back, dgain = norm_back(branch_ref[...], gain_ref[...].astype(F32)[0:1, :], dn)
    dbranch = datt_ref[...] + back
    dbranch_low = dbranch.astype(LOW)
    conv_acc[...] += dot(mixed_ref[...].T, dbranch_low)
    dmixed = dot_nt(dbranch_low, conv_ref[...])
    at = pl.multiple_of((steps - 1 - step) * tile, tile)
    same = masks[:, pl.ds(pl.multiple_of(info[0] + at, 128), tile)].T
    inputs = ext[pl.ds(at, tile + 8), :]
    small[4:5, :] += dgain
    grad = dbranch + taps[0] * dmixed
    small[0:1, :] += jnp.sum(dmixed * inputs[8:, :], axis=0, keepdims=True)
    returned = jnp.zeros((8, width), F32)
    for back_by in range(1, 4):
        masked = dmixed * same[:, back_by : back_by + 1]
        small[back_by : back_by + 1, :] += jnp.sum(masked * inputs[8 - back_by : 8 - back_by + tile, :], axis=0, keepdims=True)
        j = back_by - 1
        edge[j, 8 : 8 + tile, :] = masked
        grad = grad + taps[back_by] * edge[j, 8 + back_by : 8 + back_by + tile, :]
        returned = returned + taps[back_by] * edge[j, back_by : back_by + 8, :]
        edge[j, tile + 8 :, :] = masked[0:8, :]
    gx_ref[...] = grad
    ret_ref[...] = returned

    @pl.when(step == steps - 1)
    def _():
        pack(packed, 0, dw_acc[:, :width].astype(LOW), mes, info)
        pack(packed, width // 8, (dw_acc[:, width:] + dwkv_ref[...].astype(F32)).astype(LOW), mes, info)
        depth = 3 * width // 8
        pack(packed, depth, conv_acc[...].astype(LOW), mes, info)
        depth += width // 8
        gb = functools.reduce(jnp.add, [r[...] for r in gbs])
        for g in range(32):
            lane = 128 * (g % 4)
            line = jnp.concatenate(
                [small[g // 4 : g // 4 + 1, lane : lane + 128], gb[g : g + 1, :], jnp.zeros((14, 128), F32)], axis=0
            )
            packed[packed_at(g, mes, info), depth : depth + 16, :] = line.astype(LOW)
        early[...] = packed[16:]
        late[...] = packed[:16]


def finish(mes, info, parts, gbs, dqs, dks, dvs, dw_kv, normed, branch, datt, mixed, conv_proj, w_qkv, kernels, gain, ids, x, halo, dgain):
    rows, width = branch.shape
    tile = min(1024, rows)
    steps = rows // tile
    depth = 4 * width // 8 + 16
    nat = pl.BlockSpec((tile, width), lambda i, *_: (steps - 1 - i, 0))
    operands = (*parts, *gbs, *dqs, *dks, *dvs, dw_kv, normed, branch, datt, mixed, conv_proj, w_qkv, kernels, gain, ids, x, halo, dgain)
    specs = (
        [nat] * len(parts)
        + [full(g.shape) for g in gbs]
        + [pl.BlockSpec((d.shape[0], tile), lambda i, *_: (0, steps - 1 - i)) for d in dqs]
        + [pl.BlockSpec((tile, d.shape[1]), lambda i, *_: (steps - 1 - i, 0)) for d in dks + dvs]
        + [full(dw_kv.shape)]
        + [nat] * 4
        + [full(o.shape) for o in (conv_proj, w_qkv, kernels, gain, ids, x, halo, dgain)]
    )
    outs = [
        jax.ShapeDtypeStruct((rows, width), F32),
        jax.ShapeDtypeStruct((8, width), F32),
    ] + [jax.ShapeDtypeStruct((16, depth, 128), LOW)] * 2
    return pl.pallas_call(
        functools.partial(finish_kernel, mes, len(parts), len(gbs), len(dqs)),
        out_shape=outs,
        grid_spec=pltpu.PrefetchScalarGridSpec(
            num_scalar_prefetch=1,
            grid=(steps,),
            in_specs=specs,
            out_specs=[nat] + [full(o.shape) for o in outs[1:]],
            scratch_shapes=[
                pltpu.VMEM((rows + 8, width), F32),
                pltpu.VMEM((3, tile + 16, width), F32),
                pltpu.VMEM((8, ids.shape[1]), F32),
                pltpu.VMEM((8, width), F32),
                pltpu.VMEM((32, depth, 128), LOW),
                pltpu.VMEM((width, 3 * width), F32),
                pltpu.VMEM((width, width), F32),
            ],
        ),
        compiler_params=params(),
        cost_estimate=cost(12),
        name="finish",
    )(info, *operands)


def spread_ffn_kernel(mes, away, info, source, *rest):
    gate_up_ref, down_ref = rest[-2:]
    which = pl.program_id(1)
    turn = info[mes + away] & 7
    for k in range(8):
        col, row = 128 * (k // 2), 256 * (k % 2)
        gate_up_ref[row : row + 256, col : col + 128] = source[
            k ^ turn, pl.ds(pl.multiple_of(which * 256, 256), 256), :
        ].astype(F32)

    @pl.when(which == 0)
    def _():
        for k in range(8):
            col, row = 128 * (k // 2), 256 * (k % 2)
            for part in range(2):
                lane = row + 128 * part
                down_ref[col : col + 128, lane : lane + 128] = source[
                    k ^ turn, 512 + 128 * part : 640 + 128 * part, :
                ].astype(F32)


def spread_ffn(mes, away, info, pieces, width, hidden, into=()):
    steps = hidden // 512
    return pl.pallas_call(
        functools.partial(spread_ffn_kernel, mes, away),
        out_shape=[jax.ShapeDtypeStruct((width, 2 * hidden), F32), jax.ShapeDtypeStruct((hidden, width), F32)],
        grid_spec=pltpu.PrefetchScalarGridSpec(
            num_scalar_prefetch=1,
            grid=(2, 2),
            in_specs=[pl.BlockSpec((8,) + pieces.shape[1:], lambda i, w, info: (i, 0, 0))]
            + [pl.BlockSpec(memory_space=pl.ANY)] * len(into),
            out_specs=[
                pl.BlockSpec((width, 512), lambda i, w, info: (0, w * steps + hidden_block(mes, info, away, i))),
                pl.BlockSpec((512, width), lambda i, w, info: (hidden_block(mes, info, away, i), 0)),
            ],
        ),
        input_output_aliases={2 + j: j for j in range(len(into))},
        compiler_params=params(),
        cost_estimate=cost(5),
        name="spread_ffn",
    )(info, pieces, *into)


def group_of(mes, info, step):
    return (step & 1) ^ (info[mes + step // 2] >> 3)


def spread_kernel(mes, info, own_c, other_c, own_e, other_e, qkv_ref, out_ref, conv_ref, taps_ref, gain_a_ref, gain_f_ref, bias_ref, few):
    step = pl.program_id(0)
    turn = info[mes + step // 2] & 7
    group = group_of(mes, info, step)
    width = out_ref.shape[1]
    places = [(out_ref, 0, width)]
    places_e = [(qkv_ref, 0, 3 * width), (conv_ref, 0, width)]
    for j, pair in enumerate(((own_c, own_e), (other_c, other_e))):

        @pl.when(step // 2 == j)
        def _(pair=pair):
            for source, targets in zip(pair, (places, places_e)):
                for k in range(8):
                    spot = k ^ turn
                    at = 0
                    for out, column, columns in targets:
                        for lane in range(column, column + columns, 128):
                            out[16 * k : 16 * k + 16, lane : lane + 128] = source[spot, at : at + 16, :].astype(F32)
                            at += 16
                    if targets is places_e:
                        few[group, k] = source[spot, at : at + 16, :].astype(F32)

    @pl.when(step == 3)
    def _():
        lines = [
            jnp.concatenate([few[(4 * r + c) // 8, (4 * r + c) % 8, 0:1, :] for c in range(4)], axis=1)
            for r in range(6)
        ]
        for row, line in enumerate((0, 1, 0, 1, 2, 0, 1, 2, 3)):
            taps_ref[row : row + 1, :] = lines[line]
        gain_a_ref[...] = lines[4]
        gain_f_ref[...] = lines[5]
        rows = jnp.concatenate([few[g // 8, g % 8, 1:2, :] for g in range(32)], axis=0)
        bias_ref[...] = rows.T[: bias_ref.shape[0], :]


def spread(mes, info, own_c, other_c, own_e, other_e, width, heads):
    def source(depth, at, j):
        return pl.BlockSpec((8, depth, 128), lambda i, info: (jnp.clip(i - 2 * j, 0, 1), at, 0))

    deep = own_e.shape[1]
    out_at = own_c.shape[1] * 8 // width - 1

    columns = (3 * width, width, width)
    small = [(9, width), (1, width), (1, width), (heads, 32)]
    return pl.pallas_call(
        functools.partial(spread_kernel, mes),
        out_shape=[jax.ShapeDtypeStruct((width, c), F32) for c in columns]
        + [jax.ShapeDtypeStruct(shape, F32) for shape in small],
        grid_spec=pltpu.PrefetchScalarGridSpec(
            num_scalar_prefetch=1,
            grid=(4,),
            in_specs=[source(width // 8, out_at, j) for j in range(2)] + [source(deep, 0, j) for j in range(2)],
            out_specs=[pl.BlockSpec((width // 4, c), lambda i, info: (group_of(mes, info, i), 0)) for c in columns]
            + [full(shape) for shape in small],
            scratch_shapes=[pltpu.VMEM((4, 8, 16, 128), F32)],
        ),
        compiler_params=params(),
        cost_estimate=cost(5),
        name="spread",
    )(info, own_c, other_c, own_e, other_e)


def hop_tables(sizes):
    seq = [sizes["dp"] << b for b in range(sizes["seq"].bit_length() - 1)]
    dp = [1 << b for b in range(1, sizes["dp"].bit_length() - 1)]
    return [1] + seq + dp, [1] + dp[:1] + seq + dp[1:]


def place_of(tables):
    here = lax.axis_index(("seq", "dp"))
    places = []
    for masks in tables:
        me = jnp.int32(0)
        for mask in masks[:5]:
            me = me * 2 + jnp.where((here & mask) != 0, 1, 0)
        places.append(me)
    even = (here & 1) == 0
    return [jnp.where(even, places[0], places[1]), jnp.where(even, places[1], places[0]) ^ 16]


def swap(value, tables, hops):
    count = lax.axis_size(("seq", "dp"))
    masks = [functools.reduce(lambda x, h: x ^ table[h], hops, 0) for table in tables]
    return lax.ppermute(value, ("seq", "dp"), [(i, i ^ masks[i & 1]) for i in range(count)])


def partners(phase):
    sets = [()]
    for hop in phase:
        sets = [s + extra for s in sets for extra in ((), (hop,))]
    return sets[1:]


class Sum:
    def __init__(self, tables, sizes, early, late):
        phases, at = [], 0
        for size in sizes:
            phases.append(tuple(range(at, at + size)))
            at += size
        self.tables = tables
        self.down = phases
        self.across = range(at, len(tables[0]))
        self.value = late
        self.leaving = list(early)
        self.flights = []
        self.stage = 0
        self.other = None

    def combine(self):
        self.stage += 1
        stage, down, across = self.stage, len(self.down), len(self.across)
        if stage <= down + across:
            self.value = functools.reduce(
                jnp.add, [v.astype(F32) for v in [self.value] + self.flights]
            ).astype(LOW)
        else:
            self.value = jnp.concatenate([self.value] + self.flights, axis=0)
        if stage < down:
            count = 1 << len(self.down[stage])
            share = self.value.shape[0] // count
            pieces = [self.value[j * share : (j + 1) * share] for j in range(count)]
            self.value, self.leaving = pieces[0], pieces[1:]

    def launch(self):
        stage, down, across = self.stage, len(self.down), len(self.across)
        if stage < down:
            self.flights = [swap(v, self.tables, m) for v, m in zip(self.leaving, partners(self.down[stage]))]
        elif stage < down + across:
            self.flights = [swap(self.value, self.tables, (self.across[stage - down],))]
        else:
            left = down - 1 - (stage - down - across)
            self.flights = [swap(self.value, self.tables, m) for m in partners(self.down[left])]
            if left == 0:
                self.other = self.flights[0]

    def finish(self):
        while self.other is None:
            step_on([self])

    def held(self):
        sending = self.stage < len(self.down)
        return [self.value] + (self.leaving if sending else [])

    def hold(self, values):
        self.value = values[0]
        if self.stage < len(self.down):
            self.leaving = list(values[1:])


def step_on(sums, fresh=(), ties=(), after=()):
    if after:
        flat = lax.optimization_barrier(tuple(v for r in sums for v in r.flights) + tuple(after))
        at = 0
        for running in sums:
            running.flights = list(flat[at : at + len(running.flights)])
            at += len(running.flights)
        ties = tuple(ties) + tuple(flat[at:])
    for running in sums:
        running.combine()
    moving = list(sums) + list(fresh)
    groups = [running.held() for running in moving]
    flat = lax.optimization_barrier(tuple(v for g in groups for v in g) + tuple(ties))
    at = 0
    for running, group in zip(moving, groups):
        running.hold(flat[at : at + len(group)])
        at += len(group)
        running.launch()
    return flat[at:]


def total(terms):
    if len(terms) == 1:
        return terms[0]
    return functools.reduce(jnp.add, [t.astype(F32) for t in terms]).astype(terms[0].dtype)


def shards(sizes, tokens, word_ids, cotangent, conv_kernels, conv_proj, gain_attn, w_qkv, rel_bias, out_proj, gain_ffn, w_gate_up, w_down):
    seqs, rows, width = tokens.shape
    heads = rel_bias.shape[1]
    pairs = heads // 2
    ring = sizes["seq"]
    me = lax.axis_index("seq")
    tables = hop_tables(sizes)
    info = jnp.stack(
        [((me + k) % ring) * rows for k in range(ring)] + place_of(tables)
    ).astype(jnp.int32)
    mes = ring
    gain_one = gain_two = jnp.stack([gain_attn, gain_ffn])
    halo = lax.ppermute(tokens[:, rows - 8 :, :], "seq", [(i, (i + 1) % ring) for i in range(ring)])
    halo, travelling = lax.optimization_barrier((halo, tokens))
    block_tokens = [tokens] + [
        lax.ppermute(travelling, "seq", [((i + k) % ring, i) for i in range(ring)]) for k in range(1, ring)
    ]
    halos = [halo] + [b[:, rows - 8 :, :] for b in block_tokens[:-1]]
    units = rows // unit_of(rows)

    parts_of = []
    for s in range(seqs):
        ids = word_ids[s : s + 1]
        own = project(True, 0, info, tokens[s], halos[0][s], ids, conv_kernels, gain_one, conv_proj, w_qkv)
        branch, mixed, normed, query, query_t, key, key_t, value, value_t = own
        held = [(normed, key, key_t, value, value_t)]
        fwd = [attend(0, ids, info, rel_bias.T, key, value_t, query_t)]
        for k in range(1, ring):
            held.append(
                project(False, k, info, block_tokens[k][s], halos[k][s], ids, conv_kernels, gain_one, conv_proj, w_qkv)
            )
            fwd.append(attend(k, ids, info, rel_bias.T, held[k][1], held[k][4], query_t))
        ffn = feed_forward(
            mes, info, [f[1] for f in fwd], [f[2] for f in fwd], branch, out_proj, gain_two, cotangent[s], w_gate_up, w_down, units
        )
        parts_of.append((ids, held, fwd, query, branch, mixed, ffn))

    pieces = [total([p[-1][ring + 5 + j] for p in parts_of]) for j in range(2)]
    sum_a = Sum(tables, (1, 1, 1, 2), [pieces[0]], pieces[1])
    step_on([], [sum_a])

    results, gxs, rets, last_pieces = [], [], [], []
    for s in range(seqs):
        ids, held, fwd, query, branch, mixed, ffn = parts_of[s]
        scales = ffn[:ring]
        result, datt, dout_t, rowdot, dgain = ffn[ring : ring + 5]
        results.append(result)
        def run_back(k, first, count, go, so_far=None):
            return attend_back(
                k, first, count, ids, info, fwd[k][0], held[k][2], held[k][3], query, dout_t, scales[k], go, so_far
            )

        final = s == seqs - 1

        def moved(value, after=()):
            return step_on([sum_a], (), (value,), after) if final else (value,) + tuple(after)

        parts, dw_kvs, gbs, dq_sum = [], [], [], None
        go = moved(rowdot)[0]
        for k in range(1, ring):
            low = run_back(k, 0, pairs - 1, go)
            go, gb_low = rowdot, low[3]
            if k == 1:
                go, gb_low = moved(rowdot, (gb_low,))
            high = run_back(k, pairs - 1, 1, go)
            go = rowdot
            dq_k = [low[0], high[0]]
            dq_sum = dq_k if dq_sum is None else [a + b for a, b in zip(dq_sum, dq_k)]
            dv, gb = low[2], high[3]
            if k == ring - 1:
                dv, gb = moved(dv, (gb,))
            gbs += [gb_low, gb]
            dn, dw_kv = back_other([low[1], high[1]], [dv, high[2]], held[k][0], w_qkv)
            if k == ring - 1:
                dn, go = lax.optimization_barrier((dn, rowdot))
            parts.append(lax.ppermute(dn, "seq", [(i, (i + k) % ring) for i in range(ring)]))
            dw_kvs.append(dw_kv)
        if dq_sum is None:
            dq_sum = [jnp.zeros((width - 128, rows), F32), jnp.zeros((128, rows), F32)]
        dw_kv = total(dw_kvs) if dw_kvs else jnp.zeros((width, 2 * width), LOW)
        own = [run_back(0, 0, 1, go, (dq_sum[0], 0))]
        go, gb = moved(rowdot, (own[0][3],))
        own.append(run_back(0, 1, pairs - 2, go, (dq_sum[0], 1)))
        go, gb_next = moved(rowdot, (own[1][3],))
        own.append(run_back(0, pairs - 1, 1, go, (dq_sum[1], 0)))
        taps, gb_last = moved(conv_kernels, (own[2][3],))
        gbs += [gb, gb_next, gb_last]
        gx, ret, early, late = finish(
            mes, info, parts, gbs, [o[0] for o in own], [o[1] for o in own], [o[2] for o in own], dw_kv,
            held[0][0], branch, datt, mixed, conv_proj, w_qkv, taps, gain_one, ids, tokens[s], halos[0][s], dgain,
        )
        gxs.append(gx)
        rets.append(ret)
        last_pieces.append((early, late))

    early, late = [total([p[j] for p in last_pieces]) for j in range(2)]
    sum_e = Sum(tables, (1, 2, 2), [early], late)
    hidden = w_down.shape[0]
    gxs, ret = step_on([], [sum_e], (jnp.stack(gxs), jnp.stack(rets)))
    returned = lax.ppermute(ret, "seq", [(i, i - 1) for i in range(1, ring)])
    while sum_a.other is None:
        step_on([sum_e, sum_a])
    grads = spread_ffn(mes, 0, info, sum_a.value, width, hidden)
    grads = step_on([sum_e], (), (), grads)
    grad_tokens = gxs.at[:, rows - 8 :, :].add(returned)
    (grad_tokens,) = step_on([sum_e], (), (grad_tokens,))
    last = 2 * len(sum_e.down) + len(sum_e.across) - 1
    while sum_e.stage < last - 1:
        step_on([sum_e])
    grads = spread_ffn(mes, 1, info, sum_a.other, width, hidden, grads)
    grad_gate_up, grad_down = step_on([sum_e], (), (), grads)
    sum_e.finish()
    grad_w_qkv, grad_out_proj, grad_conv_proj, grad_kernels, grad_gain_a, grad_gain_f, grad_bias = spread(
        mes, info, sum_a.value, sum_a.other, sum_e.value, sum_e.other, width, heads
    )
    return (
        jnp.stack(results),
        grad_tokens,
        grad_kernels,
        grad_conv_proj,
        grad_gain_a.reshape(-1),
        grad_w_qkv,
        grad_bias.T,
        grad_out_proj,
        grad_gain_f.reshape(-1),
        grad_gate_up,
        grad_down,
    )


def solution(mesh):
    sizes = dict(mesh.shape)
    split = P("dp", "seq", None)
    in_specs = (split, P("dp", None), split) + (P(),) * 9
    out_specs = (split, split) + (P(),) * 9
    return jax.shard_map(
        functools.partial(shards, sizes), mesh=mesh, in_specs=in_specs, out_specs=out_specs, check_vma=False
    )
```

```python
import functools

import jax
import jax.numpy as jnp
from jax import lax
from jax.experimental import pallas as pl
from jax.experimental.pallas import tpu as pltpu
from jax.sharding import PartitionSpec as P

EVERY = ("seq", "dp")
LOW = jnp.bfloat16
F32 = jnp.float32
EDGES = (1, 2, 3, 4, 5, 6, 7, 8, 11, 16, 22, 32, 45, 64, 91)
KEY_WORDS = 128
QUERY_WORDS = 256
FOLD = 512
VMEM_BYTES = 60 * 2**20


def bucketize(offsets):
    magnitude = jnp.abs(offsets)
    bucketed = jnp.where(offsets > 0, 16, 0).astype(jnp.int32)
    for edge in EDGES:
        bucketed = bucketed + (magnitude >= edge).astype(jnp.int32)
    return bucketed


def dot(a, b):
    return jnp.dot(a, b, preferred_element_type=F32)


def dot_nt(a, b):
    return lax.dot_general(a, b, (((1,), (1,)), ((), ())), preferred_element_type=F32)


def iota(shape, dim):
    return lax.broadcasted_iota(jnp.int32, shape, dim)


def onehot(mask):
    return mask.astype(F32).astype(LOW)


def params(**kw):
    return pltpu.CompilerParams(vmem_limit_bytes=VMEM_BYTES, **kw)


def cost(micros):
    return pl.CostEstimate(flops=int(micros * 1e7), bytes_accessed=int(micros * 1e4), transcendentals=0)


def full(shape):
    return pl.BlockSpec(shape, lambda *_: (0,) * len(shape))


def make_taps(kernels):
    k = kernels.astype(F32)
    return [
        k[0:1] + k[2:3] + k[5:6],
        k[1:2] + k[3:4] + k[6:7],
        k[4:5] + k[7:8],
        k[8:9],
    ]


def same_words(ids):
    place = iota(ids.shape, 1)
    rows = [
        jnp.where((pltpu.roll(ids, back, 1) == ids) & (place >= back), 1.0, 0.0) for back in range(1, 4)
    ]
    return jnp.concatenate([jnp.zeros(ids.shape, F32)] + rows + [jnp.zeros((4, ids.shape[1]), F32)], axis=0)


def project_kernel(own, at, info, x_ref, halo_ref, ids_ref, kernels_ref, gain_ref, conv_ref, w_ref, *rest):
    step = pl.program_id(0)
    tile = rest[0].shape[0]
    ext, masks = rest[-2:]
    width = x_ref.shape[1]

    @pl.when(step == 0)
    def _():
        ext[0:8, :] = halo_ref[...].astype(F32)
        ext[8:, :] = x_ref[...].astype(F32)
        masks[...] = same_words(ids_ref[...])

    start = pl.multiple_of(step * tile, tile)
    chunk = ext[pl.ds(start, tile + 8), :]
    lane = pl.multiple_of(info[at] + step * tile, tile)
    same = masks[:, pl.ds(lane, tile)].T
    taps = make_taps(kernels_ref[...])
    inputs = chunk[8:, :]
    mixed = taps[0] * inputs
    for back in range(1, 4):
        mixed = mixed + taps[back] * chunk[8 - back : 8 - back + tile, :] * same[:, back : back + 1]
    mixed_low = mixed.astype(LOW)
    branch = inputs + dot(mixed_low, conv_ref[...])
    factor = lax.rsqrt(jnp.mean(branch * branch, axis=-1, keepdims=True) + 1e-06)
    normed = (branch * factor * gain_ref[...].astype(F32)[0:1, :]).astype(LOW)
    if own:
        branch_ref, mixed_ref, n_ref, q_ref, qt_ref, k_ref, kt_ref, v_ref, vt_ref = rest[:-2]
        qkv = dot(normed, w_ref[...]).astype(LOW)
        query = qkv[:, :width] * jnp.asarray(0.125, LOW)
        q_ref[...] = query
        qt_ref[...] = query.T
        branch_ref[...] = branch
        mixed_ref[...] = mixed_low
        key, value = qkv[:, width : 2 * width], qkv[:, 2 * width :]
    else:
        n_ref, k_ref, kt_ref, v_ref, vt_ref = rest[:-2]
        kv = dot(normed, w_ref[:, width:]).astype(LOW)
        key, value = kv[:, :width], kv[:, width:]
    n_ref[...] = normed
    k_ref[...] = key
    kt_ref[...] = key.T
    v_ref[...] = value
    vt_ref[...] = value.T


def project(own, at, info, x, halo, ids, kernels, gain, conv_proj, w_qkv):
    rows, width = x.shape
    tile = min(512, rows)
    nat = pl.BlockSpec((tile, width), lambda i, *_: (i, 0))
    tra = pl.BlockSpec((width, tile), lambda i, *_: (0, i))
    nat_low = jax.ShapeDtypeStruct((rows, width), LOW)
    tra_low = jax.ShapeDtypeStruct((width, rows), LOW)
    nat_f32 = jax.ShapeDtypeStruct((rows, width), F32)
    if own:
        outs = [(nat_f32, nat), (nat_low, nat), (nat_low, nat), (nat_low, nat), (tra_low, tra)]
    else:
        outs = [(nat_low, nat)]
    outs = outs + [(nat_low, nat), (tra_low, tra), (nat_low, nat), (tra_low, tra)]
    operands = (x, halo, ids, kernels, gain, conv_proj, w_qkv)
    return pl.pallas_call(
        functools.partial(project_kernel, own, at),
        out_shape=[s for s, _ in outs],
        grid_spec=pltpu.PrefetchScalarGridSpec(
            num_scalar_prefetch=1,
            grid=(rows // tile,),
            in_specs=[full(o.shape) for o in operands],
            out_specs=[b for _, b in outs],
            scratch_shapes=[pltpu.VMEM((rows + 8, width), F32), pltpu.VMEM((8, ids.shape[1]), F32)],
        ),
        compiler_params=params(),
        cost_estimate=cost(8 if own else 6),
        name="project_own" if own else "project_other",
    )(info, *operands)


def word_spans(ids, q_off, k_off, rows_q, rows_k, unit):
    q_first = ids[0, q_off]
    q_wins = (ids[0, q_off + rows_q - 1] - q_first) // QUERY_WORDS + 1
    firsts, wins = [], []
    for at in range(0, rows_k, unit):
        first = ids[0, k_off + at]
        firsts.append(first)
        wins.append((ids[0, k_off + at + unit - 1] - first) // KEY_WORDS + 1)
    fits = q_wins == 1
    for count in wins:
        fits = jnp.logical_and(fits, count == 1)
    return q_first, q_wins, firsts, wins, fits


def unit_of(rows_k):
    return min(512, rows_k)


def stat_rows(rows_k):
    return -(-(2 * (rows_k // unit_of(rows_k)) + 4) // 8) * 8


def attend_kernel(rows_q, rows_k, spot, ids, info, ids_ref, bias_ref, k_ref, vt_ref, qt_ref, p_ref, o_ref, stat_ref, eqt, ek, bidx, raw, tab_ref, parts, flag):
    pair = pl.program_id(0)
    unit = unit_of(rows_k)
    units = rows_k // unit
    q_off, k_off = info[0], info[spot]
    q_first, q_wins, firsts, wins, fits = word_spans(ids, q_off, k_off, rows_q, rows_k, unit)
    q_ids = ids_ref[:, pl.ds(pl.multiple_of(q_off, 128), rows_q)]

    def unit_ids(at):
        return ids_ref[:, pl.ds(pl.multiple_of(k_off + at * unit, 128), unit)]

    def query_words(win):
        return onehot(iota((QUERY_WORDS, rows_q), 0) + (q_first + win * QUERY_WORDS) == q_ids)

    def key_words(at, win):
        return onehot(iota((KEY_WORDS, unit), 0) + (firsts[at] + win * KEY_WORDS) == unit_ids(at)).T

    def buckets(at, win, q_win):
        shift = firsts[at] + win * KEY_WORDS - q_first - q_win * QUERY_WORDS
        shape = (KEY_WORDS, QUERY_WORDS)
        return bucketize(shift + iota(shape, 0) - iota(shape, 1))

    def window_bias(head, index):
        row = jnp.broadcast_to(tab_ref[pl.ds(head, 1), :], (KEY_WORDS, 128))
        parts = [
            jnp.take_along_axis(row, index[:, c : c + 128], axis=1) for c in range(0, QUERY_WORDS, 128)
        ]
        return jnp.concatenate(parts, axis=1).astype(LOW)

    @pl.when(pair == 0)
    def _():
        eqt[...] = query_words(0)
        tab_ref[:, : bias_ref.shape[1]] = bias_ref[...].astype(F32)
        for at in range(units):
            ek[at * unit : (at + 1) * unit, :] = key_words(at, 0)
            bidx[at] = buckets(at, 0, 0)

    def queries(side):
        zero = jnp.zeros((64, rows_q), LOW)
        mine = qt_ref[64 * side : 64 * side + 64, :]
        return [mine, zero] if side == 0 else [zero, mine]

    def window_rows(at):
        bias = jnp.concatenate([window_bias(2 * pair + side, bidx[at]) for side in range(2)], axis=0)
        return dot(bias, eqt[...]).astype(LOW)

    def fast_scores(side, at, spread):
        rows = slice(at * unit, (at + 1) * unit)
        mine = spread[KEY_WORDS * side : KEY_WORDS * side + KEY_WORDS, :]
        right = jnp.concatenate(queries(side) + [mine], axis=0)
        left = jnp.concatenate([k_ref[rows, :], ek[rows, :]], axis=1)
        return dot(left, right)

    def slow_scores(side, at):
        rows = slice(at * unit, (at + 1) * unit)
        raw[...] = dot(k_ref[rows, :], jnp.concatenate(queries(side), axis=0))

        def over_keys(win, carry):
            def over_queries(q_win, inner):
                bias = window_bias(2 * pair + side, buckets(at, win, q_win))
                spread = dot(bias, query_words(q_win)).astype(LOW)
                raw[...] += dot(key_words(at, win), spread)
                return inner

            return lax.fori_loop(0, q_wins, over_queries, carry)

        lax.fori_loop(0, wins[at], over_keys, 0)
        return raw[...]

    jobs = [(side, at) for side in range(2) for at in range(units)]

    def softmax_part(job, score):
        side, at = job
        rows = slice(at * unit, (at + 1) * unit)
        top = jnp.max(score, axis=0, keepdims=True)
        expo = jnp.exp(score - top).astype(LOW)
        p_ref[side, rows, :] = expo
        left = jnp.concatenate([vt_ref[64 * side : 64 * side + 64, rows], jnp.ones((16, unit), LOW)], axis=0)
        parts[side * units + at] = dot(left, expo)
        stat_ref[0, side * units + at : side * units + at + 1, :] = top

    def merge():
        for side in range(2):
            tops = [stat_ref[0, side * units + at : side * units + at + 1, :] for at in range(units)]
            peak = functools.reduce(jnp.maximum, tops)
            total = functools.reduce(
                jnp.add, [parts[side * units + at] * jnp.exp(tops[at] - peak) for at in range(units)]
            )
            o_ref[64 * side : 64 * side + 64, :] = total[:64, :]
            stat_ref[0, 2 * units + side : 2 * units + side + 1, :] = peak
            stat_ref[0, 2 * units + 2 + side : 2 * units + 3 + side, :] = total[64:65, :]

    def run_fast():
        stat_ref[...] = jnp.zeros_like(stat_ref)
        least = most = None
        spreads = [window_rows(at) for at in range(units)]
        for side, at in jobs:
            rows = slice(at * unit, (at + 1) * unit)
            expo = jnp.exp(fast_scores(side, at, spreads[at])).astype(LOW)
            p_ref[side, rows, :] = expo
            left = jnp.concatenate([vt_ref[64 * side : 64 * side + 64, rows], jnp.ones((16, unit), LOW)], axis=0)
            part = dot(left, expo)
            parts[side * units + at] = part
            sums = part[64:65, :]
            least = sums if least is None else jnp.minimum(least, sums)
            most = sums if most is None else jnp.maximum(most, sums)
        return jnp.logical_and(jnp.min(least) > 1e-25, jnp.max(most) < 1e25)

    def run_slow():
        for job in jobs:
            softmax_part(job, slow_scores(*job))

    flag[0] = 0

    @pl.when(fits)
    def _():
        flag[0] = run_fast().astype(jnp.int32)

    @pl.when(flag[0] == 0)
    def _():
        run_slow()

    merge()


def attend(spot, ids, info, rel_bias, key, value_t, query_t):
    rows_k, width = key.shape
    rows_q = query_t.shape[1]
    length = ids.shape[1]
    unit = unit_of(rows_k)
    units = rows_k // unit
    stats = stat_rows(rows_k)
    pairs = width // 128
    return pl.pallas_call(
        functools.partial(attend_kernel, rows_q, rows_k, spot),
        out_shape=[
            jax.ShapeDtypeStruct((2 * pairs, rows_k, rows_q), LOW),
            jax.ShapeDtypeStruct((width, rows_q), F32),
            jax.ShapeDtypeStruct((pairs, stats, rows_q), F32),
        ],
        grid_spec=pltpu.PrefetchScalarGridSpec(
            num_scalar_prefetch=2,
            grid=(pairs,),
            in_specs=[
                full((1, length)),
                full(rel_bias.shape),
                pl.BlockSpec((rows_k, 128), lambda p, *_: (0, p)),
                pl.BlockSpec((128, rows_k), lambda p, *_: (p, 0)),
                pl.BlockSpec((128, rows_q), lambda p, *_: (p, 0)),
            ],
            out_specs=[
                pl.BlockSpec((2, rows_k, rows_q), lambda p, *_: (p, 0, 0)),
                pl.BlockSpec((128, rows_q), lambda p, *_: (p, 0)),
                pl.BlockSpec((1, stats, rows_q), lambda p, *_: (p, 0, 0)),
            ],
            scratch_shapes=[
                pltpu.VMEM((QUERY_WORDS, rows_q), LOW),
                pltpu.VMEM((rows_k, KEY_WORDS), LOW),
                pltpu.VMEM((units, KEY_WORDS, QUERY_WORDS), jnp.int32),
                pltpu.VMEM((unit, rows_q), F32),
                pltpu.VMEM((2 * pairs, 128), F32),
                pltpu.VMEM((2 * units, 80, rows_q), F32),
                pltpu.SMEM((1,), jnp.int32),
            ],
        ),
        compiler_params=params(),
        cost_estimate=cost(20),
        name="attend",
    )(ids, info, ids, rel_bias, key, value_t, query_t)


def attend_back_kernel(rows_q, rows_k, spot, first_pair, last, ids, info, ids_ref, p_ref, kt_ref, v_ref, q_ref, dot_ref, cs_ref, rd_ref, *rest):
    if last:
        so_far_ref, rest = rest[0], rest[1:]
    dq_ref, dk_ref, dv_ref, gb_ref, eq, ekt, bmask, spread, held, by_word = rest[:10]
    dq_acc = rest[10] if last else dq_ref
    at = pl.program_id(1)
    pair = first_pair + pl.program_id(0)
    unit = unit_of(rows_k)
    units = rows_k // unit
    q_off, k_off = info[0], info[spot]
    q_first = ids[0, q_off]
    q_wins = (ids[0, q_off + rows_q - 1] - q_first) // QUERY_WORDS + 1
    q_ids = ids_ref[:, pl.ds(pl.multiple_of(q_off, 128), rows_q)]

    def query_words(win):
        return onehot(iota((QUERY_WORDS, rows_q), 0) + (q_first + win * QUERY_WORDS) == q_ids).T

    def first_word(index):
        return ids[0, k_off + index * unit]

    def key_words(index, win):
        k_ids = ids_ref[:, pl.ds(pl.multiple_of(k_off + index * unit, 128), unit)]
        return onehot(iota((KEY_WORDS, unit), 0) + (first_word(index) + win * KEY_WORDS) == k_ids)

    def bucket_mask(index, win, q_win):
        lane = iota((32, FOLD), 1)
        ahead = jnp.where(lane < FOLD - KEY_WORDS, lane, lane - FOLD)
        shift = first_word(index) + win * KEY_WORDS - q_first - q_win * QUERY_WORDS
        return (bucketize(shift - ahead) == iota((32, FOLD), 0)).astype(F32)

    @pl.when(jnp.logical_and(at == 0, pl.program_id(0) == 0))
    def _():
        eq[...] = query_words(0)
        gb_ref[...] = jnp.zeros_like(gb_ref)
        spread[...] = jnp.zeros_like(spread)
        for index in range(units):
            ekt[index] = key_words(index, 0)
            bmask[index] = bucket_mask(index, 0, 0)

    def fold(grids, mask, heads):
        half = KEY_WORDS // 2
        while half >= 8:
            grids = [g[:half, :] + pltpu.roll(g[half:, :], FOLD - half, 1) for g in grids]
            half //= 2
        row = iota((8, FOLD), 0)
        for bit in (4, 2, 1):
            grids = [jnp.where((row & bit) != 0, pltpu.roll(g, FOLD - bit, 1), g) for g in grids]
        sums = [jnp.sum(mask * jnp.sum(g, axis=0, keepdims=True), axis=1, keepdims=True) for g in grids]
        place = iota(gb_ref.shape, 1)
        gb_ref[...] += functools.reduce(
            jnp.add, [jnp.where(place == head, s, 0.0) for head, s in zip(heads, sums)]
        )

    def scale_row(side):
        return cs_ref[0, pl.ds(side * units + at, 1), :]

    def scaled_dout(side):
        return (dot_ref[64 * side : 64 * side + 64, :].astype(F32) * scale_row(side)).astype(LOW)

    def grad_scores(side, scaled):
        zero = jnp.zeros((64, rows_q), LOW)
        rowdot = rd_ref[pl.ds(2 * pair + side, 1), :] * scale_row(side)
        right = jnp.concatenate([scaled, zero] if side == 0 else [zero, scaled], axis=0)
        grad_p = dot(v_ref[...], right)
        return (p_ref[side].astype(F32) * (grad_p - rowdot)).astype(LOW)

    scaled = [scaled_dout(side) for side in range(2)]
    natural = jnp.concatenate(scaled, axis=0).T
    dks, dvs, dqs, by_words = [], [], [], []
    for side in range(2):
        ds = grad_scores(side, scaled[side])
        key_t = kt_ref[64 * side : 64 * side + 64, :]
        both = dot(jnp.concatenate([key_t, ekt[at]], axis=0), ds)
        dqs.append(both[:64, :])
        by_words.append(both[64:, :].astype(LOW))
        dvs.append(dot(p_ref[side], natural))
        dks.append(dot(ds, q_ref[...]))
    grid = dot(jnp.concatenate(by_words, axis=0), eq[...])
    grid = jnp.concatenate([grid, jnp.zeros((2 * KEY_WORDS, FOLD - QUERY_WORDS), F32)], axis=1)
    fold([grid[:KEY_WORDS, :], grid[KEY_WORDS:, :]], bmask[at], [2 * pair, 2 * pair + 1])
    first = iota((unit, 128), 1) < 64
    dk_ref[...] = jnp.where(first, dks[0], dks[1]).astype(LOW)
    dv_ref[...] = jnp.where(first, dvs[0], dvs[1]).astype(LOW)

    @pl.when(at == 0)
    def _():
        grads = jnp.concatenate(dqs, axis=0)
        dq_acc[...] = so_far_ref[...] + grads if last else grads

    @pl.when(at > 0)
    def _():
        dq_acc[...] += jnp.concatenate(dqs, axis=0)

    if last:

        @pl.when(at == units - 1)
        def _():
            dq_ref[...] = (dq_acc[...] * 0.125).astype(LOW)

    k_wins = (ids[0, k_off + at * unit + unit - 1] - first_word(at)) // KEY_WORDS + 1

    @pl.when(jnp.logical_or(q_wins > 1, k_wins > 1))
    def _():
        for side in range(2):
            held[...] = grad_scores(side, scaled_dout(side))

            def over_keys(win, carry, side=side):
                by_word[...] = dot(key_words(at, win), held[...]).astype(LOW)

                def over_queries(q_win, inner):
                    spread[:, :QUERY_WORDS] = dot(by_word[...], query_words(q_win))
                    fold([spread[...]], bucket_mask(at, win, q_win), [2 * pair + side])
                    return inner

                return lax.fori_loop(jnp.where(win == 0, 1, 0), q_wins, over_queries, carry)

            lax.fori_loop(0, k_wins, over_keys, 0)


def attend_back(spot, first_pair, pairs, ids, info, p, key_t, value, query, dout_t, scales, rowdot, so_far=None):
    width, rows_k = key_t.shape
    rows_q = query.shape[0]
    length = ids.shape[1]
    unit = unit_of(rows_k)
    units = rows_k // unit
    stats = scales.shape[1]
    last = so_far is not None
    so_far, skip = so_far if last else (None, 0)
    dq_spec = pl.BlockSpec((128, rows_q), lambda g, i, *_: (g, 0))
    return pl.pallas_call(
        functools.partial(attend_back_kernel, rows_q, rows_k, spot, first_pair, last),
        out_shape=[
            jax.ShapeDtypeStruct((128 * pairs, rows_q), LOW if last else F32),
            jax.ShapeDtypeStruct((rows_k, 128 * pairs), LOW),
            jax.ShapeDtypeStruct((rows_k, 128 * pairs), LOW),
            jax.ShapeDtypeStruct((32, 128), F32),
        ],
        grid_spec=pltpu.PrefetchScalarGridSpec(
            num_scalar_prefetch=2,
            grid=(pairs, units),
            in_specs=[
                full((1, length)),
                pl.BlockSpec((2, unit, rows_q), lambda g, i, *_: (first_pair + g, i, 0)),
                pl.BlockSpec((128, unit), lambda g, i, *_: (first_pair + g, i)),
                pl.BlockSpec((unit, 128), lambda g, i, *_: (i, first_pair + g)),
                pl.BlockSpec((rows_q, 128), lambda g, i, *_: (0, first_pair + g)),
                pl.BlockSpec((128, rows_q), lambda g, i, *_: (first_pair + g, 0)),
                pl.BlockSpec((1, stats, rows_q), lambda g, i, *_: (first_pair + g, 0, 0)),
                full(rowdot.shape),
            ]
            + [pl.BlockSpec((128, rows_q), lambda g, i, *_: (skip + g, 0))] * last,
            out_specs=[
                dq_spec,
                pl.BlockSpec((unit, 128), lambda g, i, *_: (i, g)),
                pl.BlockSpec((unit, 128), lambda g, i, *_: (i, g)),
                full((32, 128)),
            ],
            scratch_shapes=[
                pltpu.VMEM((rows_q, QUERY_WORDS), LOW),
                pltpu.VMEM((units, KEY_WORDS, unit), LOW),
                pltpu.VMEM((units, 32, FOLD), F32),
                pltpu.VMEM((KEY_WORDS, FOLD), F32),
                pltpu.VMEM((unit, rows_q), LOW),
                pltpu.VMEM((KEY_WORDS, rows_q), LOW),
            ]
            + [pltpu.VMEM((128, rows_q), F32)] * last,
        ),
        compiler_params=params(),
        cost_estimate=cost(7 * pairs),
        name="attend_back",
    )(*((ids, info, ids, p, key_t, value, query, dout_t, scales, rowdot) + ((so_far,) if last else ())))


def norm_back(v, gain, incoming):
    factor = lax.rsqrt(jnp.mean(v * v, axis=-1, keepdims=True) + 1e-06)
    scaled = incoming * gain
    inner = jnp.mean(scaled * v, axis=-1, keepdims=True)
    back = factor * scaled - v * (factor * factor * factor * inner)
    return back, jnp.sum(incoming * v * factor, axis=0, keepdims=True)


def ffn_kernel(blocks, units, mes, info, *refs):
    step = pl.program_id(0)
    outs, stats = refs[:blocks], refs[blocks : 2 * blocks]
    branch_ref, out_proj_ref, gain_ref, cot_ref, wg_ref, wu_ref, wd_ref = refs[2 * blocks : 2 * blocks + 7]
    rest = refs[2 * blocks + 7 :]
    scales = rest[:blocks]
    result_ref, datt_ref, dout_ref, rd_ref, dgain_ref = rest[blocks : blocks + 5]
    pieces = rest[blocks + 5 : blocks + 7]
    attn, attn_low, after, n2, n2t, y_acc, dn_acc, packed, held, sems = rest[blocks + 7 :]
    heads = attn.shape[0] // 64
    chunk = wg_ref.shape[1]
    rows = after.shape[0]

    @pl.when(step == 0)
    def _():
        for head in range(heads):
            pair, side = head // 2, head % 2
            peaks = [s[pair, 2 * units + side : 2 * units + side + 1, :] for s in stats]
            top = functools.reduce(jnp.maximum, peaks)
            shares = [jnp.exp(peak - top) for peak in peaks]
            sums = [s[pair, 2 * units + 2 + side : 2 * units + 3 + side, :] for s in stats]
            inverse = 1.0 / functools.reduce(jnp.add, [a * b for a, b in zip(shares, sums)])
            band = slice(64 * head, 64 * head + 64)
            attn[band, :] = functools.reduce(
                jnp.add, [o[band, :] * (share * inverse) for o, share in zip(outs, shares)]
            )
            for s, c in zip(stats, scales):
                c[pair, side * units : (side + 1) * units, :] = (
                    jnp.exp(s[pair, side * units : (side + 1) * units, :] - top) * inverse
                )
        attn_low[...] = attn[...].astype(LOW)
        joined = branch_ref[...] + dot(attn_low[...].T, out_proj_ref[...])
        after[...] = joined
        factor = lax.rsqrt(jnp.mean(joined * joined, axis=-1, keepdims=True) + 1e-06)
        normed = (joined * factor * gain_ref[...].astype(F32)[1:2, :]).astype(LOW)
        n2[...] = normed
        n2t[...] = normed.T

    weights = jnp.concatenate([wg_ref[...], wu_ref[...]], axis=1)
    both = dot(n2[...], weights)
    gate, up = both[:, :chunk], both[:, chunk:]
    grad_hidden = dot_nt(cot_ref[...], wd_ref[...])
    square = gate * gate
    inner = gate * (0.7978845608028654 + (0.7978845608028654 * 0.044715) * square)
    part = 0.5 + 0.5 * jnp.tanh(inner)
    act = gate * part
    slope = part + 2.0 * act * (1.0 - part) * (
        0.7978845608028654 + (3.0 * 0.7978845608028654 * 0.044715) * square
    )
    hidden = (act * up).astype(LOW)
    grad_both = jnp.concatenate(
        [(grad_hidden * up * slope).astype(LOW), (grad_hidden * act).astype(LOW)], axis=1
    )
    y_part = dot(hidden, wd_ref[...])
    dn_part = dot_nt(grad_both, weights)

    @pl.when(step == 0)
    def _():
        y_acc[...] = y_part
        dn_acc[...] = dn_part

    @pl.when(step > 0)
    def _():
        y_acc[...] += y_part
        dn_acc[...] += dn_part

    grad_w = dot(n2t[...], grad_both).astype(LOW)
    grad_d = dot(hidden.T, cot_ref[...]).astype(LOW)
    turn = info[mes + 1 - step // 2] & 7

    def leaving(j):
        target = pieces[j // 2].at[8 * (j % 2) : 8 * (j % 2) + 8, 0:768, :]
        return pltpu.make_async_copy(held.at[j % 2], target, sems.at[j % 2])

    for j in range(4):

        @pl.when(step == j)
        def _(j=j):
            if j >= 2:
                leaving(j - 2).wait()
            for k in range(8):
                col, row = 128 * (k // 2), 256 * (k % 2)
                spot = k ^ turn
                held[j % 2, spot, 0:256, :] = grad_w[row : row + 256, col : col + 128]
                held[j % 2, spot, 256:512, :] = grad_w[row : row + 256, chunk + col : chunk + col + 128]
                held[j % 2, spot, 512:640, :] = grad_d[col : col + 128, row : row + 128]
                held[j % 2, spot, 640:768, :] = grad_d[col : col + 128, row + 128 : row + 256]
            leaving(j).start()

    @pl.when(step == pl.num_programs(0) - 1)
    def _():
        result_ref[...] = (after[...] + y_acc[...]).astype(LOW)
        back, dgain = norm_back(after[...], gain_ref[...].astype(F32)[1:2, :], dn_acc[...])
        datt = cot_ref[...].astype(F32) + back
        datt_ref[...] = datt
        dgain_ref[...] = jnp.broadcast_to(dgain, dgain_ref.shape)
        datt_low = datt.astype(LOW)
        dout = dot_nt(out_proj_ref[...], datt_low).astype(LOW)
        dout_ref[...] = dout
        pack(packed, 0, dot(attn_low[...], datt_low).astype(LOW), mes, info)
        rest_of = [
            pltpu.make_async_copy(packed.at[16 - 16 * j : 32 - 16 * j], pieces[j].at[:, 768:, :], sems.at[2 + j])
            for j in range(2)
        ]
        for copy in rest_of:
            copy.start()
        prod = dout.astype(F32) * attn[...]
        for head in range(heads):
            rd_ref[head : head + 1, :] = jnp.sum(prod[64 * head : 64 * head + 64, :], axis=0, keepdims=True)
        for copy in rest_of + [leaving(2), leaving(3)]:
            copy.wait()


def hidden_block(mes, info, away, position):
    place = info[mes + away] >> 3
    return 2 * (place >> 1) + (position ^ (place & 1))


def feed_forward(mes, info, outs, stats, branch, out_proj, gain, cot, w_gate_up, w_down, units):
    rows, width = branch.shape
    hidden = w_down.shape[0]
    chunk = 512
    steps = hidden // chunk
    blocks = len(outs)
    heads = width // 64
    once = lambda shape: pl.BlockSpec(shape, lambda *_: (0,) * len(shape), pipeline_mode=pl.Buffered(1))
    nat = (rows, width)

    def block(i, info):
        return hidden_block(mes, info, 1 - i // 2, i % 2)

    pieces = [(16, 768 + width // 8, 128)] * 2
    return pl.pallas_call(
        functools.partial(ffn_kernel, blocks, units, mes),
        out_shape=[jax.ShapeDtypeStruct(s.shape, F32) for s in stats]
        + [
            jax.ShapeDtypeStruct(nat, LOW),
            jax.ShapeDtypeStruct(nat, F32),
            jax.ShapeDtypeStruct((width, rows), LOW),
            jax.ShapeDtypeStruct((heads, rows), F32),
            jax.ShapeDtypeStruct((8, width), F32),
        ]
        + [jax.ShapeDtypeStruct(p, LOW) for p in pieces],
        grid_spec=pltpu.PrefetchScalarGridSpec(
            num_scalar_prefetch=1,
            grid=(steps,),
            in_specs=[once(o.shape) for o in outs]
            + [once(s.shape) for s in stats]
            + [
                once(nat),
                once((width, width)),
                once(gain.shape),
                once(nat),
                pl.BlockSpec((width, chunk), lambda i, info: (0, block(i, info))),
                pl.BlockSpec((width, chunk), lambda i, info: (0, block(i, info) + steps)),
                pl.BlockSpec((chunk, width), lambda i, info: (block(i, info), 0)),
            ],
            out_specs=[once(s.shape) for s in stats]
            + [
                once(nat),
                once(nat),
                once((width, rows)),
                once((heads, rows)),
                once((8, width)),
            ]
            + [pl.BlockSpec(memory_space=pl.ANY)] * len(pieces),
            scratch_shapes=[
                pltpu.VMEM((width, rows), F32),
                pltpu.VMEM((width, rows), LOW),
                pltpu.VMEM(nat, F32),
                pltpu.VMEM(nat, LOW),
                pltpu.VMEM((width, rows), LOW),
                pltpu.VMEM(nat, F32),
                pltpu.VMEM(nat, F32),
                pltpu.VMEM((32, width // 8, 128), LOW),
                pltpu.VMEM((2, 8, 768, 128), LOW),
                pltpu.SemaphoreType.DMA((4,)),
            ],
        ),
        compiler_params=params(),
        cost_estimate=cost(35),
        name="feed_forward",
    )(info, *outs, *stats, branch, out_proj, gain, cot, w_gate_up, w_gate_up, w_down)


def back_other_kernel(count, *refs):
    dks, dvs = refs[:count], refs[count : 2 * count]
    n_ref, w_ref, dn_ref, dw_ref, acc = refs[2 * count :]
    width = n_ref.shape[1]
    both = jnp.concatenate([r[...] for r in dks + dvs], axis=1)
    dn_ref[...] = dot_nt(both, w_ref[:, width:]).astype(LOW)
    part = dot(n_ref[...].T, both)

    @pl.when(pl.program_id(0) == 0)
    def _():
        acc[...] = part

    @pl.when(pl.program_id(0) > 0)
    def _():
        acc[...] += part

    @pl.when(pl.program_id(0) == pl.num_programs(0) - 1)
    def _():
        dw_ref[...] = acc[...].astype(LOW)


def back_other(dks, dvs, normed, w_qkv):
    rows, width = normed.shape
    tile = min(1024, rows)
    nat = pl.BlockSpec((tile, width), lambda i: (i, 0))
    return pl.pallas_call(
        functools.partial(back_other_kernel, len(dks)),
        grid=(rows // tile,),
        out_shape=[jax.ShapeDtypeStruct((rows, width), LOW), jax.ShapeDtypeStruct((width, 2 * width), LOW)],
        in_specs=[pl.BlockSpec((tile, d.shape[1]), lambda i: (i, 0)) for d in dks + dvs] + [nat, full(w_qkv.shape)],
        out_specs=[nat, full((width, 2 * width))],
        scratch_shapes=[pltpu.VMEM((width, 2 * width), F32)],
        compiler_params=params(),
        cost_estimate=cost(5),
        name="back_other",
    )(*dks, *dvs, normed, w_qkv)


def packed_at(g, mes, info):
    here = g ^ info[mes]
    return jnp.where(here < 16, here, 16 + (g ^ info[mes + 1]))


def pack(out, at, value, mes, info):
    rows = value.shape[0] // 32
    for g in range(32):
        for lane in range(value.shape[1] // 128):
            start = at + lane * rows
            out[packed_at(g, mes, info), start : start + rows, :] = value[g * rows : (g + 1) * rows, lane * 128 : (lane + 1) * 128]


def finish_kernel(mes, parts_count, few, calls, info, *refs):
    parts, gbs = refs[:parts_count], refs[parts_count : parts_count + few]
    at = parts_count + few
    dqs, dks, dvs = (refs[at + calls * j : at + calls * (j + 1)] for j in range(3))
    rest = refs[at + 3 * calls :]
    dwkv_ref, n_ref, branch_ref, datt_ref, mixed_ref, conv_ref, w_ref, kernels_ref, gain_ref, ids_ref, x_ref, halo_ref, dgain_ref = rest[:13]
    gx_ref, ret_ref, early, late, ext, edge, masks, small, packed, dw_acc, conv_acc = rest[13:]
    step = pl.program_id(0)
    steps = pl.num_programs(0)
    tile, width = branch_ref.shape
    taps = make_taps(kernels_ref[...])

    @pl.when(step == 0)
    def _():
        masks[...] = same_words(ids_ref[...])
        ext[0:8, :] = halo_ref[...].astype(F32)
        ext[8:, :] = x_ref[...].astype(F32)
        for j in range(3):
            edge[j, tile + 8 :, :] = jnp.zeros((8, width), F32)
            edge[j, 0:8, :] = jnp.zeros((8, width), F32)
        small[...] = jnp.zeros_like(small)
        small[5:6, :] = dgain_ref[0:1, :]
        if tile != x_ref.shape[0]:
            conv_acc[...] = jnp.zeros_like(conv_acc)

    dq = jnp.concatenate([r[...] for r in dqs], axis=0).T
    dqkv = jnp.concatenate([dq] + [r[...] for r in dks + dvs], axis=1)
    dn = dot_nt(dqkv, w_ref[...])
    for part in parts:
        dn = dn + part[...].astype(F32)
    dw = dot(n_ref[...].T, dqkv)

    @pl.when(step == 0)
    def _():
        dw_acc[...] = dw

    @pl.when(step > 0)
    def _():
        dw_acc[...] += dw

    back, dgain = norm_back(branch_ref[...], gain_ref[...].astype(F32)[0:1, :], dn)
    dbranch = datt_ref[...] + back
    dbranch_low = dbranch.astype(LOW)
    conv_part = dot(mixed_ref[...].T, dbranch_low)
    conv_acc[...] = conv_part if tile == x_ref.shape[0] else conv_acc[...] + conv_part
    dmixed = dot_nt(dbranch_low, conv_ref[...])
    at = pl.multiple_of((steps - 1 - step) * tile, tile)
    same = masks[:, pl.ds(pl.multiple_of(info[0] + at, 128), tile)].T
    inputs = ext[pl.ds(at, tile + 8), :]
    small[4:5, :] += dgain
    grad = dbranch + taps[0] * dmixed
    small[0:1, :] += jnp.sum(dmixed * inputs[8:, :], axis=0, keepdims=True)
    returned = jnp.zeros((8, width), F32)
    for back_by in range(1, 4):
        masked = dmixed * same[:, back_by : back_by + 1]
        small[back_by : back_by + 1, :] += jnp.sum(masked * inputs[8 - back_by : 8 - back_by + tile, :], axis=0, keepdims=True)
        j = back_by - 1
        edge[j, 8 : 8 + tile, :] = masked
        grad = grad + taps[back_by] * edge[j, 8 + back_by : 8 + back_by + tile, :]
        returned = returned + taps[back_by] * edge[j, back_by : back_by + 8, :]
        edge[j, tile + 8 :, :] = masked[0:8, :]
    gx_ref[...] = grad
    ret_ref[...] = returned

    @pl.when(step == steps - 1)
    def _():
        pack(packed, 0, dw_acc[:, :width].astype(LOW), mes, info)
        pack(packed, width // 8, (dw_acc[:, width:] + dwkv_ref[...].astype(F32)).astype(LOW), mes, info)
        depth = 3 * width // 8
        pack(packed, depth, conv_acc[...].astype(LOW), mes, info)
        depth += width // 8
        gb = functools.reduce(jnp.add, [r[...] for r in gbs])
        for g in range(32):
            lane = 128 * (g % 4)
            line = jnp.concatenate(
                [small[g // 4 : g // 4 + 1, lane : lane + 128], gb[g : g + 1, :], jnp.zeros((14, 128), F32)], axis=0
            )
            packed[packed_at(g, mes, info), depth : depth + 16, :] = line.astype(LOW)
        early[...] = packed[16:]
        late[...] = packed[:16]


def finish(mes, info, parts, gbs, dqs, dks, dvs, dw_kv, normed, branch, datt, mixed, conv_proj, w_qkv, kernels, gain, ids, x, halo, dgain):
    rows, width = branch.shape
    tile = min(1024, rows)
    steps = rows // tile
    depth = 4 * width // 8 + 16
    nat = pl.BlockSpec((tile, width), lambda i, *_: (steps - 1 - i, 0))
    operands = (*parts, *gbs, *dqs, *dks, *dvs, dw_kv, normed, branch, datt, mixed, conv_proj, w_qkv, kernels, gain, ids, x, halo, dgain)
    specs = (
        [nat] * len(parts)
        + [full(g.shape) for g in gbs]
        + [pl.BlockSpec((d.shape[0], tile), lambda i, *_: (0, steps - 1 - i)) for d in dqs]
        + [pl.BlockSpec((tile, d.shape[1]), lambda i, *_: (steps - 1 - i, 0)) for d in dks + dvs]
        + [full(dw_kv.shape)]
        + [nat] * 4
        + [full(o.shape) for o in (conv_proj, w_qkv, kernels, gain, ids, x, halo, dgain)]
    )
    outs = [
        jax.ShapeDtypeStruct((rows, width), F32),
        jax.ShapeDtypeStruct((8, width), F32),
    ] + [jax.ShapeDtypeStruct((16, depth, 128), LOW)] * 2
    return pl.pallas_call(
        functools.partial(finish_kernel, mes, len(parts), len(gbs), len(dqs)),
        out_shape=outs,
        grid_spec=pltpu.PrefetchScalarGridSpec(
            num_scalar_prefetch=1,
            grid=(steps,),
            in_specs=specs,
            out_specs=[nat] + [full(o.shape) for o in outs[1:]],
            scratch_shapes=[
                pltpu.VMEM((rows + 8, width), F32),
                pltpu.VMEM((3, tile + 16, width), F32),
                pltpu.VMEM((8, ids.shape[1]), F32),
                pltpu.VMEM((8, width), F32),
                pltpu.VMEM((32, depth, 128), LOW),
                pltpu.VMEM((width, 3 * width), F32),
                pltpu.VMEM((width, width), F32),
            ],
        ),
        compiler_params=params(),
        cost_estimate=cost(12),
        name="finish",
    )(info, *operands)


def spread_ffn_kernel(mes, away, info, source, *rest):
    gate_up_ref, down_ref = rest[-2:]
    which = pl.program_id(1)
    turn = info[mes + away] & 7
    for k in range(8):
        col, row = 128 * (k // 2), 256 * (k % 2)
        gate_up_ref[row : row + 256, col : col + 128] = source[
            k ^ turn, pl.ds(pl.multiple_of(which * 256, 256), 256), :
        ].astype(F32)

    @pl.when(which == 0)
    def _():
        for k in range(8):
            col, row = 128 * (k // 2), 256 * (k % 2)
            for part in range(2):
                lane = row + 128 * part
                down_ref[col : col + 128, lane : lane + 128] = source[
                    k ^ turn, 512 + 128 * part : 640 + 128 * part, :
                ].astype(F32)


def spread_ffn(mes, away, info, pieces, width, hidden, into=()):
    steps = hidden // 512
    return pl.pallas_call(
        functools.partial(spread_ffn_kernel, mes, away),
        out_shape=[jax.ShapeDtypeStruct((width, 2 * hidden), F32), jax.ShapeDtypeStruct((hidden, width), F32)],
        grid_spec=pltpu.PrefetchScalarGridSpec(
            num_scalar_prefetch=1,
            grid=(2, 2),
            in_specs=[pl.BlockSpec((8,) + pieces.shape[1:], lambda i, w, info: (i, 0, 0))]
            + [pl.BlockSpec(memory_space=pl.ANY)] * len(into),
            out_specs=[
                pl.BlockSpec((width, 512), lambda i, w, info: (0, w * steps + hidden_block(mes, info, away, i))),
                pl.BlockSpec((512, width), lambda i, w, info: (hidden_block(mes, info, away, i), 0)),
            ],
        ),
        input_output_aliases={2 + j: j for j in range(len(into))},
        compiler_params=params(),
        cost_estimate=cost(5),
        name="spread_ffn",
    )(info, pieces, *into)


def group_of(mes, info, step):
    return (step & 1) ^ (info[mes + step // 2] >> 3)


def spread_kernel(mes, info, own_c, other_c, own_e, other_e, qkv_ref, out_ref, conv_ref, taps_ref, gain_a_ref, gain_f_ref, bias_ref, few):
    step = pl.program_id(0)
    turn = info[mes + step // 2] & 7
    group = group_of(mes, info, step)
    width = out_ref.shape[1]
    places = [(out_ref, 0, width)]
    places_e = [(qkv_ref, 0, 3 * width), (conv_ref, 0, width)]
    for j, pair in enumerate(((own_c, own_e), (other_c, other_e))):

        @pl.when(step // 2 == j)
        def _(pair=pair):
            for source, targets in zip(pair, (places, places_e)):
                for k in range(8):
                    spot = k ^ turn
                    at = 0
                    for out, column, columns in targets:
                        for lane in range(column, column + columns, 128):
                            out[16 * k : 16 * k + 16, lane : lane + 128] = source[spot, at : at + 16, :].astype(F32)
                            at += 16
                    if targets is places_e:
                        few[group, k] = source[spot, at : at + 16, :].astype(F32)

    @pl.when(step == 3)
    def _():
        lines = [
            jnp.concatenate([few[(4 * r + c) // 8, (4 * r + c) % 8, 0:1, :] for c in range(4)], axis=1)
            for r in range(6)
        ]
        for row, line in enumerate((0, 1, 0, 1, 2, 0, 1, 2, 3)):
            taps_ref[row : row + 1, :] = lines[line]
        gain_a_ref[...] = lines[4]
        gain_f_ref[...] = lines[5]
        rows = jnp.concatenate([few[g // 8, g % 8, 1:2, :] for g in range(32)], axis=0)
        bias_ref[...] = rows.T[: bias_ref.shape[0], :]


def spread(mes, info, own_c, other_c, own_e, other_e, width, heads):
    def source(depth, at, j):
        return pl.BlockSpec((8, depth, 128), lambda i, info: (jnp.clip(i - 2 * j, 0, 1), at, 0))

    deep = own_e.shape[1]
    out_at = own_c.shape[1] * 8 // width - 1

    columns = (3 * width, width, width)
    small = [(9, width), (1, width), (1, width), (heads, 32)]
    return pl.pallas_call(
        functools.partial(spread_kernel, mes),
        out_shape=[jax.ShapeDtypeStruct((width, c), F32) for c in columns]
        + [jax.ShapeDtypeStruct(shape, F32) for shape in small],
        grid_spec=pltpu.PrefetchScalarGridSpec(
            num_scalar_prefetch=1,
            grid=(4,),
            in_specs=[source(width // 8, out_at, j) for j in range(2)] + [source(deep, 0, j) for j in range(2)],
            out_specs=[pl.BlockSpec((width // 4, c), lambda i, info: (group_of(mes, info, i), 0)) for c in columns]
            + [full(shape) for shape in small],
            scratch_shapes=[pltpu.VMEM((4, 8, 16, 128), F32)],
        ),
        compiler_params=params(),
        cost_estimate=cost(5),
        name="spread",
    )(info, own_c, other_c, own_e, other_e)


def hop_tables(sizes):
    seq = [sizes["dp"] << b for b in range(sizes["seq"].bit_length() - 1)]
    dp = [1 << b for b in range(1, sizes["dp"].bit_length() - 1)]
    return [1] + seq + dp, [1] + dp[:1] + seq + dp[1:]


def place_of(tables):
    here = lax.axis_index(("seq", "dp"))
    places = []
    for masks in tables:
        me = jnp.int32(0)
        for mask in masks[:5]:
            me = me * 2 + jnp.where((here & mask) != 0, 1, 0)
        places.append(me)
    even = (here & 1) == 0
    return [jnp.where(even, places[0], places[1]), jnp.where(even, places[1], places[0]) ^ 16]


def swap(value, tables, hops):
    count = lax.axis_size(("seq", "dp"))
    masks = [functools.reduce(lambda x, h: x ^ table[h], hops, 0) for table in tables]
    return lax.ppermute(value, ("seq", "dp"), [(i, i ^ masks[i & 1]) for i in range(count)])


def partners(phase):
    sets = [()]
    for hop in phase:
        sets = [s + extra for s in sets for extra in ((), (hop,))]
    return sets[1:]


class Sum:
    def __init__(self, tables, sizes, early, late):
        phases, at = [], 0
        for size in sizes:
            phases.append(tuple(range(at, at + size)))
            at += size
        self.tables = tables
        self.down = phases
        self.across = range(at, len(tables[0]))
        self.value = late
        self.leaving = list(early)
        self.flights = []
        self.stage = 0
        self.other = None

    def combine(self):
        self.stage += 1
        stage, down, across = self.stage, len(self.down), len(self.across)
        if stage <= down + across:
            self.value = functools.reduce(
                jnp.add, [v.astype(F32) for v in [self.value] + self.flights]
            ).astype(LOW)
        else:
            self.value = jnp.concatenate([self.value] + self.flights, axis=0)
        if stage < down:
            count = 1 << len(self.down[stage])
            share = self.value.shape[0] // count
            pieces = [self.value[j * share : (j + 1) * share] for j in range(count)]
            self.value, self.leaving = pieces[0], pieces[1:]

    def launch(self):
        stage, down, across = self.stage, len(self.down), len(self.across)
        if stage < down:
            self.flights = [swap(v, self.tables, m) for v, m in zip(self.leaving, partners(self.down[stage]))]
        elif stage < down + across:
            self.flights = [swap(self.value, self.tables, (self.across[stage - down],))]
        else:
            left = down - 1 - (stage - down - across)
            self.flights = [swap(self.value, self.tables, m) for m in partners(self.down[left])]
            if left == 0:
                self.other = self.flights[0]

    def finish(self):
        while self.other is None:
            step_on([self])

    def held(self):
        sending = self.stage < len(self.down)
        return [self.value] + (self.leaving if sending else [])

    def hold(self, values):
        self.value = values[0]
        if self.stage < len(self.down):
            self.leaving = list(values[1:])


def step_on(sums, fresh=(), ties=(), after=()):
    if after:
        flat = lax.optimization_barrier(tuple(v for r in sums for v in r.flights) + tuple(after))
        at = 0
        for running in sums:
            running.flights = list(flat[at : at + len(running.flights)])
            at += len(running.flights)
        ties = tuple(ties) + tuple(flat[at:])
    for running in sums:
        running.combine()
    moving = list(sums) + list(fresh)
    groups = [running.held() for running in moving]
    flat = lax.optimization_barrier(tuple(v for g in groups for v in g) + tuple(ties))
    at = 0
    for running, group in zip(moving, groups):
        running.hold(flat[at : at + len(group)])
        at += len(group)
        running.launch()
    return flat[at:]


def total(terms):
    if len(terms) == 1:
        return terms[0]
    return functools.reduce(jnp.add, [t.astype(F32) for t in terms]).astype(terms[0].dtype)


def shards(sizes, tokens, word_ids, cotangent, conv_kernels, conv_proj, gain_attn, w_qkv, rel_bias, out_proj, gain_ffn, w_gate_up, w_down):
    seqs, rows, width = tokens.shape
    heads = rel_bias.shape[1]
    pairs = heads // 2
    ring = sizes["seq"]
    me = lax.axis_index("seq")
    tables = hop_tables(sizes)
    info = jnp.stack(
        [((me + k) % ring) * rows for k in range(ring)] + place_of(tables)
    ).astype(jnp.int32)
    mes = ring
    gain_one = gain_two = jnp.stack([gain_attn, gain_ffn])
    halo = lax.ppermute(tokens[:, rows - 8 :, :], "seq", [(i, (i + 1) % ring) for i in range(ring)])
    halo, travelling = lax.optimization_barrier((halo, tokens))
    block_tokens = [tokens] + [
        lax.ppermute(travelling, "seq", [((i + k) % ring, i) for i in range(ring)]) for k in range(1, ring)
    ]
    halos = [halo] + [b[:, rows - 8 :, :] for b in block_tokens[:-1]]
    units = rows // unit_of(rows)

    parts_of = []
    for s in range(seqs):
        ids = word_ids[s : s + 1]
        own = project(True, 0, info, tokens[s], halos[0][s], ids, conv_kernels, gain_one, conv_proj, w_qkv)
        branch, mixed, normed, query, query_t, key, key_t, value, value_t = own
        held = [(normed, key, key_t, value, value_t)]
        fwd = [attend(0, ids, info, rel_bias.T, key, value_t, query_t)]
        for k in range(1, ring):
            held.append(
                project(False, k, info, block_tokens[k][s], halos[k][s], ids, conv_kernels, gain_one, conv_proj, w_qkv)
            )
            fwd.append(attend(k, ids, info, rel_bias.T, held[k][1], held[k][4], query_t))
        ffn = feed_forward(
            mes, info, [f[1] for f in fwd], [f[2] for f in fwd], branch, out_proj, gain_two, cotangent[s], w_gate_up, w_down, units
        )
        parts_of.append((ids, held, fwd, query, branch, mixed, ffn))

    pieces = [total([p[-1][ring + 5 + j] for p in parts_of]) for j in range(2)]
    sum_a = Sum(tables, (1, 1, 1, 2), [pieces[0]], pieces[1])
    step_on([], [sum_a])

    results, gxs, rets, last_pieces = [], [], [], []
    for s in range(seqs):
        ids, held, fwd, query, branch, mixed, ffn = parts_of[s]
        scales = ffn[:ring]
        result, datt, dout_t, rowdot, dgain = ffn[ring : ring + 5]
        results.append(result)
        def run_back(k, first, count, go, so_far=None):
            return attend_back(
                k, first, count, ids, info, fwd[k][0], held[k][2], held[k][3], query, dout_t, scales[k], go, so_far
            )

        final = s == seqs - 1

        def moved(value, after=()):
            return step_on([sum_a], (), (value,), after) if final else (value,) + tuple(after)

        parts, dw_kvs, gbs, dq_sum = [], [], [], None
        go = moved(rowdot)[0]
        for k in range(1, ring):
            low = run_back(k, 0, pairs - 1, go)
            go, gb_low = rowdot, low[3]
            if k == 1:
                go, gb_low = moved(rowdot, (gb_low,))
            high = run_back(k, pairs - 1, 1, go)
            go = rowdot
            dq_k = [low[0], high[0]]
            dq_sum = dq_k if dq_sum is None else [a + b for a, b in zip(dq_sum, dq_k)]
            dv, gb = low[2], high[3]
            if k == ring - 1:
                dv, gb = moved(dv, (gb,))
            gbs += [gb_low, gb]
            dn, dw_kv = back_other([low[1], high[1]], [dv, high[2]], held[k][0], w_qkv)
            if k == ring - 1:
                dn, go = lax.optimization_barrier((dn, rowdot))
            parts.append(lax.ppermute(dn, "seq", [(i, (i + k) % ring) for i in range(ring)]))
            dw_kvs.append(dw_kv)
        if dq_sum is None:
            dq_sum = [jnp.zeros((width - 128, rows), F32), jnp.zeros((128, rows), F32)]
        dw_kv = total(dw_kvs) if dw_kvs else jnp.zeros((width, 2 * width), LOW)
        own = [run_back(0, 0, 1, go, (dq_sum[0], 0))]
        go, gb = moved(rowdot, (own[0][3],))
        own.append(run_back(0, 1, pairs - 2, go, (dq_sum[0], 1)))
        go, gb_next = moved(rowdot, (own[1][3],))
        own.append(run_back(0, pairs - 1, 1, go, (dq_sum[1], 0)))
        taps, gb_last = moved(conv_kernels, (own[2][3],))
        gbs += [gb, gb_next, gb_last]
        gx, ret, early, late = finish(
            mes, info, parts, gbs, [o[0] for o in own], [o[1] for o in own], [o[2] for o in own], dw_kv,
            held[0][0], branch, datt, mixed, conv_proj, w_qkv, taps, gain_one, ids, tokens[s], halos[0][s], dgain,
        )
        gxs.append(gx)
        rets.append(ret)
        last_pieces.append((early, late))

    early, late = [total([p[j] for p in last_pieces]) for j in range(2)]
    sum_e = Sum(tables, (1, 2, 2), [early], late)
    hidden = w_down.shape[0]
    gxs, ret = step_on([], [sum_e], (jnp.stack(gxs), jnp.stack(rets)))
    returned = lax.ppermute(ret, "seq", [(i, i - 1) for i in range(1, ring)])
    while sum_a.other is None:
        step_on([sum_e, sum_a])
    grads = spread_ffn(mes, 0, info, sum_a.value, width, hidden)
    grads = step_on([sum_e], (), (), grads)
    grad_tokens = gxs.at[:, rows - 8 :, :].add(returned)
    (grad_tokens,) = step_on([sum_e], (), (grad_tokens,))
    last = 2 * len(sum_e.down) + len(sum_e.across) - 1
    while sum_e.stage < last - 1:
        step_on([sum_e])
    grads = spread_ffn(mes, 1, info, sum_a.other, width, hidden, grads)
    grad_gate_up, grad_down = step_on([sum_e], (), (), grads)
    sum_e.finish()
    grad_w_qkv, grad_out_proj, grad_conv_proj, grad_kernels, grad_gain_a, grad_gain_f, grad_bias = spread(
        mes, info, sum_a.value, sum_a.other, sum_e.value, sum_e.other, width, heads
    )
    return (
        jnp.stack(results),
        grad_tokens,
        grad_kernels,
        grad_conv_proj,
        grad_gain_a.reshape(-1),
        grad_w_qkv,
        grad_bias.T,
        grad_out_proj,
        grad_gain_f.reshape(-1),
        grad_gate_up,
        grad_down,
    )


def solution(mesh):
    sizes = dict(mesh.shape)
    split = P("dp", "seq", None)
    in_specs = (split, P("dp", None), split) + (P(),) * 9
    out_specs = (split, split) + (P(),) * 9
    return jax.shard_map(
        functools.partial(shards, sizes), mesh=mesh, in_specs=in_specs, out_specs=out_specs, check_vma=False
    )
```
